32 devices in a mesh: groups: 2 (over x), tm: 16 (over z, y, core).
Axes of the slice: x: 2, y: 2, z: 4, core: 2. Of those that a mesh axis runs over, the one named last changes fastest.
Arguments:
- perambulator: bfloat16 [64, 768, 1536], P('groups', 'tm'), parts along dimension 0, may hold values from -6 to 6
- elementals: bfloat16 [32, 16, 192, 384], P(('groups', 'tm')), parts along dimension 0, may hold values from -0.3125 to 0.3125
- diagrams: int32 [32, 3, 2], P('tm'), may hold values from 0 to 15
- counts: int32 [32], P('tm'), may hold values from 1 to 3, as said below
Outputs:
- correlator: float32 [64, 3, 2], P(('groups', 'tm')), parts along dimension 0
The draws below stay inside these ranges and needn't reach their ends.
There are 2 independent parts, one for each index of `groups`. The reference program is written for one: setup_inputs(seed, part) draws one part's arguments, and reference() takes and returns one part's arrays. A program takes and returns all parts, laid end to end along the dimension named above; an argument that names none is the same for every part. Nothing has to cross between parts.
Inputs may be any that keep to these rules, and one draw needn't show every extreme that they name: `counts`: each pair lists 1 to 3 diagrams; in every draw some pair lists exactly 3. `diagrams`: slots at or beyond a pair's count are ignored.
All inputs are finite; a program needn't handle non-finite values.
Results may differ from the reference program's by a relative error of at most 0.0029.
Values may be sent and summed in bfloat16 or wider, within the bound.
No kernel may reach another device: no remote copies, remote signals or barrier semaphores. Data moves between devices by JAX's collectives and lax.ppermute only.
A program may use at most 128 MiB of HBM per device.

```python
import jax
import jax.numpy as jnp
from jax import lax

NV = 192
W = 768
PAIRS_DEV = 2
DG = 3
NELEM = 16
NT = 16
PAIRS = 32
N_TM = 16


def draw_counts(key, part):
    first_key, second_key = jax.random.split(key, 2)
    choose_hot = jax.random.randint(first_key, (PAIRS,), 0, 4)
    lengths = jnp.where(choose_hot == 0, DG, 1).astype(jnp.int32)
    forced = jax.random.randint(second_key, (), 0, PAIRS)
    return lengths.at[forced].set(DG)


def place_ends(entries, rng, smallest, top_value):
    longest = entries.shape.index(max(entries.shape))
    spots = []
    for shift in (0, 1):
        where = [jax.random.randint(jax.random.fold_in(rng, axis), (), 0, length) for axis, length in enumerate(entries.shape)]
        where[longest] = (where[longest] + shift) % entries.shape[longest]
        spots.append(tuple(where))
    return entries.at[spots[0]].set(smallest).at[spots[1]].set(top_value)


def block_levels(own_key, extent, shards, least, top_value):
    level = 1.0
    for dim, shards_of in shards:
        heights = jax.random.uniform(jax.random.fold_in(jax.random.fold_in(own_key, 6), dim), (shards_of,), jnp.float32, least / len(shards), top_value / len(shards))
        level = level * jnp.repeat(jnp.exp(heights), extent[dim] // shards_of).reshape((-1,) + (1,) * (len(extent) - 1 - dim))
    return level


def gaussian(own_key, extent, spread, bound, cuts=(), kind=jnp.bfloat16):
    array = jax.random.normal(own_key, extent, jnp.float32) * spread
    if len(cuts) > 0:
        array = block_levels(own_key, extent, cuts, -0.22, 0.18) * array
    return jnp.clip(array, min=-bound, max=bound).astype(kind)


def setup_inputs(seed: int = 0, part: int = 0) -> dict:
    key_of = jax.random.split(jax.random.key(seed), 5)
    own_keys = jax.random.split(jax.random.fold_in(key_of[4], part), 5)
    perambulator = gaussian(own_keys[0], (PAIRS, W, 2 * W), 1.0, 6.0, ((1, 16),))
    elementals = gaussian(own_keys[1], (NT, NELEM, NV, 2 * NV), (2 * NV) ** -0.5, 0.3125, ((0, 16),))
    diagrams = place_ends(jax.random.randint(key_of[2], (PAIRS, DG, 2), 0, NELEM), jax.random.fold_in(key_of[2], 1), 0, NELEM - 1).astype(jnp.int32)
    counts = draw_counts(jax.random.fold_in(key_of[4], 71), part)
    return dict(perambulator=perambulator, elementals=elementals, diagrams=diagrams, counts=counts)


def swap_parts(pair_tile, vectors):
    full_width = pair_tile.shape[0]
    spin_count = full_width // vectors
    view = pair_tile.reshape(full_width, spin_count, 2, vectors)
    return jnp.stack([-view[:, :, 1, :], view[:, :, 0, :]], axis=2).reshape(full_width, 2 * full_width)


def trace_value(pair_tile, swapped_tile, sink_phi, source_phi):
    full_width = pair_tile.shape[0]
    vectors = sink_phi.shape[0]
    spin_count = full_width // vectors
    real_part = sink_phi[:, :vectors]
    imag_part = sink_phi[:, vectors:]
    embedding = jnp.concatenate([jnp.concatenate([real_part.T, imag_part.T], axis=1), jnp.concatenate([-imag_part.T, real_part.T], axis=1)], axis=0)
    rows_view = pair_tile.reshape(full_width * spin_count, 2 * vectors)
    left_side = jnp.dot(rows_view, embedding, preferred_element_type=jnp.float32).astype(jnp.bfloat16)
    left_view = left_side.reshape(spin_count, vectors, 2 * full_width).astype(jnp.float32)
    tile_view = pair_tile.reshape(spin_count, vectors, 2 * full_width).astype(jnp.float32)
    swap_view = swapped_tile.reshape(spin_count, vectors, 2 * full_width).astype(jnp.float32)
    block_real = jnp.einsum("sjr,skr->jk", left_view, tile_view, precision=lax.Precision.HIGHEST)
    block_imag = jnp.einsum("sjr,skr->jk", left_view, swap_view, precision=lax.Precision.HIGHEST)
    source_real = source_phi[:, :vectors].astype(jnp.float32)
    source_imag = source_phi[:, vectors:].astype(jnp.float32)
    trace_real = (jnp.sum(source_real * block_real) - jnp.sum(source_imag * block_imag)) / full_width
    trace_imag = (jnp.sum(source_real * block_imag) + jnp.sum(source_imag * block_real)) / full_width
    return jnp.stack([trace_real, trace_imag])


def pair_values(pair_tile, sink_set, source_set, sink_index, source_index, live_count):
    slot_count = sink_index.shape[0]
    swapped_tile = swap_parts(pair_tile, sink_set.shape[1])

    def add_one(diagram, values):
        sink_phi = lax.dynamic_index_in_dim(sink_set, sink_index[diagram], 0, keepdims=False)
        source_phi = lax.dynamic_index_in_dim(source_set, source_index[diagram], 0, keepdims=False)
        pair_trace = trace_value(pair_tile, swapped_tile, sink_phi, source_phi)
        return lax.dynamic_update_slice(values, pair_trace[None, :], (diagram, jnp.int32(0)))

    return lax.fori_loop(jnp.int32(0), live_count, add_one, jnp.zeros((slot_count, 2), jnp.float32))


def reference(perambulator, elementals, diagrams, counts):
    time_slices = elementals.shape[0]

    def one_pair(packed):
        pair_tile, diagram_rows, live_count, pair_index = packed
        owner_time = pair_index // PAIRS_DEV
        offset = pair_index % PAIRS_DEV
        separation = (offset + 1) * N_TM // (PAIRS_DEV + 1)
        sink_time = (owner_time + separation) % time_slices
        sink_set = lax.dynamic_index_in_dim(elementals, sink_time, 0, keepdims=False)
        source_set = lax.dynamic_index_in_dim(elementals, owner_time, 0, keepdims=False)
        return pair_values(pair_tile, sink_set, source_set, diagram_rows[:, 0], diagram_rows[:, 1], live_count)

    return lax.map(one_pair, (perambulator, diagrams, counts, jnp.arange(PAIRS, dtype=jnp.int32)))
```

```python
import functools

import jax
import jax.numpy as jnp
from jax import lax
from jax.experimental import pallas as pl
from jax.experimental.pallas import tpu as pltpu
from jax.sharding import PartitionSpec as P

NT_DIMS = (((1,), (1,)), ((), ()))


def exchanged(x, mask):
    devices = lax.axis_size("tm")
    return lax.ppermute(x, "tm", [(i, i ^ mask) for i in range(devices)])


def passed_along(x, by, mask=0):
    devices = lax.axis_size("tm")
    return lax.ppermute(x, "tm", [(i, ((i + by) % devices) ^ mask) for i in range(devices)])


def halves_swapped(x):
    vectors = x.shape[1] // 2
    return jnp.concatenate([x[:, vectors:], x[:, :vectors]], axis=1)


def spin_kernel(
    piece_count, slots, counts_ref, place_ref, *refs
):
    pieces = refs[:piece_count]
    sink_ref, source_ref, out_ref, tile_ref, swap_ref = refs[piece_count:]
    rows = pieces[0].shape[1]
    vectors, width = tile_ref.shape
    packed = 2 * vectors
    spins = width // packed
    pair = pl.program_id(0)
    place = place_ref[0]
    for k in range(piece_count):
        start = pl.multiple_of((place ^ k) * rows, rows)
        tile_ref[pl.ds(start, rows), :] = pieces[k][0]
    lane = lax.broadcasted_iota(jnp.int32, (vectors, packed), 1)
    first_half = lane < vectors
    for b in range(spins):
        part = halves_swapped(tile_ref[:, b * packed : (b + 1) * packed])
        swap_ref[:, b * packed : (b + 1) * packed] = jnp.where(first_half, -part, part)
    for d in range(slots):
        live = d < counts_ref[pair]

        @pl.when(jnp.logical_not(live))
        def _():
            out_ref[pair, d, 0] = 0.0
            out_ref[pair, d, 1] = 0.0

        @pl.when(live)
        def _():
            sink = sink_ref[0, d]
            embedding = jnp.concatenate(
                [jnp.where(first_half, sink, -sink), halves_swapped(sink)], axis=0
            )
            block_real = jnp.zeros((vectors, vectors), jnp.float32)
            block_imag = jnp.zeros((vectors, vectors), jnp.float32)
            for b in range(spins):
                tile = tile_ref[:, b * packed : (b + 1) * packed]
                swap = swap_ref[:, b * packed : (b + 1) * packed]
                left = lax.dot_general(
                    tile, embedding, NT_DIMS, preferred_element_type=jnp.float32
                ).astype(jnp.bfloat16)
                block_real += lax.dot_general(
                    left, tile, NT_DIMS, preferred_element_type=jnp.float32
                )
                block_imag += lax.dot_general(
                    left, swap, NT_DIMS, preferred_element_type=jnp.float32
                )
            source = source_ref[0, d].astype(jnp.float32)
            real = source[:, :vectors]
            imag = source[:, vectors:]
            out_ref[pair, d, 0] = jnp.sum(real * block_real - imag * block_imag)
            out_ref[pair, d, 1] = jnp.sum(real * block_imag + imag * block_real)


def spin_sums(pieces, sinks, sources, counts, place):
    pair_count, slots, vectors, packed = sinks.shape
    rows, width = pieces[0].shape[1:]
    if rows % 16 != 0:
        order = jnp.arange(len(pieces), dtype=jnp.int32) ^ place
        joined = jnp.take(jnp.stack(pieces, axis=1), order, axis=1)
        pieces = [joined.reshape(pair_count, len(order) * rows, width)]
        rows = pieces[0].shape[1]
        place = jnp.int32(0)
    smem = pl.BlockSpec(memory_space=pltpu.SMEM)
    set_spec = pl.BlockSpec((1, slots, vectors, packed), lambda p: (p, 0, 0, 0))
    flops = 2 * pair_count * slots * width * vectors * packed * 2
    moved = 2 * (pair_count * vectors * width + 2 * pair_count * slots * vectors * packed)
    return pl.pallas_call(
        functools.partial(spin_kernel, len(pieces), slots),
        grid=(pair_count,),
        in_specs=[smem, smem]
        + [pl.BlockSpec((1, rows, width), lambda p: (p, 0, 0))] * len(pieces)
        + [set_spec, set_spec],
        out_specs=smem,
        out_shape=jax.ShapeDtypeStruct((pair_count, slots, 2), jnp.float32),
        scratch_shapes=[
            pltpu.VMEM((vectors, width), jnp.bfloat16),
            pltpu.VMEM((vectors, width), jnp.bfloat16),
        ],
        compiler_params=pltpu.CompilerParams(vmem_limit_bytes=40 * 1024 * 1024),
        cost_estimate=pl.CostEstimate(flops=flops, bytes_accessed=moved, transcendentals=0),
    )(counts, place.reshape(1), *pieces, sinks, sources)


def body(perambulator, elementals, diagrams, counts):
    devices = lax.axis_size("tm")
    me = lax.axis_index("tm")
    pair_count, slots = diagrams.shape[:2]
    columns, width = perambulator.shape[1:]
    vectors, packed = elementals.shape[2:]
    spins = columns * devices // vectors
    layer = devices // spins
    half = devices // 2
    own_set = elementals[0]
    mine_high = me // half
    low = me % half

    other_counts = exchanged(counts, half)
    sink_sets = []
    for slot in range(pair_count):
        by = (slot + 1) * devices // (pair_count + 1)
        wanted = passed_along(diagrams[slot, :, 0], by)
        chosen = jnp.take(own_set, wanted, axis=0)
        sink_sets.append((passed_along(chosen, -by), passed_along(chosen, -by, half)))
    own_sources = jnp.take(own_set, diagrams[:, :, 1].reshape(-1), axis=0)
    other_sources = exchanged(own_sources, half)

    grouped = perambulator.reshape(2, half, pair_count, columns, width)
    pieces = []
    for k in range(half):
        sent = lax.dynamic_index_in_dim(grouped, low ^ k, 1, keepdims=False)
        sent = sent.reshape(2 * pair_count, columns, width)
        pieces.append(exchanged(sent, k) if k else sent)

    own_sources = own_sources.reshape(pair_count, slots, vectors, packed)
    other_sources = other_sources.reshape(pair_count, slots, vectors, packed)
    own_sinks = jnp.stack([own for own, _ in sink_sets])
    other_sinks = jnp.stack([other for _, other in sink_sets])

    def low_first(own, other):
        return jnp.where(
            mine_high == 0,
            jnp.concatenate([own, other]),
            jnp.concatenate([other, own]),
        )

    all_counts = low_first(counts, other_counts)
    sinks = low_first(own_sinks, other_sinks)
    sources = low_first(own_sources, other_sources)
    place = me % layer
    total = jnp.zeros((2 * pair_count, slots, 2), jnp.float32)
    for first in range(0, half, layer):
        total = total + spin_sums(
            pieces[first : first + layer], sinks, sources, all_counts, place
        )
    total = total.reshape(2, pair_count, slots, 2)
    kept = lax.dynamic_index_in_dim(total, mine_high, 0, keepdims=False)
    given = lax.dynamic_index_in_dim(total, 1 - mine_high, 0, keepdims=False)
    return (kept + exchanged(given, half)) / (spins * vectors)


def solution(mesh):
    return jax.shard_map(
        body,
        mesh=mesh,
        in_specs=(
            P("groups", "tm", None),
            P(("groups", "tm"), None, None, None),
            P("tm", None, None),
            P("tm"),
        ),
        out_specs=P(("groups", "tm"), None, None),
        check_vma=False,
    )
```

```python
import functools

import jax
import jax.numpy as jnp
from jax import lax
from jax.experimental import pallas as pl
from jax.experimental.pallas import tpu as pltpu
from jax.sharding import PartitionSpec as P

NT_DIMS = (((1,), (1,)), ((), ()))


def exchanged(x, mask):
    devices = lax.axis_size("tm")
    return lax.ppermute(x, "tm", [(i, i ^ mask) for i in range(devices)])


def passed_along(x, by, mask=0):
    devices = lax.axis_size("tm")
    return lax.ppermute(x, "tm", [(i, ((i + by) % devices) ^ mask) for i in range(devices)])


def halves_swapped(x):
    vectors = x.shape[1] // 2
    return jnp.concatenate([x[:, vectors:], x[:, :vectors]], axis=1)


def pair_kernel(slot, count_ref, tau_ref, sink_ref, source_ref, out_ref, tile_ref, swap_ref, left_ref):
    slots = sink_ref.shape[0]
    rows, packed = tile_ref.shape
    vectors = packed // 2
    blocks = rows // vectors
    first_half = lax.broadcasted_iota(jnp.int32, (vectors, packed), 1) < vectors

    @pl.when(pl.program_id(0) == 0)
    def _():
        for d in range(slots):
            out_ref[d, 0] = 0.0
            out_ref[d, 1] = 0.0

    for b in range(blocks):
        tile = tau_ref[:, 0, :, b * packed : (b + 1) * packed].reshape(vectors, packed)
        tile_ref[b * vectors : (b + 1) * vectors, :] = tile
        part = halves_swapped(tile)
        swap_ref[b * vectors : (b + 1) * vectors, :] = jnp.where(first_half, -part, part)

    for d in range(slots):

        @pl.when(d < count_ref[slot])
        def _():
            sink = sink_ref[d]
            embedding = jnp.concatenate(
                [jnp.where(first_half, sink, -sink), halves_swapped(sink)], axis=0
            )
            left_ref[...] = lax.dot_general(
                tile_ref[...], embedding, NT_DIMS, preferred_element_type=jnp.float32
            ).astype(jnp.bfloat16)

            def joined(ref):
                return jnp.concatenate(
                    [ref[b * vectors : (b + 1) * vectors, :] for b in range(blocks)], axis=1
                )

            left = joined(left_ref)
            block_real = lax.dot_general(
                left, joined(tile_ref), NT_DIMS, preferred_element_type=jnp.float32
            )
            block_imag = lax.dot_general(
                left, joined(swap_ref), NT_DIMS, preferred_element_type=jnp.float32
            )
            source = source_ref[0, d].astype(jnp.float32)
            real = source[:, :vectors]
            imag = source[:, vectors:]
            out_ref[d, 0] += jnp.sum(real * block_real - imag * block_imag)
            out_ref[d, 1] += jnp.sum(real * block_imag + imag * block_real)


def pair_sums(tau, slot, sinks, sources, counts):
    slots, vectors, packed = sinks.shape
    spins = tau.shape[0] * tau.shape[2] // vectors
    layer, columns, width = tau.shape[0] // spins, tau.shape[2], tau.shape[3]
    smem = pl.BlockSpec(memory_space=pltpu.SMEM)
    flops = 4 * spins * slots * width * vectors * packed
    moved = 2 * (spins * vectors * width + 2 * slots * vectors * packed)
    rows = vectors * width // packed
    return pl.pallas_call(
        functools.partial(pair_kernel, slot),
        grid=(spins,),
        in_specs=[
            smem,
            pl.BlockSpec((layer, 1, columns, width), lambda s: (s, slot, 0, 0)),
            pl.BlockSpec((slots, vectors, packed), lambda s: (0, 0, 0)),
            pl.BlockSpec((1, slots, vectors, packed), lambda s: (slot, 0, 0, 0)),
        ],
        out_specs=smem,
        out_shape=jax.ShapeDtypeStruct((slots, 2), jnp.float32),
        scratch_shapes=[pltpu.VMEM((rows, packed), jnp.bfloat16)] * 3,
        compiler_params=pltpu.CompilerParams(vmem_limit_bytes=32 * 1024 * 1024),
        cost_estimate=pl.CostEstimate(flops=flops, bytes_accessed=moved, transcendentals=0),
    )(counts, tau, sinks, sources)


def body(perambulator, elementals, diagrams, counts):
    devices = lax.axis_size("tm")
    me = lax.axis_index("tm")
    pair_count, slots = diagrams.shape[:2]
    columns, width = perambulator.shape[1:]
    vectors, packed = elementals.shape[2:]
    half = devices // 2
    own_set = elementals[0]
    high = (me >= half).astype(jnp.int32)
    halves = [list(range(half)), list(range(half, devices))]

    def regrouped(which):
        sent = lax.dynamic_index_in_dim(grouped, which, 0, keepdims=False)
        tau = lax.all_to_all(
            sent, "tm", split_axis=0, concat_axis=0, axis_index_groups=halves, tiled=True
        )
        if columns % 16 != 0:
            tau = jnp.moveaxis(tau, 1, 0).reshape(pair_count, -1, vectors, width)
            tau = jnp.moveaxis(tau, 0, 1)
        return tau

    grouped = perambulator.reshape(2, half, pair_count, columns, width)
    given_tau = regrouped(1 - high)
    given_counts = exchanged(counts, half)
    own_sources = jnp.take(own_set, diagrams[:, :, 1].reshape(-1), axis=0, mode="clip")
    given_sources = exchanged(own_sources, half).reshape(pair_count, slots, vectors, packed)
    own_sources = own_sources.reshape(pair_count, slots, vectors, packed)
    chosen = []
    for slot in range(pair_count):
        by = (slot + 1) * devices // (pair_count + 1)
        wanted = passed_along(diagrams[slot, :, 0], by)
        chosen.append((by, jnp.take(own_set, wanted, axis=0, mode="clip")))
    given_sinks = [passed_along(sets, -by, half) for by, sets in chosen]
    own_sinks = [passed_along(sets, -by) for by, sets in chosen]
    own_tau = regrouped(high)

    def sums(tau, sinks, sources, counts):
        return jnp.stack(
            [pair_sums(tau, slot, sinks[slot], sources, counts) for slot in range(pair_count)]
        )

    given = sums(given_tau, given_sinks, given_sources, given_counts)
    given, counts = lax.optimization_barrier((given, counts))
    got = exchanged(given, half)
    kept = sums(own_tau, own_sinks, own_sources, counts)
    return (kept + got) / (columns * devices)


def solution(mesh):
    return jax.shard_map(
        body,
        mesh=mesh,
        in_specs=(
            P("groups", "tm", None),
            P(("groups", "tm"), None, None, None),
            P("tm", None, None),
            P("tm"),
        ),
        out_specs=P(("groups", "tm"), None, None),
        check_vma=False,
    )
```

```python
import functools

import jax
import jax.numpy as jnp
from jax import lax
from jax.experimental import pallas as pl
from jax.experimental.pallas import tpu as pltpu
from jax.sharding import PartitionSpec as P

NT_DIMS = (((1,), (1,)), ((), ()))


def exchanged(x, mask):
    devices = lax.axis_size("tm")
    return lax.ppermute(x, "tm", [(i, i ^ mask) for i in range(devices)])


def passed_along(x, by, mask=0):
    devices = lax.axis_size("tm")
    return lax.ppermute(x, "tm", [(i, ((i + by) % devices) ^ mask) for i in range(devices)])


def halves_swapped(x):
    vectors = x.shape[1] // 2
    return jnp.concatenate([x[:, vectors:], x[:, :vectors]], axis=1)


def tied(x, *earlier):
    anywhere = pl.BlockSpec(memory_space=pl.ANY)
    return pl.pallas_call(
        lambda *refs: None,
        in_specs=[anywhere] * (1 + len(earlier)),
        out_specs=anywhere,
        out_shape=jax.ShapeDtypeStruct(x.shape, x.dtype),
        input_output_aliases={0: 0},
    )(x, *earlier)


def pair_kernel(slot, count_ref, tau_ref, sink_ref, source_ref, *refs):
    out_ref, tile_ref, swap_ref, left_ref = refs[-4:]
    slots = sink_ref.shape[0]
    rows, packed = tile_ref.shape
    vectors = packed // 2
    blocks = rows // vectors
    first_half = lax.broadcasted_iota(jnp.int32, (vectors, packed), 1) < vectors

    @pl.when(pl.program_id(0) == 0)
    def _():
        for d in range(slots):
            out_ref[d, 0] = 0.0
            out_ref[d, 1] = 0.0

    for b in range(blocks):
        tile = tau_ref[:, 0, :, b * packed : (b + 1) * packed].reshape(vectors, packed)
        tile_ref[b * vectors : (b + 1) * vectors, :] = tile
        part = halves_swapped(tile)
        swap_ref[b * vectors : (b + 1) * vectors, :] = jnp.where(first_half, -part, part)

    for d in range(slots):

        @pl.when(d < count_ref[slot])
        def _():
            sink = sink_ref[d]
            embedding = jnp.concatenate(
                [jnp.where(first_half, sink, -sink), halves_swapped(sink)], axis=0
            )
            left_ref[...] = lax.dot_general(
                tile_ref[...], embedding, NT_DIMS, preferred_element_type=jnp.float32
            ).astype(jnp.bfloat16)

            def joined(ref):
                return jnp.concatenate(
                    [ref[b * vectors : (b + 1) * vectors, :] for b in range(blocks)], axis=1
                )

            left = joined(left_ref)
            block_real = lax.dot_general(
                left, joined(tile_ref), NT_DIMS, preferred_element_type=jnp.float32
            )
            block_imag = lax.dot_general(
                left, joined(swap_ref), NT_DIMS, preferred_element_type=jnp.float32
            )
            source = source_ref[0, d].astype(jnp.float32)
            real = source[:, :vectors]
            imag = source[:, vectors:]
            out_ref[d, 0] += jnp.sum(real * block_real - imag * block_imag)
            out_ref[d, 1] += jnp.sum(real * block_imag + imag * block_real)


def pair_sums(tau, slot, sinks, sources, counts, *earlier):
    slots, vectors, packed = sinks.shape
    spins = tau.shape[0] * tau.shape[2] // vectors
    layer, columns, width = tau.shape[0] // spins, tau.shape[2], tau.shape[3]
    smem = pl.BlockSpec(memory_space=pltpu.SMEM)
    flops = 4 * spins * slots * width * vectors * packed
    moved = 2 * (spins * vectors * width + 2 * slots * vectors * packed)
    rows = vectors * width // packed
    return pl.pallas_call(
        functools.partial(pair_kernel, slot),
        grid=(spins,),
        in_specs=[
            smem,
            pl.BlockSpec((layer, 1, columns, width), lambda s: (s, slot, 0, 0)),
            pl.BlockSpec((slots, vectors, packed), lambda s: (0, 0, 0)),
            pl.BlockSpec((1, slots, vectors, packed), lambda s: (slot, 0, 0, 0)),
        ]
        + [pl.BlockSpec(memory_space=pl.ANY)] * len(earlier),
        out_specs=smem,
        out_shape=jax.ShapeDtypeStruct((slots, 2), jnp.float32),
        scratch_shapes=[pltpu.VMEM((rows, packed), jnp.bfloat16)] * 3,
        compiler_params=pltpu.CompilerParams(vmem_limit_bytes=32 * 1024 * 1024),
        cost_estimate=pl.CostEstimate(flops=flops, bytes_accessed=moved, transcendentals=0),
    )(counts, tau, sinks, sources, *earlier)


def body(perambulator, elementals, diagrams, counts):
    devices = lax.axis_size("tm")
    me = lax.axis_index("tm")
    pair_count, slots = diagrams.shape[:2]
    columns, width = perambulator.shape[1:]
    vectors, packed = elementals.shape[2:]
    half = devices // 2
    own_set = elementals[0]
    high = (me >= half).astype(jnp.int32)
    halves = [list(range(half)), list(range(half, devices))]

    grouped = perambulator.reshape(2, half, pair_count, columns, width)

    def regrouped(which, *earlier):
        sent = lax.dynamic_index_in_dim(grouped, which, 0, keepdims=False)
        tau = lax.all_to_all(
            tied(sent, *earlier),
            "tm",
            split_axis=0,
            concat_axis=0,
            axis_index_groups=halves,
            tiled=True,
        )
        if columns % 16 != 0:
            tau = jnp.moveaxis(tau, 1, 0).reshape(pair_count, -1, vectors, width)
            tau = jnp.moveaxis(tau, 0, 1)
        return tau

    steps = [(slot + 1) * devices // (pair_count + 1) for slot in range(pair_count)]
    wanted = [passed_along(diagrams[slot, :, 0], by) for slot, by in enumerate(steps)]
    given_counts = exchanged(counts, half)
    own_sources = jnp.take(own_set, diagrams[:, :, 1].reshape(-1), axis=0, mode="clip")
    given_sources = exchanged(own_sources, half).reshape(pair_count, slots, vectors, packed)
    own_sources = own_sources.reshape(pair_count, slots, vectors, packed)
    given_tau = regrouped(1 - high, *wanted)
    own_tau = regrouped(high, given_tau)
    chosen = [jnp.take(own_set, index, axis=0, mode="clip") for index in wanted]
    given_sinks = [passed_along(sets, -by, half) for by, sets in zip(steps, chosen)]
    own_sinks = [passed_along(sets, -by) for by, sets in zip(steps, chosen)]

    given = [
        pair_sums(given_tau, slot, given_sinks[slot], given_sources, given_counts)
        for slot in range(pair_count)
    ]
    got = exchanged(jnp.stack(given), half)
    kept = [
        pair_sums(own_tau, slot, own_sinks[slot], own_sources, counts, *given)
        for slot in range(pair_count)
    ]
    return (jnp.stack(kept) + got) / (columns * devices)


def solution(mesh):
    return jax.shard_map(
        body,
        mesh=mesh,
        in_specs=(
            P("groups", "tm", None),
            P(("groups", "tm"), None, None, None),
            P("tm", None, None),
            P("tm"),
        ),
        out_specs=P(("groups", "tm"), None, None),
        check_vma=False,
    )
```

```python
import functools

import jax
import jax.numpy as jnp
from jax import lax
from jax.experimental import pallas as pl
from jax.experimental.pallas import tpu as pltpu
from jax.sharding import PartitionSpec as P

NT_DIMS = (((1,), (1,)), ((), ()))


def exchanged(x, mask):
    devices = lax.axis_size("tm")
    return lax.ppermute(x, "tm", [(i, i ^ mask) for i in range(devices)])


def passed_along(x, by, mask=0):
    devices = lax.axis_size("tm")
    return lax.ppermute(x, "tm", [(i, ((i + by) % devices) ^ mask) for i in range(devices)])


def halves_swapped(x):
    vectors = x.shape[1] // 2
    return jnp.concatenate([x[:, vectors:], x[:, :vectors]], axis=1)


def tied(x, *earlier, flops=0):
    anywhere = pl.BlockSpec(memory_space=pl.ANY)
    return pl.pallas_call(
        lambda *refs: None,
        in_specs=[anywhere] * (1 + len(earlier)),
        out_specs=anywhere,
        out_shape=jax.ShapeDtypeStruct(x.shape, x.dtype),
        input_output_aliases={0: 0},
        cost_estimate=pl.CostEstimate(flops=flops, bytes_accessed=0, transcendentals=0),
    )(x, *earlier)


def pair_kernel(slot, count_ref, tau_ref, sink_ref, source_ref, *refs):
    out_ref, tile_ref, swap_ref, left_ref = refs[-4:]
    slots = sink_ref.shape[0]
    rows, packed = tile_ref.shape
    vectors = packed // 2
    blocks = rows // vectors
    first_half = lax.broadcasted_iota(jnp.int32, (vectors, packed), 1) < vectors

    @pl.when(pl.program_id(0) == 0)
    def _():
        for d in range(slots):
            out_ref[d, 0] = 0.0
            out_ref[d, 1] = 0.0

    for b in range(blocks):
        tile = tau_ref[:, 0, :, b * packed : (b + 1) * packed].reshape(vectors, packed)
        tile_ref[b * vectors : (b + 1) * vectors, :] = tile
        part = halves_swapped(tile)
        swap_ref[b * vectors : (b + 1) * vectors, :] = jnp.where(first_half, -part, part)

    for d in range(slots):

        @pl.when(d < count_ref[slot])
        def _():
            sink = sink_ref[d]
            embedding = jnp.concatenate(
                [jnp.where(first_half, sink, -sink), halves_swapped(sink)], axis=0
            )
            left_ref[...] = lax.dot_general(
                tile_ref[...], embedding, NT_DIMS, preferred_element_type=jnp.float32
            ).astype(jnp.bfloat16)

            def joined(ref):
                return jnp.concatenate(
                    [ref[b * vectors : (b + 1) * vectors, :] for b in range(blocks)], axis=1
                )

            left = joined(left_ref)
            block_real = lax.dot_general(
                left, joined(tile_ref), NT_DIMS, preferred_element_type=jnp.float32
            )
            block_imag = lax.dot_general(
                left, joined(swap_ref), NT_DIMS, preferred_element_type=jnp.float32
            )
            source = source_ref[0, d].astype(jnp.float32)
            real = source[:, :vectors]
            imag = source[:, vectors:]
            out_ref[d, 0] += jnp.sum(real * block_real - imag * block_imag)
            out_ref[d, 1] += jnp.sum(real * block_imag + imag * block_real)


def pair_sums(tau, slot, sinks, sources, counts, *earlier):
    slots, vectors, packed = sinks.shape
    spins = tau.shape[0] * tau.shape[2] // vectors
    layer, columns, width = tau.shape[0] // spins, tau.shape[2], tau.shape[3]
    smem = pl.BlockSpec(memory_space=pltpu.SMEM)
    flops = 4 * spins * slots * width * vectors * packed
    moved = 2 * (spins * vectors * width + 2 * slots * vectors * packed)
    rows = vectors * width // packed
    return pl.pallas_call(
        functools.partial(pair_kernel, slot),
        grid=(spins,),
        in_specs=[
            smem,
            pl.BlockSpec((layer, 1, columns, width), lambda s: (s, slot, 0, 0)),
            pl.BlockSpec((slots, vectors, packed), lambda s: (0, 0, 0)),
            pl.BlockSpec((1, slots, vectors, packed), lambda s: (slot, 0, 0, 0)),
        ]
        + [pl.BlockSpec(memory_space=pl.ANY)] * len(earlier),
        out_specs=smem,
        out_shape=jax.ShapeDtypeStruct((slots, 2), jnp.float32),
        scratch_shapes=[pltpu.VMEM((rows, packed), jnp.bfloat16)] * 3,
        compiler_params=pltpu.CompilerParams(vmem_limit_bytes=32 * 1024 * 1024),
        cost_estimate=pl.CostEstimate(flops=flops, bytes_accessed=moved, transcendentals=0),
    )(counts, tau, sinks, sources, *earlier)


def body(perambulator, elementals, diagrams, counts):
    devices = lax.axis_size("tm")
    me = lax.axis_index("tm")
    pair_count, slots = diagrams.shape[:2]
    columns, width = perambulator.shape[1:]
    vectors, packed = elementals.shape[2:]
    half = devices // 2
    own_set = elementals[0]
    high = (me >= half).astype(jnp.int32)
    halves = [list(range(half)), list(range(half, devices))]

    grouped = perambulator.reshape(2, half, pair_count, columns, width)

    def regrouped(which, *earlier):
        sent = lax.dynamic_index_in_dim(grouped, which, 0, keepdims=False)
        tau = lax.all_to_all(
            tied(sent, *earlier),
            "tm",
            split_axis=0,
            concat_axis=0,
            axis_index_groups=halves,
            tiled=True,
        )
        if columns % 16 != 0:
            tau = jnp.moveaxis(tau, 1, 0).reshape(pair_count, -1, vectors, width)
            tau = jnp.moveaxis(tau, 0, 1)
        return tau

    steps = [(slot + 1) * devices // (pair_count + 1) for slot in range(pair_count)]
    wanted = [passed_along(diagrams[slot, :, 0], by) for slot, by in enumerate(steps)]
    given_counts = exchanged(counts, half)
    own_sources = jnp.take(own_set, diagrams[:, :, 1].reshape(-1), axis=0, mode="clip")
    given_sources = exchanged(own_sources, half).reshape(pair_count, slots, vectors, packed)
    own_sources = own_sources.reshape(pair_count, slots, vectors, packed)
    chosen = [jnp.take(own_set, index, axis=0, mode="clip") for index in wanted]
    given_tau = regrouped(1 - high, given_counts, *wanted)
    in_flight = tied(given_counts, own_sources, *chosen, flops=10**11)
    own_tau = regrouped(high, given_tau, in_flight)
    given_sinks = [passed_along(sets, -by, half) for by, sets in zip(steps, chosen)]
    own_sinks = [passed_along(sets, -by) for by, sets in zip(steps, chosen)]

    given = [
        pair_sums(given_tau, slot, given_sinks[slot], given_sources, in_flight)
        for slot in range(pair_count)
    ]
    got = exchanged(jnp.stack(given), half)
    kept = [
        pair_sums(own_tau, slot, own_sinks[slot], own_sources, counts, *given)
        for slot in range(pair_count)
    ]
    return (jnp.stack(kept) + got) / (columns * devices)


def solution(mesh):
    return jax.shard_map(
        body,
        mesh=mesh,
        in_specs=(
            P("groups", "tm", None),
            P(("groups", "tm"), None, None, None),
            P("tm", None, None),
            P("tm"),
        ),
        out_specs=P(("groups", "tm"), None, None),
        check_vma=False,
    )
```

```python
import functools

import jax
import jax.numpy as jnp
from jax import lax
from jax.experimental import pallas as pl
from jax.experimental.pallas import tpu as pltpu
from jax.sharding import PartitionSpec as P

NT_DIMS = (((1,), (1,)), ((), ()))


def exchanged(x, mask):
    devices = lax.axis_size("tm")
    return lax.ppermute(x, "tm", [(i, i ^ mask) for i in range(devices)])


def passed_along(x, by, mask=0):
    devices = lax.axis_size("tm")
    return lax.ppermute(x, "tm", [(i, ((i + by) % devices) ^ mask) for i in range(devices)])


def halves_swapped(x):
    vectors = x.shape[1] // 2
    return jnp.concatenate([x[:, vectors:], x[:, :vectors]], axis=1)


def tied(x, *earlier):
    anywhere = pl.BlockSpec(memory_space=pl.ANY)
    return pl.pallas_call(
        lambda *refs: None,
        in_specs=[anywhere] * (1 + len(earlier)),
        out_specs=anywhere,
        out_shape=jax.ShapeDtypeStruct(x.shape, x.dtype),
        input_output_aliases={0: 0},
    )(x, *earlier)


def pair_kernel(slot, count_ref, tau_ref, sink_ref, source_ref, *refs):
    out_ref, tile_ref, swap_ref, left_ref = refs[-4:]
    slots = sink_ref.shape[0]
    rows, packed = tile_ref.shape
    vectors = packed // 2
    blocks = rows // vectors
    first_half = lax.broadcasted_iota(jnp.int32, (vectors, packed), 1) < vectors

    @pl.when(pl.program_id(0) == 0)
    def _():
        for d in range(slots):
            out_ref[d, 0] = 0.0
            out_ref[d, 1] = 0.0

    for b in range(blocks):
        tile = tau_ref[:, 0, :, b * packed : (b + 1) * packed].reshape(vectors, packed)
        tile_ref[b * vectors : (b + 1) * vectors, :] = tile
        part = halves_swapped(tile)
        swap_ref[b * vectors : (b + 1) * vectors, :] = jnp.where(first_half, -part, part)

    for d in range(slots):

        @pl.when(d < count_ref[slot])
        def _():
            sink = sink_ref[d]
            embedding = jnp.concatenate(
                [jnp.where(first_half, sink, -sink), halves_swapped(sink)], axis=0
            )
            left_ref[...] = lax.dot_general(
                tile_ref[...], embedding, NT_DIMS, preferred_element_type=jnp.float32
            ).astype(jnp.bfloat16)

            def joined(ref):
                return jnp.concatenate(
                    [ref[b * vectors : (b + 1) * vectors, :] for b in range(blocks)], axis=1
                )

            left = joined(left_ref)
            block_real = lax.dot_general(
                left, joined(tile_ref), NT_DIMS, preferred_element_type=jnp.float32
            )
            block_imag = lax.dot_general(
                left, joined(swap_ref), NT_DIMS, preferred_element_type=jnp.float32
            )
            source = source_ref[0, d].astype(jnp.float32)
            real = source[:, :vectors]
            imag = source[:, vectors:]
            out_ref[d, 0] += jnp.sum(real * block_real - imag * block_imag)
            out_ref[d, 1] += jnp.sum(real * block_imag + imag * block_real)


def pair_sums(tau, slot, sinks, sources, counts, *earlier):
    slots, vectors, packed = sinks.shape
    spins = tau.shape[0] * tau.shape[2] // vectors
    layer, columns, width = tau.shape[0] // spins, tau.shape[2], tau.shape[3]
    smem = pl.BlockSpec(memory_space=pltpu.SMEM)
    flops = 4 * spins * slots * width * vectors * packed
    moved = 2 * (spins * vectors * width + 2 * slots * vectors * packed)
    rows = vectors * width // packed
    return pl.pallas_call(
        functools.partial(pair_kernel, slot),
        grid=(spins,),
        in_specs=[
            smem,
            pl.BlockSpec((layer, 1, columns, width), lambda s: (s, slot, 0, 0)),
            pl.BlockSpec((slots, vectors, packed), lambda s: (0, 0, 0)),
            pl.BlockSpec((1, slots, vectors, packed), lambda s: (slot, 0, 0, 0)),
        ]
        + [pl.BlockSpec(memory_space=pl.ANY)] * len(earlier),
        out_specs=smem,
        out_shape=jax.ShapeDtypeStruct((slots, 2), jnp.float32),
        scratch_shapes=[pltpu.VMEM((rows, packed), jnp.bfloat16)] * 3,
        compiler_params=pltpu.CompilerParams(vmem_limit_bytes=32 * 1024 * 1024),
        cost_estimate=pl.CostEstimate(flops=flops, bytes_accessed=moved, transcendentals=0),
    )(counts, tau, sinks, sources, *earlier)


def body(perambulator, elementals, diagrams, counts):
    devices = lax.axis_size("tm")
    me = lax.axis_index("tm")
    pair_count, slots = diagrams.shape[:2]
    columns, width = perambulator.shape[1:]
    vectors, packed = elementals.shape[2:]
    half = devices // 2
    own_set = elementals[0]
    high = (me >= half).astype(jnp.int32)
    halves = [list(range(half)), list(range(half, devices))]

    grouped = perambulator.reshape(2, half, pair_count, columns, width)

    def regrouped(which, *earlier):
        sent = lax.dynamic_index_in_dim(grouped, which, 0, keepdims=False)
        tau = lax.all_to_all(
            tied(sent, *earlier),
            "tm",
            split_axis=0,
            concat_axis=0,
            axis_index_groups=halves,
            tiled=True,
        )
        if columns % 16 != 0:
            tau = jnp.moveaxis(tau, 1, 0).reshape(pair_count, -1, vectors, width)
            tau = jnp.moveaxis(tau, 0, 1)
        return tau

    steps = [(slot + 1) * devices // (pair_count + 1) for slot in range(pair_count)]
    wanted = [passed_along(diagrams[slot, :, 0], by) for slot, by in enumerate(steps)]
    given_counts = exchanged(counts, half)
    own_sources = jnp.take(own_set, diagrams[:, :, 1].reshape(-1), axis=0, mode="clip")
    own_sources = own_sources.reshape(pair_count, slots, vectors, packed)
    given_sources = exchanged(own_sources, half)
    chosen = [jnp.take(own_set, index, axis=0, mode="clip") for index in wanted]
    given_sinks = [passed_along(sets, -by, half) for by, sets in zip(steps, chosen)]
    given_tau = regrouped(1 - high, given_counts, *wanted)
    own_tau = regrouped(high, given_tau, given_sources, *given_sinks)
    own_sinks = [passed_along(sets, -by) for by, sets in zip(steps, chosen)]

    given = [
        pair_sums(given_tau, slot, given_sinks[slot], given_sources, given_counts)
        for slot in range(pair_count)
    ]
    kept = [
        pair_sums(own_tau, slot, own_sinks[slot], own_sources, counts, *given)
        for slot in range(pair_count)
    ]
    got = exchanged(tied(jnp.stack(given), kept[0]), half)
    return (jnp.stack(kept) + got) / (columns * devices)


def solution(mesh):
    return jax.shard_map(
        body,
        mesh=mesh,
        in_specs=(
            P("groups", "tm", None),
            P(("groups", "tm"), None, None, None),
            P("tm", None, None),
            P("tm"),
        ),
        out_specs=P(("groups", "tm"), None, None),
        check_vma=False,
    )
```

```python
import functools

import jax
import jax.numpy as jnp
from jax import lax
from jax.experimental import pallas as pl
from jax.experimental.pallas import tpu as pltpu
from jax.sharding import PartitionSpec as P

NT_DIMS = (((1,), (1,)), ((), ()))
ANYWHERE = pl.BlockSpec(memory_space=pl.ANY)
SMEM = pl.BlockSpec(memory_space=pltpu.SMEM)


def exchanged(x, mask):
    devices = lax.axis_size("tm")
    return lax.ppermute(x, "tm", [(i, i ^ mask) for i in range(devices)])


def passed_along(x, by, mask=0):
    devices = lax.axis_size("tm")
    return lax.ppermute(x, "tm", [(i, ((i + by) % devices) ^ mask) for i in range(devices)])


def regroup_kernel(high_ref, source_ref, *refs):
    out_ref, sems = refs[-2:]
    high = high_ref[0]
    copies = []
    for j in range(source_ref.shape[1]):
        for side in range(2):
            which = 1 - high if side == 0 else high
            copies.append(
                pltpu.make_async_copy(
                    source_ref.at[which, j], out_ref.at[j, side], sems.at[2 * j + side]
                )
            )
    for copy in copies:
        copy.start()
    for copy in copies:
        copy.wait()


def regrouped(perambulator, high, half, pair_count, *earlier):
    columns, width = perambulator.shape[1:]
    source = perambulator.reshape(2, half, pair_count, columns, width)
    return pl.pallas_call(
        regroup_kernel,
        in_specs=[SMEM, ANYWHERE] + [ANYWHERE] * len(earlier),
        out_specs=ANYWHERE,
        out_shape=jax.ShapeDtypeStruct((half, 2, pair_count, columns, width), perambulator.dtype),
        scratch_shapes=[pltpu.SemaphoreType.DMA((2 * half,))],
    )(high.reshape(1), source, *earlier)


def halves_swapped(x):
    vectors = x.shape[1] // 2
    return jnp.concatenate([x[:, vectors:], x[:, :vectors]], axis=1)


def pairs_kernel(pair_count, counts_ref, tau_ref, *refs):
    sink_refs = refs[: 2 * pair_count]
    source_refs = refs[2 * pair_count : 2 * pair_count + 2]
    out_ref, sinks, sources, swap_ref, left_ref, sink_sems, source_sems = refs[-7:]
    slots, vectors, packed = sinks.shape[1:]
    spins, _, width = swap_ref.shape
    blocks = width // packed
    pieces = tau_ref.shape[0] // spins
    pair = pl.program_id(0)
    first_half = lax.broadcasted_iota(jnp.int32, (vectors, packed), 1) < vectors

    @pl.when(pair == 0)
    def _():
        for p in range(2 * pair_count):
            side, slot = divmod(p, pair_count)
            for d in range(slots):
                out_ref[p, d, 0] = 0.0
                out_ref[p, d, 1] = 0.0

                @pl.when(d < counts_ref[p])
                def _():
                    pltpu.make_async_copy(
                        sink_refs[p].at[d], sinks.at[p, d], sink_sems.at[p, d]
                    ).start()
                    pltpu.make_async_copy(
                        source_refs[side].at[slot, d], sources.at[p, d], source_sems.at[p, d]
                    ).start()

    def tile(s):
        return tau_ref[s * pieces : (s + 1) * pieces, 0].reshape(vectors, width)

    def part(x, b):
        return x[:, b * packed : (b + 1) * packed]

    for s in range(spins):
        for b in range(blocks):
            swapped = halves_swapped(part(tile(s), b))
            swap_ref[s, :, b * packed : (b + 1) * packed] = jnp.where(
                first_half, -swapped, swapped
            )

    @pl.loop(0, counts_ref[pair])
    def _(d):
        pltpu.make_async_copy(
            sink_refs[0].at[0], sinks.at[pair, d], sink_sems.at[pair, d]
        ).wait()
        sink = sinks[pair, d]
        embedding = jnp.concatenate(
            [jnp.where(first_half, sink, -sink), halves_swapped(sink)], axis=0
        )
        block_real = jnp.zeros((vectors, vectors), jnp.float32)
        block_imag = jnp.zeros((vectors, vectors), jnp.float32)
        for s in range(spins):
            stacked = jnp.concatenate([part(tile(s), b) for b in range(blocks)], axis=0)
            left = lax.dot_general(
                stacked, embedding, NT_DIMS, preferred_element_type=jnp.float32
            ).astype(jnp.bfloat16)
            for b in range(blocks):
                left_ref[s, :, b * packed : (b + 1) * packed] = left[
                    b * vectors : (b + 1) * vectors
                ]
        for s in range(spins):
            block_real += lax.dot_general(
                left_ref[s], tile(s), NT_DIMS, preferred_element_type=jnp.float32
            )
            block_imag += lax.dot_general(
                left_ref[s], swap_ref[s], NT_DIMS, preferred_element_type=jnp.float32
            )
        pltpu.make_async_copy(
            source_refs[0].at[0, 0], sources.at[pair, d], source_sems.at[pair, d]
        ).wait()
        source = sources[pair, d].astype(jnp.float32)
        real = source[:, :vectors]
        imag = source[:, vectors:]
        out_ref[pair, d, 0] = jnp.sum(real * block_real - imag * block_imag)
        out_ref[pair, d, 1] = jnp.sum(real * block_imag + imag * block_real)


def pairs_sums(tau, sinks, sources, counts):
    pairs = len(sinks)
    slots, vectors, packed = sinks[0].shape
    pieces, _, columns, width = tau.shape
    spins = pieces * columns // vectors
    flops = 4 * pairs * spins * slots * width * vectors * packed
    moved = 2 * pairs * (spins * vectors * width + 2 * slots * vectors * packed)
    return pl.pallas_call(
        functools.partial(pairs_kernel, pairs // 2),
        grid=(pairs,),
        in_specs=[SMEM, pl.BlockSpec((pieces, 1, columns, width), lambda p: (0, p, 0, 0))]
        + [ANYWHERE] * (pairs + 2),
        out_specs=SMEM,
        out_shape=jax.ShapeDtypeStruct((pairs, slots, 2), jnp.float32),
        scratch_shapes=[
            pltpu.VMEM((pairs, slots, vectors, packed), jnp.bfloat16),
            pltpu.VMEM((pairs, slots, vectors, packed), jnp.bfloat16),
            pltpu.VMEM((spins, vectors, width), jnp.bfloat16),
            pltpu.VMEM((spins, vectors, width), jnp.bfloat16),
            pltpu.SemaphoreType.DMA((pairs, slots)),
            pltpu.SemaphoreType.DMA((pairs, slots)),
        ],
        compiler_params=pltpu.CompilerParams(vmem_limit_bytes=40 * 1024 * 1024),
        cost_estimate=pl.CostEstimate(flops=flops, bytes_accessed=moved, transcendentals=0),
    )(counts, tau, *sinks, *sources)


def body(perambulator, elementals, diagrams, counts):
    devices = lax.axis_size("tm")
    me = lax.axis_index("tm")
    pair_count, slots = diagrams.shape[:2]
    columns, width = perambulator.shape[1:]
    vectors, packed = elementals.shape[2:]
    half = devices // 2
    own_set = elementals[0]
    high = (me >= half).astype(jnp.int32)
    halves = [list(range(half)), list(range(half, devices))]

    steps = [(slot + 1) * devices // (pair_count + 1) for slot in range(pair_count)]
    wanted = [passed_along(diagrams[slot, :, 0], by) for slot, by in enumerate(steps)]
    given_counts = exchanged(counts, half)
    own_sources = jnp.take(own_set, diagrams[:, :, 1].reshape(-1), axis=0, mode="clip")
    own_sources = own_sources.reshape(pair_count, slots, vectors, packed)
    given_sources = exchanged(own_sources, half)
    chosen = [jnp.take(own_set, index, axis=0, mode="clip") for index in wanted]
    given_sinks = [passed_along(sets, -by, half) for by, sets in zip(steps, chosen)]
    own_sinks = [passed_along(sets, -by) for by, sets in zip(steps, chosen)]

    tau = lax.all_to_all(
        regrouped(perambulator, high, half, pair_count, given_counts, *wanted),
        "tm",
        split_axis=0,
        concat_axis=0,
        axis_index_groups=halves,
        tiled=True,
    ).reshape(half, 2 * pair_count, columns, width)
    if columns % 16 != 0:
        tau = jnp.moveaxis(tau, 1, 0).reshape(2 * pair_count, -1, vectors, width)
        tau = jnp.moveaxis(tau, 0, 1)

    sums = pairs_sums(
        tau,
        given_sinks + own_sinks,
        (given_sources, own_sources),
        jnp.concatenate([given_counts, counts]),
    )
    got = exchanged(sums[:pair_count], half)
    return (sums[pair_count:] + got) / (columns * devices)


def solution(mesh):
    return jax.shard_map(
        body,
        mesh=mesh,
        in_specs=(
            P("groups", "tm", None),
            P(("groups", "tm"), None, None, None),
            P("tm", None, None),
            P("tm"),
        ),
        out_specs=P(("groups", "tm"), None, None),
        check_vma=False,
    )
```

```python
import functools

import jax
import jax.numpy as jnp
from jax import lax
from jax.experimental import pallas as pl
from jax.experimental.pallas import tpu as pltpu
from jax.sharding import PartitionSpec as P

NT_DIMS = (((1,), (1,)), ((), ()))
ANYWHERE = pl.BlockSpec(memory_space=pl.ANY)
HBM = pl.BlockSpec(memory_space=pltpu.HBM)
SMEM = pl.BlockSpec(memory_space=pltpu.SMEM)


def exchanged(x, mask):
    devices = lax.axis_size("tm")
    return lax.ppermute(x, "tm", [(i, i ^ mask) for i in range(devices)])


def passed_along(x, by, mask=0):
    devices = lax.axis_size("tm")
    return lax.ppermute(x, "tm", [(i, ((i + by) % devices) ^ mask) for i in range(devices)])


def regroup_kernel(high_ref, source_ref, out_ref, sems):
    high = high_ref[0]
    copies = []
    for j in range(source_ref.shape[1]):
        for side in range(2):
            which = 1 - high if side == 0 else high
            copies.append(
                pltpu.make_async_copy(
                    source_ref.at[which, j], out_ref.at[j, side], sems.at[2 * j + side]
                )
            )
    for copy in copies:
        copy.start()
    for copy in copies:
        copy.wait()


def regrouped(perambulator, high, half, pair_count):
    columns, width = perambulator.shape[1:]
    source = perambulator.reshape(2, half, pair_count, columns, width)
    return pl.pallas_call(
        regroup_kernel,
        in_specs=[SMEM, HBM],
        out_specs=pl.BlockSpec(memory_space=pltpu.VMEM),
        out_shape=jax.ShapeDtypeStruct((half, 2, pair_count, columns, width), perambulator.dtype),
        scratch_shapes=[pltpu.SemaphoreType.DMA((2 * half,))],
        compiler_params=pltpu.CompilerParams(vmem_limit_bytes=56 * 1024 * 1024),
    )(high.reshape(1), source)


def tied(x, *earlier):
    return pl.pallas_call(
        lambda *refs: None,
        in_specs=[ANYWHERE] * (1 + len(earlier)),
        out_specs=ANYWHERE,
        out_shape=jax.ShapeDtypeStruct(x.shape, x.dtype),
        input_output_aliases={0: 0},
    )(x, *earlier)


def halves_swapped(x):
    vectors = x.shape[1] // 2
    return jnp.concatenate([x[:, vectors:], x[:, :vectors]], axis=1)


def pairs_kernel(pair_count, counts_ref, tau_ref, *refs):
    sink_refs = refs[: 2 * pair_count]
    source_refs = refs[2 * pair_count : 2 * pair_count + 2]
    out_ref, sinks, sources, swap_ref, left_ref, sink_sems, source_sems = refs[-7:]
    slots, vectors, packed = sinks.shape[1:]
    spins, _, width = swap_ref.shape
    blocks = width // packed
    pieces = tau_ref.shape[0] // spins
    pair = pl.program_id(0)
    first_half = lax.broadcasted_iota(jnp.int32, (vectors, packed), 1) < vectors

    @pl.when(pair == 0)
    def _():
        for p in range(2 * pair_count):
            side, slot = divmod(p, pair_count)
            for d in range(slots):
                out_ref[p, d, 0] = 0.0
                out_ref[p, d, 1] = 0.0

                @pl.when(d < counts_ref[p])
                def _():
                    pltpu.make_async_copy(
                        sink_refs[p].at[d], sinks.at[p, d], sink_sems.at[p, d]
                    ).start()
                    pltpu.make_async_copy(
                        source_refs[side].at[slot, d], sources.at[p, d], source_sems.at[p, d]
                    ).start()

    def tile(s):
        return tau_ref[s * pieces : (s + 1) * pieces, 0].reshape(vectors, width)

    def part(x, b):
        return x[:, b * packed : (b + 1) * packed]

    for s in range(spins):
        for b in range(blocks):
            swapped = halves_swapped(part(tile(s), b))
            swap_ref[s, :, b * packed : (b + 1) * packed] = jnp.where(
                first_half, -swapped, swapped
            )

    @pl.loop(0, counts_ref[pair])
    def _(d):
        pltpu.make_async_copy(
            sink_refs[0].at[0], sinks.at[pair, d], sink_sems.at[pair, d]
        ).wait()
        sink = sinks[pair, d]
        embedding = jnp.concatenate(
            [jnp.where(first_half, sink, -sink), halves_swapped(sink)], axis=0
        )
        block_real = jnp.zeros((vectors, vectors), jnp.float32)
        block_imag = jnp.zeros((vectors, vectors), jnp.float32)
        for s in range(spins):
            stacked = jnp.concatenate([part(tile(s), b) for b in range(blocks)], axis=0)
            left = lax.dot_general(
                stacked, embedding, NT_DIMS, preferred_element_type=jnp.float32
            ).astype(jnp.bfloat16)
            for b in range(blocks):
                left_ref[s, :, b * packed : (b + 1) * packed] = left[
                    b * vectors : (b + 1) * vectors
                ]
        for s in range(spins):
            block_real += lax.dot_general(
                left_ref[s], tile(s), NT_DIMS, preferred_element_type=jnp.float32
            )
            block_imag += lax.dot_general(
                left_ref[s], swap_ref[s], NT_DIMS, preferred_element_type=jnp.float32
            )
        pltpu.make_async_copy(
            source_refs[0].at[0, 0], sources.at[pair, d], source_sems.at[pair, d]
        ).wait()
        source = sources[pair, d].astype(jnp.float32)
        real = source[:, :vectors]
        imag = source[:, vectors:]
        out_ref[pair, d, 0] = jnp.sum(real * block_real - imag * block_imag)
        out_ref[pair, d, 1] = jnp.sum(real * block_imag + imag * block_real)


def pairs_sums(tau, sinks, sources, counts):
    pairs = len(sinks)
    slots, vectors, packed = sinks[0].shape
    pieces, _, columns, width = tau.shape
    spins = pieces * columns // vectors
    flops = 4 * pairs * spins * slots * width * vectors * packed
    moved = 2 * pairs * (spins * vectors * width + 2 * slots * vectors * packed)
    return pl.pallas_call(
        functools.partial(pairs_kernel, pairs // 2),
        grid=(pairs,),
        in_specs=[SMEM, pl.BlockSpec((pieces, 1, columns, width), lambda p: (0, p, 0, 0))]
        + [HBM] * (pairs + 2),
        out_specs=SMEM,
        out_shape=jax.ShapeDtypeStruct((pairs, slots, 2), jnp.float32),
        scratch_shapes=[
            pltpu.VMEM((pairs, slots, vectors, packed), jnp.bfloat16),
            pltpu.VMEM((pairs, slots, vectors, packed), jnp.bfloat16),
            pltpu.VMEM((spins, vectors, width), jnp.bfloat16),
            pltpu.VMEM((spins, vectors, width), jnp.bfloat16),
            pltpu.SemaphoreType.DMA((pairs, slots)),
            pltpu.SemaphoreType.DMA((pairs, slots)),
        ],
        compiler_params=pltpu.CompilerParams(vmem_limit_bytes=56 * 1024 * 1024),
        cost_estimate=pl.CostEstimate(flops=flops, bytes_accessed=moved, transcendentals=0),
    )(counts, tau, *sinks, *sources)


def body(perambulator, elementals, diagrams, counts):
    devices = lax.axis_size("tm")
    me = lax.axis_index("tm")
    pair_count, slots = diagrams.shape[:2]
    columns, width = perambulator.shape[1:]
    vectors, packed = elementals.shape[2:]
    half = devices // 2
    own_set = elementals[0]
    high = (me >= half).astype(jnp.int32)
    halves = [list(range(half)), list(range(half, devices))]

    steps = [(slot + 1) * devices // (pair_count + 1) for slot in range(pair_count)]
    wanted = [passed_along(diagrams[slot, :, 0], by) for slot, by in enumerate(steps)]
    given_counts = exchanged(counts, half)
    own_sources = jnp.take(own_set, diagrams[:, :, 1].reshape(-1), axis=0, mode="clip")
    own_sources = own_sources.reshape(pair_count, slots, vectors, packed)
    given_sources = exchanged(own_sources, half)
    chosen = [jnp.take(own_set, index, axis=0, mode="clip") for index in wanted]
    given_sinks = [passed_along(sets, -by, half) for by, sets in zip(steps, chosen)]
    own_sinks = [passed_along(sets, -by) for by, sets in zip(steps, chosen)]

    tau = lax.all_to_all(
        tied(regrouped(perambulator, high, half, pair_count), given_counts, *wanted),
        "tm",
        split_axis=0,
        concat_axis=0,
        axis_index_groups=halves,
        tiled=True,
    ).reshape(half, 2 * pair_count, columns, width)
    if columns % 16 != 0:
        tau = jnp.moveaxis(tau, 1, 0).reshape(2 * pair_count, -1, vectors, width)
        tau = jnp.moveaxis(tau, 0, 1)

    sums = pairs_sums(
        tau,
        given_sinks + own_sinks,
        (given_sources, own_sources),
        jnp.concatenate([given_counts, counts]),
    )
    got = exchanged(sums[:pair_count], half)
    return (sums[pair_count:] + got) / (columns * devices)


def solution(mesh):
    return jax.shard_map(
        body,
        mesh=mesh,
        in_specs=(
            P("groups", "tm", None),
            P(("groups", "tm"), None, None, None),
            P("tm", None, None),
            P("tm"),
        ),
        out_specs=P(("groups", "tm"), None, None),
        check_vma=False,
    )
```

```python
import functools

import jax
import jax.numpy as jnp
from jax import lax
from jax.experimental import pallas as pl
from jax.experimental.pallas import tpu as pltpu
from jax.sharding import PartitionSpec as P

NT_DIMS = (((1,), (1,)), ((), ()))
ANYWHERE = pl.BlockSpec(memory_space=pl.ANY)
HBM = pl.BlockSpec(memory_space=pltpu.HBM)
SMEM = pl.BlockSpec(memory_space=pltpu.SMEM)


def exchanged(x, mask):
    devices = lax.axis_size("tm")
    return lax.ppermute(x, "tm", [(i, i ^ mask) for i in range(devices)])


def passed_along(x, by, mask=0):
    devices = lax.axis_size("tm")
    return lax.ppermute(x, "tm", [(i, ((i + by) % devices) ^ mask) for i in range(devices)])


def slice_kernel(which_ref, source_ref, out_ref, sems):
    copies = [
        pltpu.make_async_copy(source_ref.at[which_ref[0], j], out_ref.at[j], sems.at[j])
        for j in range(source_ref.shape[1])
    ]
    for copy in copies:
        copy.start()
    for copy in copies:
        copy.wait()


def sliced(source, which):
    return pl.pallas_call(
        slice_kernel,
        in_specs=[SMEM, HBM],
        out_specs=pl.BlockSpec(memory_space=pltpu.VMEM),
        out_shape=jax.ShapeDtypeStruct(source.shape[1:], source.dtype),
        scratch_shapes=[pltpu.SemaphoreType.DMA((source.shape[1],))],
        compiler_params=pltpu.CompilerParams(vmem_limit_bytes=56 * 1024 * 1024),
    )(which.reshape(1), source)


def tied(x, *earlier):
    return pl.pallas_call(
        lambda *refs: None,
        in_specs=[ANYWHERE] * (1 + len(earlier)),
        out_specs=ANYWHERE,
        out_shape=jax.ShapeDtypeStruct(x.shape, x.dtype),
        input_output_aliases={0: 0},
    )(x, *earlier)


def halves_swapped(x):
    vectors = x.shape[1] // 2
    return jnp.concatenate([x[:, vectors:], x[:, :vectors]], axis=1)


def pairs_kernel(pairs, counts_ref, tau_ref, *refs):
    sink_refs = refs[:pairs]
    source_ref = refs[pairs]
    out_ref, sinks, sources, swap_ref, left_ref, sink_sems, source_sems = refs[-7:]
    slots, vectors, packed = sinks.shape[1:]
    spins, _, width = swap_ref.shape
    blocks = width // packed
    pieces = tau_ref.shape[0] // spins
    pair = pl.program_id(0)
    first_half = lax.broadcasted_iota(jnp.int32, (vectors, packed), 1) < vectors

    @pl.when(pair == 0)
    def _():
        for p in range(pairs):
            for d in range(slots):
                out_ref[p, d, 0] = 0.0
                out_ref[p, d, 1] = 0.0

                @pl.when(d < counts_ref[p])
                def _():
                    pltpu.make_async_copy(
                        sink_refs[p].at[d], sinks.at[p, d], sink_sems.at[p, d]
                    ).start()
                    pltpu.make_async_copy(
                        source_ref.at[p, d], sources.at[p, d], source_sems.at[p, d]
                    ).start()

    def tile(s):
        return tau_ref[s * pieces : (s + 1) * pieces, 0].reshape(vectors, width)

    def part(x, b):
        return x[:, b * packed : (b + 1) * packed]

    for s in range(spins):
        for b in range(blocks):
            swapped = halves_swapped(part(tile(s), b))
            swap_ref[s, :, b * packed : (b + 1) * packed] = jnp.where(
                first_half, -swapped, swapped
            )

    @pl.loop(0, counts_ref[pair])
    def _(d):
        pltpu.make_async_copy(
            sink_refs[0].at[0], sinks.at[pair, d], sink_sems.at[pair, d]
        ).wait()
        sink = sinks[pair, d]
        embedding = jnp.concatenate(
            [jnp.where(first_half, sink, -sink), halves_swapped(sink)], axis=0
        )
        block_real = jnp.zeros((vectors, vectors), jnp.float32)
        block_imag = jnp.zeros((vectors, vectors), jnp.float32)
        for s in range(spins):
            stacked = jnp.concatenate([part(tile(s), b) for b in range(blocks)], axis=0)
            left = lax.dot_general(
                stacked, embedding, NT_DIMS, preferred_element_type=jnp.float32
            ).astype(jnp.bfloat16)
            for b in range(blocks):
                left_ref[s, :, b * packed : (b + 1) * packed] = left[
                    b * vectors : (b + 1) * vectors
                ]
        for s in range(spins):
            block_real += lax.dot_general(
                left_ref[s], tile(s), NT_DIMS, preferred_element_type=jnp.float32
            )
            block_imag += lax.dot_general(
                left_ref[s], swap_ref[s], NT_DIMS, preferred_element_type=jnp.float32
            )
        pltpu.make_async_copy(
            source_ref.at[0, 0], sources.at[pair, d], source_sems.at[pair, d]
        ).wait()
        source = sources[pair, d].astype(jnp.float32)
        real = source[:, :vectors]
        imag = source[:, vectors:]
        out_ref[pair, d, 0] = jnp.sum(real * block_real - imag * block_imag)
        out_ref[pair, d, 1] = jnp.sum(real * block_imag + imag * block_real)


def pairs_sums(tau, sinks, sources, counts, *earlier):
    pairs = len(sinks)
    slots, vectors, packed = sinks[0].shape
    pieces, _, columns, width = tau.shape
    spins = pieces * columns // vectors
    flops = 4 * pairs * spins * slots * width * vectors * packed
    moved = 2 * pairs * (spins * vectors * width + 2 * slots * vectors * packed)
    return pl.pallas_call(
        functools.partial(pairs_kernel, pairs),
        grid=(pairs,),
        in_specs=[SMEM, pl.BlockSpec((pieces, 1, columns, width), lambda p: (0, p, 0, 0))]
        + [HBM] * (pairs + 1)
        + [ANYWHERE] * len(earlier),
        out_specs=SMEM,
        out_shape=jax.ShapeDtypeStruct((pairs, slots, 2), jnp.float32),
        scratch_shapes=[
            pltpu.VMEM((pairs, slots, vectors, packed), jnp.bfloat16),
            pltpu.VMEM((pairs, slots, vectors, packed), jnp.bfloat16),
            pltpu.VMEM((spins, vectors, width), jnp.bfloat16),
            pltpu.VMEM((spins, vectors, width), jnp.bfloat16),
            pltpu.SemaphoreType.DMA((pairs, slots)),
            pltpu.SemaphoreType.DMA((pairs, slots)),
        ],
        compiler_params=pltpu.CompilerParams(vmem_limit_bytes=56 * 1024 * 1024),
        cost_estimate=pl.CostEstimate(flops=flops, bytes_accessed=moved, transcendentals=0),
    )(counts, tau, *sinks, sources, *earlier)


def body(perambulator, elementals, diagrams, counts):
    devices = lax.axis_size("tm")
    me = lax.axis_index("tm")
    pair_count, slots = diagrams.shape[:2]
    columns, width = perambulator.shape[1:]
    vectors, packed = elementals.shape[2:]
    half = devices // 2
    own_set = elementals[0]
    high = (me >= half).astype(jnp.int32)
    halves = [list(range(half)), list(range(half, devices))]

    steps = [(slot + 1) * devices // (pair_count + 1) for slot in range(pair_count)]
    wanted = [passed_along(diagrams[slot, :, 0], by) for slot, by in enumerate(steps)]
    given_counts = exchanged(counts, half)
    own_sources = jnp.take(own_set, diagrams[:, :, 1].reshape(-1), axis=0, mode="clip")
    own_sources = own_sources.reshape(pair_count, slots, vectors, packed)
    given_sources = exchanged(own_sources, half)
    chosen = [jnp.take(own_set, index, axis=0, mode="clip") for index in wanted]
    given_sinks = [passed_along(sets, -by, half) for by, sets in zip(steps, chosen)]
    own_sinks = [passed_along(sets, -by) for by, sets in zip(steps, chosen)]

    grouped = perambulator.reshape(2, half, pair_count, columns, width)

    def regrouped(which, *earlier):
        tau = lax.all_to_all(
            tied(sliced(grouped, which), *earlier),
            "tm",
            split_axis=0,
            concat_axis=0,
            axis_index_groups=halves,
            tiled=True,
        )
        if columns % 16 != 0:
            tau = jnp.moveaxis(tau, 1, 0).reshape(pair_count, -1, vectors, width)
            tau = jnp.moveaxis(tau, 0, 1)
        return tau

    given_tau = regrouped(1 - high, given_counts, *wanted)
    own_tau = regrouped(high, given_tau, given_sources, *given_sinks)
    given = pairs_sums(given_tau, given_sinks, given_sources, given_counts)
    got = exchanged(given, half)
    kept = pairs_sums(own_tau, own_sinks, own_sources, counts, given)
    return (kept + got) / (columns * devices)


def solution(mesh):
    return jax.shard_map(
        body,
        mesh=mesh,
        in_specs=(
            P("groups", "tm", None),
            P(("groups", "tm"), None, None, None),
            P("tm", None, None),
            P("tm"),
        ),
        out_specs=P(("groups", "tm"), None, None),
        check_vma=False,
    )
```

```python
import functools

import jax
import jax.numpy as jnp
from jax import lax
from jax.experimental import pallas as pl
from jax.experimental.pallas import tpu as pltpu
from jax.sharding import PartitionSpec as P

NT_DIMS = (((1,), (1,)), ((), ()))
ANYWHERE = pl.BlockSpec(memory_space=pl.ANY)
VMEM_BYTES = 32 * 1024 * 1024
VMEM = pl.BlockSpec(memory_space=pltpu.VMEM)
SMEM = pl.BlockSpec(memory_space=pltpu.SMEM)


def exchanged(x, mask):
    devices = lax.axis_size("tm")
    return lax.ppermute(x, "tm", [(i, i ^ mask) for i in range(devices)])


def passed_along(x, by, mask=0):
    devices = lax.axis_size("tm")
    return lax.ppermute(x, "tm", [(i, ((i + by) % devices) ^ mask) for i in range(devices)])


def slice_kernel(which_ref, source_ref, out_ref, sems):
    copies = [
        pltpu.make_async_copy(source_ref.at[which_ref[0], j], out_ref.at[j], sems.at[j])
        for j in range(source_ref.shape[1])
    ]
    for copy in copies:
        copy.start()
    for copy in copies:
        copy.wait()


def sliced(source, which):
    return pl.pallas_call(
        slice_kernel,
        in_specs=[SMEM, ANYWHERE],
        out_specs=VMEM,
        out_shape=jax.ShapeDtypeStruct(source.shape[1:], source.dtype),
        scratch_shapes=[pltpu.SemaphoreType.DMA((source.shape[1],))],
        compiler_params=pltpu.CompilerParams(vmem_limit_bytes=58 * 1024 * 1024),
    )(which.reshape(1), source)


def tied(x, *earlier):
    return pl.pallas_call(
        lambda *refs: None,
        in_specs=[ANYWHERE] * (1 + len(earlier)),
        out_specs=ANYWHERE,
        out_shape=jax.ShapeDtypeStruct(x.shape, x.dtype),
        input_output_aliases={0: 0},
    )(x, *earlier)


def halves_swapped(x):
    vectors = x.shape[1] // 2
    return jnp.concatenate([x[:, vectors:], x[:, :vectors]], axis=1)


def pairs_kernel(pairs, scale, counts_ref, begin_ref, tau_ref, *refs):
    sink_refs = refs[:pairs]
    source_ref = refs[pairs]
    out_ref, swap_ref, left_ref = refs[-3:]
    slots, vectors, packed = source_ref.shape[1:]
    spins, _, width = swap_ref.shape
    blocks = width // packed
    pieces = tau_ref.shape[0] // spins
    pair = pl.program_id(0)
    first_half = lax.broadcasted_iota(jnp.int32, (vectors, packed), 1) < vectors

    @pl.when(pair == 0)
    def _():
        for p in range(pairs):
            for d in range(slots):
                out_ref[p, d, 0] = begin_ref[p, d, 0] * scale
                out_ref[p, d, 1] = begin_ref[p, d, 1] * scale

    def tile(s):
        return tau_ref[s * pieces : (s + 1) * pieces, 0].reshape(vectors, width)

    def part(x, b):
        return x[:, b * packed : (b + 1) * packed]

    for s in range(spins):
        for b in range(blocks):
            swapped = halves_swapped(part(tile(s), b))
            swap_ref[s, :, b * packed : (b + 1) * packed] = jnp.where(
                first_half, -swapped, swapped
            )

    def add_diagram(sink_ref, d):
        sink = sink_ref[d]
        embedding = jnp.concatenate(
            [jnp.where(first_half, sink, -sink), halves_swapped(sink)], axis=0
        )
        block_real = jnp.zeros((vectors, vectors), jnp.float32)
        block_imag = jnp.zeros((vectors, vectors), jnp.float32)
        for s in range(spins):
            stacked = jnp.concatenate([part(tile(s), b) for b in range(blocks)], axis=0)
            left = lax.dot_general(
                stacked, embedding, NT_DIMS, preferred_element_type=jnp.float32
            ).astype(jnp.bfloat16)
            for b in range(blocks):
                left_ref[s, :, b * packed : (b + 1) * packed] = left[
                    b * vectors : (b + 1) * vectors
                ]
        for s in range(spins):
            block_real += lax.dot_general(
                left_ref[s], tile(s), NT_DIMS, preferred_element_type=jnp.float32
            )
            block_imag += lax.dot_general(
                left_ref[s], swap_ref[s], NT_DIMS, preferred_element_type=jnp.float32
            )
        source = source_ref[pair, d].astype(jnp.float32)
        real = source[:, :vectors]
        imag = source[:, vectors:]
        out_ref[pair, d, 0] += jnp.sum(real * block_real - imag * block_imag) * scale
        out_ref[pair, d, 1] += jnp.sum(real * block_imag + imag * block_real) * scale

    for p in range(pairs):

        @pl.when(pair == p)
        def _():
            pl.loop(0, counts_ref[p])(functools.partial(add_diagram, sink_refs[p]))


def pairs_sums(tau, sinks, sources, counts, begin, scale):
    pairs = len(sinks)
    slots, vectors, packed = sinks[0].shape
    pieces, _, columns, width = tau.shape
    spins = pieces * columns // vectors
    flops = 4 * pairs * spins * slots * width * vectors * packed
    moved = 2 * pairs * (spins * vectors * width + 2 * slots * vectors * packed)
    return pl.pallas_call(
        functools.partial(pairs_kernel, pairs, scale),
        grid=(pairs,),
        in_specs=[SMEM, SMEM, pl.BlockSpec((pieces, 1, columns, width), lambda p: (0, p, 0, 0))]
        + [VMEM] * (pairs + 1),
        out_specs=SMEM,
        out_shape=jax.ShapeDtypeStruct((pairs, slots, 2), jnp.float32),
        scratch_shapes=[
            pltpu.VMEM((spins, vectors, width), jnp.bfloat16),
            pltpu.VMEM((spins, vectors, width), jnp.bfloat16),
        ],
        compiler_params=pltpu.CompilerParams(vmem_limit_bytes=VMEM_BYTES),
        cost_estimate=pl.CostEstimate(flops=flops, bytes_accessed=moved, transcendentals=0),
    )(counts, begin, tau, *sinks, sources)


def body(perambulator, elementals, diagrams, counts):
    devices = lax.axis_size("tm")
    me = lax.axis_index("tm")
    pair_count, slots = diagrams.shape[:2]
    columns, width = perambulator.shape[1:]
    vectors, packed = elementals.shape[2:]
    half = devices // 2
    own_set = elementals[0]
    high = (me >= half).astype(jnp.int32)
    halves = [list(range(half)), list(range(half, devices))]

    steps = [(slot + 1) * devices // (pair_count + 1) for slot in range(pair_count)]
    wanted = [passed_along(diagrams[slot, :, 0], by) for slot, by in enumerate(steps)]
    given_counts = exchanged(counts, half)
    own_sources = jnp.take(own_set, diagrams[:, :, 1].reshape(-1), axis=0, mode="clip")
    own_sources = own_sources.reshape(pair_count, slots, vectors, packed)
    given_sources = exchanged(own_sources, half)
    chosen = [jnp.take(own_set, index, axis=0, mode="clip") for index in wanted]
    given_sinks = [passed_along(sets, -by, half) for by, sets in zip(steps, chosen)]
    own_sinks = [passed_along(sets, -by) for by, sets in zip(steps, chosen)]

    grouped = perambulator.reshape(2, half, pair_count, columns, width)

    def regrouped(which, *earlier):
        tau = lax.all_to_all(
            tied(sliced(grouped, which), *earlier),
            "tm",
            split_axis=0,
            concat_axis=0,
            axis_index_groups=halves,
            tiled=True,
        )
        if columns % 16 != 0:
            tau = jnp.moveaxis(tau, 1, 0).reshape(pair_count, -1, vectors, width)
            tau = jnp.moveaxis(tau, 0, 1)
        return tau

    given_tau = regrouped(1 - high, given_counts, *wanted)
    own_tau = regrouped(high, given_tau, given_sources, *given_sinks, *own_sinks)
    zeros = jnp.zeros((pair_count, slots, 2), jnp.float32)
    given = pairs_sums(given_tau, given_sinks, given_sources, given_counts, zeros, 1.0)
    got = exchanged(given, half)
    return pairs_sums(own_tau, own_sinks, own_sources, counts, got, 1.0 / (columns * devices))


def solution(mesh):
    return jax.shard_map(
        body,
        mesh=mesh,
        in_specs=(
            P("groups", "tm", None),
            P(("groups", "tm"), None, None, None),
            P("tm", None, None),
            P("tm"),
        ),
        out_specs=P(("groups", "tm"), None, None),
        check_vma=False,
    )
```

```python
import functools

import jax
import jax.numpy as jnp
from jax import lax
from jax.experimental import pallas as pl
from jax.experimental.pallas import tpu as pltpu
from jax.sharding import PartitionSpec as P

NT_DIMS = (((1,), (1,)), ((), ()))
ANYWHERE = pl.BlockSpec(memory_space=pl.ANY)
VMEM_BYTES = 56 * 1024 * 1024
HBM = pl.BlockSpec(memory_space=pltpu.HBM)
VMEM = pl.BlockSpec(memory_space=pltpu.VMEM)
SMEM = pl.BlockSpec(memory_space=pltpu.SMEM)


def exchanged(x, mask):
    devices = lax.axis_size("tm")
    return lax.ppermute(x, "tm", [(i, i ^ mask) for i in range(devices)])


def passed_along(x, by, mask=0):
    devices = lax.axis_size("tm")
    return lax.ppermute(x, "tm", [(i, ((i + by) % devices) ^ mask) for i in range(devices)])


def regroup_kernel(high_ref, source_ref, out_ref, sems):
    high = high_ref[0]
    copies = []
    for j in range(source_ref.shape[1]):
        for side in range(2):
            which = 1 - high if side == 0 else high
            copies.append(
                pltpu.make_async_copy(
                    source_ref.at[which, j], out_ref.at[j, side], sems.at[2 * j + side]
                )
            )
    for copy in copies:
        copy.start()
    for copy in copies:
        copy.wait()


def regrouped(perambulator, high, half, pair_count):
    columns, width = perambulator.shape[1:]
    source = perambulator.reshape(2, half, pair_count, columns, width)
    return pl.pallas_call(
        regroup_kernel,
        in_specs=[SMEM, HBM],
        out_specs=VMEM,
        out_shape=jax.ShapeDtypeStruct((half, 2, pair_count, columns, width), perambulator.dtype),
        scratch_shapes=[pltpu.SemaphoreType.DMA((2 * half,))],
        compiler_params=pltpu.CompilerParams(vmem_limit_bytes=58 * 1024 * 1024),
    )(high.reshape(1), source)


def select_kernel(index_ref, set_ref, out_ref, sems):
    copies = [
        pltpu.make_async_copy(
            set_ref.at[jnp.clip(index_ref[i], 0, set_ref.shape[0] - 1)], out_ref.at[i], sems.at[i]
        )
        for i in range(out_ref.shape[0])
    ]
    for copy in copies:
        copy.start()
    for copy in copies:
        copy.wait()


def selected(elementals, index):
    return pl.pallas_call(
        select_kernel,
        in_specs=[SMEM, ANYWHERE],
        out_specs=VMEM,
        out_shape=jax.ShapeDtypeStruct(index.shape + elementals.shape[1:], elementals.dtype),
        scratch_shapes=[pltpu.SemaphoreType.DMA(index.shape)],
    )(index, elementals)


def tied(x, *earlier):
    return pl.pallas_call(
        lambda *refs: None,
        in_specs=[ANYWHERE] * (1 + len(earlier)),
        out_specs=ANYWHERE,
        out_shape=jax.ShapeDtypeStruct(x.shape, x.dtype),
        input_output_aliases={0: 0},
    )(x, *earlier)


def halves_swapped(x):
    vectors = x.shape[1] // 2
    return jnp.concatenate([x[:, vectors:], x[:, :vectors]], axis=1)


def pairs_kernel(pairs, scale, counts_ref, begin_ref, tau_ref, *refs):
    sink_refs = refs[:pairs]
    source_ref = refs[pairs]
    out_ref, sinks, sources, swap_ref, left_ref, sink_sems, source_sems = refs[-7:]
    slots, vectors, packed = sinks.shape[1:]
    spins, _, width = swap_ref.shape
    blocks = width // packed
    pieces = tau_ref.shape[0] // spins
    pair = pl.program_id(0)
    first_half = lax.broadcasted_iota(jnp.int32, (vectors, packed), 1) < vectors

    @pl.when(pair == 0)
    def _():
        for p in range(pairs):
            for d in range(slots):
                out_ref[p, d, 0] = begin_ref[p, d, 0] * scale
                out_ref[p, d, 1] = begin_ref[p, d, 1] * scale

                @pl.when(d < counts_ref[p])
                def _():
                    pltpu.make_async_copy(
                        sink_refs[p].at[d], sinks.at[p, d], sink_sems.at[p, d]
                    ).start()
                    pltpu.make_async_copy(
                        source_ref.at[p, d], sources.at[p, d], source_sems.at[p, d]
                    ).start()

    def tile(s):
        return tau_ref[s * pieces : (s + 1) * pieces, 0].reshape(vectors, width)

    def part(x, b):
        return x[:, b * packed : (b + 1) * packed]

    for s in range(spins):
        for b in range(blocks):
            swapped = halves_swapped(part(tile(s), b))
            swap_ref[s, :, b * packed : (b + 1) * packed] = jnp.where(
                first_half, -swapped, swapped
            )

    @pl.loop(0, counts_ref[pair])
    def _(d):
        pltpu.make_async_copy(
            sink_refs[0].at[0], sinks.at[pair, d], sink_sems.at[pair, d]
        ).wait()
        sink = sinks[pair, d]
        embedding = jnp.concatenate(
            [jnp.where(first_half, sink, -sink), halves_swapped(sink)], axis=0
        )
        block_real = jnp.zeros((vectors, vectors), jnp.float32)
        block_imag = jnp.zeros((vectors, vectors), jnp.float32)
        for s in range(spins):
            stacked = jnp.concatenate([part(tile(s), b) for b in range(blocks)], axis=0)
            left = lax.dot_general(
                stacked, embedding, NT_DIMS, preferred_element_type=jnp.float32
            ).astype(jnp.bfloat16)
            for b in range(blocks):
                left_ref[s, :, b * packed : (b + 1) * packed] = left[
                    b * vectors : (b + 1) * vectors
                ]
        for s in range(spins):
            block_real += lax.dot_general(
                left_ref[s], tile(s), NT_DIMS, preferred_element_type=jnp.float32
            )
            block_imag += lax.dot_general(
                left_ref[s], swap_ref[s], NT_DIMS, preferred_element_type=jnp.float32
            )
        pltpu.make_async_copy(
            source_ref.at[0, 0], sources.at[pair, d], source_sems.at[pair, d]
        ).wait()
        source = sources[pair, d].astype(jnp.float32)
        real = source[:, :vectors]
        imag = source[:, vectors:]
        out_ref[pair, d, 0] += jnp.sum(real * block_real - imag * block_imag) * scale
        out_ref[pair, d, 1] += jnp.sum(real * block_imag + imag * block_real) * scale


def pairs_sums(tau, first, sinks, sources, counts, begin, scale):
    pairs = len(sinks)
    slots, vectors, packed = sinks[0].shape
    pieces, _, columns, width = tau.shape
    spins = pieces * columns // vectors
    flops = 4 * pairs * spins * slots * width * vectors * packed
    moved = 2 * pairs * (spins * vectors * width + 2 * slots * vectors * packed)
    return pl.pallas_call(
        functools.partial(pairs_kernel, pairs, scale),
        grid=(pairs,),
        in_specs=[
            SMEM,
            SMEM,
            pl.BlockSpec((pieces, 1, columns, width), lambda p: (0, first + p, 0, 0)),
        ]
        + [HBM] * (pairs + 1),
        out_specs=SMEM,
        out_shape=jax.ShapeDtypeStruct((pairs, slots, 2), jnp.float32),
        scratch_shapes=[
            pltpu.VMEM((pairs, slots, vectors, packed), jnp.bfloat16),
            pltpu.VMEM((pairs, slots, vectors, packed), jnp.bfloat16),
            pltpu.VMEM((spins, vectors, width), jnp.bfloat16),
            pltpu.VMEM((spins, vectors, width), jnp.bfloat16),
            pltpu.SemaphoreType.DMA((pairs, slots)),
            pltpu.SemaphoreType.DMA((pairs, slots)),
        ],
        compiler_params=pltpu.CompilerParams(vmem_limit_bytes=VMEM_BYTES),
        cost_estimate=pl.CostEstimate(flops=flops, bytes_accessed=moved, transcendentals=0),
    )(counts, begin, tau, *sinks, sources)


def body(perambulator, elementals, diagrams, counts):
    devices = lax.axis_size("tm")
    me = lax.axis_index("tm")
    pair_count, slots = diagrams.shape[:2]
    columns, width = perambulator.shape[1:]
    vectors, packed = elementals.shape[2:]
    half = devices // 2
    own_set = elementals[0]
    high = (me >= half).astype(jnp.int32)
    halves = [list(range(half)), list(range(half, devices))]

    steps = [(slot + 1) * devices // (pair_count + 1) for slot in range(pair_count)]
    wanted = [passed_along(diagrams[slot, :, 0], by) for slot, by in enumerate(steps)]
    given_counts = exchanged(counts, half)
    own_sources = selected(own_set, diagrams[:, :, 1].reshape(-1))
    own_sources = own_sources.reshape(pair_count, slots, vectors, packed)
    given_sources = exchanged(own_sources, half)
    chosen = [selected(own_set, index) for index in wanted]
    given_sinks = [passed_along(sets, -by, half) for by, sets in zip(steps, chosen)]
    own_sinks = [
        passed_along(tied(sets, sent), -by) for by, sets, sent in zip(steps, chosen, given_sinks)
    ]

    tau = lax.all_to_all(
        tied(regrouped(perambulator, high, half, pair_count), given_counts, *wanted),
        "tm",
        split_axis=0,
        concat_axis=0,
        axis_index_groups=halves,
        tiled=True,
    ).reshape(half, 2 * pair_count, columns, width)
    if columns % 16 != 0:
        tau = jnp.moveaxis(tau, 1, 0).reshape(2 * pair_count, -1, vectors, width)
        tau = jnp.moveaxis(tau, 0, 1)

    zeros = jnp.zeros((pair_count, slots, 2), jnp.float32)
    given = pairs_sums(tau, 0, given_sinks, given_sources, given_counts, zeros, 1.0)
    got = exchanged(given, half)
    scale = 1.0 / (columns * devices)
    return pairs_sums(tau, pair_count, own_sinks, own_sources, counts, got, scale)


def solution(mesh):
    return jax.shard_map(
        body,
        mesh=mesh,
        in_specs=(
            P("groups", "tm", None),
            P(("groups", "tm"), None, None, None),
            P("tm", None, None),
            P("tm"),
        ),
        out_specs=P(("groups", "tm"), None, None),
        check_vma=False,
    )
```

```python
import functools

import jax
import jax.numpy as jnp
from jax import lax
from jax.experimental import pallas as pl
from jax.experimental.pallas import tpu as pltpu
from jax.sharding import PartitionSpec as P

NT_DIMS = (((1,), (1,)), ((), ()))
ANYWHERE = pl.BlockSpec(memory_space=pl.ANY)
VMEM_BYTES = 56 * 1024 * 1024
HBM = pl.BlockSpec(memory_space=pltpu.HBM)
VMEM = pl.BlockSpec(memory_space=pltpu.VMEM)
SMEM = pl.BlockSpec(memory_space=pltpu.SMEM)


def exchanged(x, mask):
    devices = lax.axis_size("tm")
    return lax.ppermute(x, "tm", [(i, i ^ mask) for i in range(devices)])


def passed_along(x, by, mask=0):
    devices = lax.axis_size("tm")
    return lax.ppermute(x, "tm", [(i, ((i + by) % devices) ^ mask) for i in range(devices)])


def regroup_kernel(high_ref, source_ref, out_ref, sems):
    high = high_ref[0]
    copies = []
    for j in range(source_ref.shape[1]):
        for side in range(2):
            which = 1 - high if side == 0 else high
            copies.append(
                pltpu.make_async_copy(
                    source_ref.at[which, j], out_ref.at[j, side], sems.at[2 * j + side]
                )
            )
    for copy in copies:
        copy.start()
    for copy in copies:
        copy.wait()


def regrouped(perambulator, high, half, pair_count):
    columns, width = perambulator.shape[1:]
    source = perambulator.reshape(2, half, pair_count, columns, width)
    return pl.pallas_call(
        regroup_kernel,
        in_specs=[SMEM, HBM],
        out_specs=VMEM,
        out_shape=jax.ShapeDtypeStruct((half, 2, pair_count, columns, width), perambulator.dtype),
        scratch_shapes=[pltpu.SemaphoreType.DMA((2 * half,))],
        compiler_params=pltpu.CompilerParams(vmem_limit_bytes=58 * 1024 * 1024),
    )(high.reshape(1), source)


def tied(x, *earlier):
    return pl.pallas_call(
        lambda *refs: None,
        in_specs=[ANYWHERE] * (1 + len(earlier)),
        out_specs=ANYWHERE,
        out_shape=jax.ShapeDtypeStruct(x.shape, x.dtype),
        input_output_aliases={0: 0},
    )(x, *earlier)


def halves_swapped(x):
    vectors = x.shape[1] // 2
    return jnp.concatenate([x[:, vectors:], x[:, :vectors]], axis=1)


def pairs_kernel(pairs, first, scale, counts_ref, one_ref, other_ref, tau_ref, *refs):
    sink_refs = refs[:pairs]
    source_ref = refs[pairs]
    out_ref, sinks, sources, swap_ref, left_ref, sink_sems, source_sems = refs[-7:]
    slots, vectors, packed = sinks.shape[1:]
    spins, _, width = swap_ref.shape
    blocks = width // packed
    pieces = tau_ref.shape[0] // spins
    pair = pl.program_id(0)
    first_half = lax.broadcasted_iota(jnp.int32, (vectors, packed), 1) < vectors

    @pl.when(pair == 0)
    def _():
        for p in range(out_ref.shape[0]):
            for d in range(slots):
                for part in range(2):
                    out_ref[p, d, part] = (one_ref[p, d, part] + other_ref[p, d, part]) * scale
        for p in range(pairs):
            for d in range(slots):

                @pl.when(d < counts_ref[first + p])
                def _():
                    pltpu.make_async_copy(
                        sink_refs[p].at[d], sinks.at[p, d], sink_sems.at[p, d]
                    ).start()
                    pltpu.make_async_copy(
                        source_ref.at[first + p, d], sources.at[p, d], source_sems.at[p, d]
                    ).start()

    def tile(s):
        return tau_ref[s * pieces : (s + 1) * pieces, 0].reshape(vectors, width)

    def part(x, b):
        return x[:, b * packed : (b + 1) * packed]

    for s in range(spins):
        for b in range(blocks):
            swapped = halves_swapped(part(tile(s), b))
            swap_ref[s, :, b * packed : (b + 1) * packed] = jnp.where(
                first_half, -swapped, swapped
            )

    @pl.loop(0, counts_ref[first + pair])
    def _(d):
        pltpu.make_async_copy(
            sink_refs[0].at[0], sinks.at[pair, d], sink_sems.at[pair, d]
        ).wait()
        sink = sinks[pair, d]
        embedding = jnp.concatenate(
            [jnp.where(first_half, sink, -sink), halves_swapped(sink)], axis=0
        )
        block_real = jnp.zeros((vectors, vectors), jnp.float32)
        block_imag = jnp.zeros((vectors, vectors), jnp.float32)
        for s in range(spins):
            stacked = jnp.concatenate([part(tile(s), b) for b in range(blocks)], axis=0)
            left = lax.dot_general(
                stacked, embedding, NT_DIMS, preferred_element_type=jnp.float32
            ).astype(jnp.bfloat16)
            for b in range(blocks):
                left_ref[s, :, b * packed : (b + 1) * packed] = left[
                    b * vectors : (b + 1) * vectors
                ]
        for s in range(spins):
            block_real += lax.dot_general(
                left_ref[s], tile(s), NT_DIMS, preferred_element_type=jnp.float32
            )
            block_imag += lax.dot_general(
                left_ref[s], swap_ref[s], NT_DIMS, preferred_element_type=jnp.float32
            )
        pltpu.make_async_copy(
            source_ref.at[0, 0], sources.at[pair, d], source_sems.at[pair, d]
        ).wait()
        source = sources[pair, d].astype(jnp.float32)
        real = source[:, :vectors]
        imag = source[:, vectors:]
        out_ref[first + pair, d, 0] += jnp.sum(real * block_real - imag * block_imag) * scale
        out_ref[first + pair, d, 1] += jnp.sum(real * block_imag + imag * block_real) * scale


def pairs_sums(tau, side, first, sinks, sources, counts, one, other, scale):
    pairs = len(sinks)
    slots, vectors, packed = sinks[0].shape
    pieces, _, columns, width = tau.shape
    spins = pieces * columns // vectors
    lead = side * counts.shape[0] + first
    flops = 4 * pairs * spins * slots * width * vectors * packed
    moved = 2 * pairs * (spins * vectors * width + 2 * slots * vectors * packed)
    return pl.pallas_call(
        functools.partial(pairs_kernel, pairs, first, scale),
        grid=(pairs,),
        in_specs=[
            SMEM,
            SMEM,
            SMEM,
            pl.BlockSpec((pieces, 1, columns, width), lambda p: (0, lead + p, 0, 0)),
        ]
        + [HBM] * (pairs + 1),
        out_specs=SMEM,
        out_shape=jax.ShapeDtypeStruct(one.shape, jnp.float32),
        scratch_shapes=[
            pltpu.VMEM((pairs, slots, vectors, packed), jnp.bfloat16),
            pltpu.VMEM((pairs, slots, vectors, packed), jnp.bfloat16),
            pltpu.VMEM((spins, vectors, width), jnp.bfloat16),
            pltpu.VMEM((spins, vectors, width), jnp.bfloat16),
            pltpu.SemaphoreType.DMA((pairs, slots)),
            pltpu.SemaphoreType.DMA((pairs, slots)),
        ],
        compiler_params=pltpu.CompilerParams(vmem_limit_bytes=VMEM_BYTES),
        cost_estimate=pl.CostEstimate(flops=flops, bytes_accessed=moved, transcendentals=0),
    )(counts, one, other, tau, *sinks, sources)


def body(perambulator, elementals, diagrams, counts):
    devices = lax.axis_size("tm")
    me = lax.axis_index("tm")
    pair_count, slots = diagrams.shape[:2]
    columns, width = perambulator.shape[1:]
    vectors, packed = elementals.shape[2:]
    half = devices // 2
    own_set = elementals[0]
    high = (me >= half).astype(jnp.int32)
    halves = [list(range(half)), list(range(half, devices))]

    steps = [(slot + 1) * devices // (pair_count + 1) for slot in range(pair_count)]
    wanted = [passed_along(diagrams[slot, :, 0], by) for slot, by in enumerate(steps)]
    given_counts = exchanged(counts, half)
    own_sources = jnp.take(own_set, diagrams[:, :, 1].reshape(-1), axis=0, mode="clip")
    own_sources = own_sources.reshape(pair_count, slots, vectors, packed)
    given_sources = exchanged(own_sources, half)
    chosen = [jnp.take(own_set, index, axis=0, mode="clip") for index in wanted]
    given_sinks = [passed_along(sets, -by, half) for by, sets in zip(steps, chosen)]
    last = pair_count - 1
    own_sinks = [
        passed_along(sets if slot < last else tied(sets, given_sinks[0]), -by)
        for slot, (by, sets) in enumerate(zip(steps, chosen))
    ]

    tau = lax.all_to_all(
        tied(regrouped(perambulator, high, half, pair_count), given_counts, *wanted),
        "tm",
        split_axis=0,
        concat_axis=0,
        axis_index_groups=halves,
        tiled=True,
    ).reshape(half, 2 * pair_count, columns, width)
    if columns % 16 != 0:
        tau = jnp.moveaxis(tau, 1, 0).reshape(2 * pair_count, -1, vectors, width)
        tau = jnp.moveaxis(tau, 0, 1)

    zeros = jnp.zeros((pair_count, slots, 2), jnp.float32)
    given = pairs_sums(tau, 0, 0, given_sinks, given_sources, given_counts, zeros, zeros, 1.0)
    got = exchanged(given, half)
    kept = pairs_sums(tau, 1, 0, own_sinks[:last], own_sources, counts, zeros, zeros, 1.0)
    scale = 1.0 / (columns * devices)
    return pairs_sums(tau, 1, last, own_sinks[last:], own_sources, counts, kept, got, scale)


def solution(mesh):
    return jax.shard_map(
        body,
        mesh=mesh,
        in_specs=(
            P("groups", "tm", None),
            P(("groups", "tm"), None, None, None),
            P("tm", None, None),
            P("tm"),
        ),
        out_specs=P(("groups", "tm"), None, None),
        check_vma=False,
    )
```

```python
import functools

import jax
import jax.numpy as jnp
from jax import lax
from jax.experimental import pallas as pl
from jax.experimental.pallas import tpu as pltpu
from jax.sharding import PartitionSpec as P

NT_DIMS = (((1,), (1,)), ((), ()))
ANYWHERE = pl.BlockSpec(memory_space=pl.ANY)
VMEM_BYTES = 24 * 1024 * 1024
HBM = pl.BlockSpec(memory_space=pltpu.HBM)
VMEM = pl.BlockSpec(memory_space=pltpu.VMEM)
SMEM = pl.BlockSpec(memory_space=pltpu.SMEM)


def exchanged(x, mask):
    devices = lax.axis_size("tm")
    return lax.ppermute(x, "tm", [(i, i ^ mask) for i in range(devices)])


def passed_along(x, by, mask=0):
    devices = lax.axis_size("tm")
    return lax.ppermute(x, "tm", [(i, ((i + by) % devices) ^ mask) for i in range(devices)])


def regroup_kernel(high_ref, source_ref, out_ref, block_ref, in_sems, out_sems):
    high = high_ref[0]
    copies = []
    for j in range(source_ref.shape[1]):
        for side in range(2):
            which = 1 - high if side == 0 else high
            block = block_ref.at[j, side]
            n = 2 * j + side
            copies.append(
                (
                    pltpu.make_async_copy(source_ref.at[which, j], block, in_sems.at[n]),
                    pltpu.make_async_copy(block, out_ref.at[j, side], out_sems.at[n]),
                )
            )
    for copy_in, _ in copies:
        copy_in.start()
    for copy_in, copy_out in copies:
        copy_in.wait()
        copy_out.start()
    for _, copy_out in copies:
        copy_out.wait()


def regrouped(perambulator, high, half, pair_count):
    columns, width = perambulator.shape[1:]
    source = perambulator.reshape(2, half, pair_count, columns, width)
    shape = (half, 2, pair_count, columns, width)
    return pl.pallas_call(
        regroup_kernel,
        in_specs=[SMEM, HBM],
        out_specs=HBM,
        out_shape=jax.ShapeDtypeStruct(shape, perambulator.dtype),
        scratch_shapes=[
            pltpu.VMEM(shape, perambulator.dtype),
            pltpu.SemaphoreType.DMA((2 * half,)),
            pltpu.SemaphoreType.DMA((2 * half,)),
        ],
        compiler_params=pltpu.CompilerParams(vmem_limit_bytes=58 * 1024 * 1024),
    )(high.reshape(1), source)


def tied(x, *earlier):
    return pl.pallas_call(
        lambda *refs: None,
        in_specs=[ANYWHERE] * (1 + len(earlier)),
        out_specs=ANYWHERE,
        out_shape=jax.ShapeDtypeStruct(x.shape, x.dtype),
        input_output_aliases={0: 0},
    )(x, *earlier)


def halves_swapped(x):
    vectors = x.shape[1] // 2
    return jnp.concatenate([x[:, vectors:], x[:, :vectors]], axis=1)


def pairs_kernel(pairs, first, scale, counts_ref, one_ref, other_ref, tau_ref, *refs):
    sink_refs = refs[:pairs]
    source_ref = refs[pairs]
    out_ref, sources, swap_ref, left_ref, source_sems = refs[-5:]
    slots, vectors, packed = sources.shape[1:]
    spins, _, width = swap_ref.shape
    blocks = width // packed
    pieces = tau_ref.shape[0] // spins
    pair = pl.program_id(0)
    first_half = lax.broadcasted_iota(jnp.int32, (vectors, packed), 1) < vectors

    @pl.when(pair == 0)
    def _():
        for p in range(out_ref.shape[0]):
            for d in range(slots):
                for side in range(2):
                    out_ref[p, side, d] = (one_ref[p, side, d] + other_ref[p, side, d]) * scale
        for p in range(pairs):
            for d in range(slots):

                @pl.when(d < counts_ref[first + p])
                def _():
                    pltpu.make_async_copy(
                        source_ref.at[first + p, d], sources.at[p, d], source_sems.at[p, d]
                    ).start()

    def tile(s):
        return tau_ref[s * pieces : (s + 1) * pieces, 0].reshape(vectors, width)

    def part(x, b):
        return x[:, b * packed : (b + 1) * packed]

    for s in range(spins):
        for b in range(blocks):
            swapped = halves_swapped(part(tile(s), b))
            swap_ref[s, :, b * packed : (b + 1) * packed] = jnp.where(
                first_half, -swapped, swapped
            )

    def add_diagram(sink_ref, d):
        sink = sink_ref[d]
        embedding = jnp.concatenate(
            [jnp.where(first_half, sink, -sink), halves_swapped(sink)], axis=0
        )
        block_real = jnp.zeros((vectors, vectors), jnp.float32)
        block_imag = jnp.zeros((vectors, vectors), jnp.float32)
        for s in range(spins):
            stacked = jnp.concatenate([part(tile(s), b) for b in range(blocks)], axis=0)
            left = lax.dot_general(
                stacked, embedding, NT_DIMS, preferred_element_type=jnp.float32
            ).astype(jnp.bfloat16)
            for b in range(blocks):
                left_ref[s, :, b * packed : (b + 1) * packed] = left[
                    b * vectors : (b + 1) * vectors
                ]
        for s in range(spins):
            block_real += lax.dot_general(
                left_ref[s], tile(s), NT_DIMS, preferred_element_type=jnp.float32
            )
            block_imag += lax.dot_general(
                left_ref[s], swap_ref[s], NT_DIMS, preferred_element_type=jnp.float32
            )
        pltpu.make_async_copy(
            source_ref.at[0, 0], sources.at[pair, d], source_sems.at[pair, d]
        ).wait()
        source = sources[pair, d].astype(jnp.float32)
        real = source[:, :vectors]
        imag = source[:, vectors:]
        out_ref[first + pair, 0, d] += jnp.sum(real * block_real - imag * block_imag) * scale
        out_ref[first + pair, 1, d] += jnp.sum(real * block_imag + imag * block_real) * scale

    for p in range(pairs):

        @pl.when(pair == p)
        def _():
            pl.loop(0, counts_ref[first + p])(functools.partial(add_diagram, sink_refs[p]))


def pairs_sums(tau, side, first, sinks, sources, counts, one, other, scale):
    pairs = len(sinks)
    slots, vectors, packed = sinks[0].shape
    pieces, _, columns, width = tau.shape
    spins = pieces * columns // vectors
    lead = side * counts.shape[0] + first
    flops = 4 * pairs * spins * slots * width * vectors * packed
    moved = 2 * pairs * (spins * vectors * width + 2 * slots * vectors * packed)
    return pl.pallas_call(
        functools.partial(pairs_kernel, pairs, first, scale),
        grid=(pairs,),
        in_specs=[
            SMEM,
            SMEM,
            SMEM,
            pl.BlockSpec((pieces, 1, columns, width), lambda p: (0, lead + p, 0, 0)),
        ]
        + [VMEM] * pairs
        + [ANYWHERE],
        out_specs=SMEM,
        out_shape=jax.ShapeDtypeStruct(one.shape, jnp.float32),
        scratch_shapes=[
            pltpu.VMEM((pairs, slots, vectors, packed), jnp.bfloat16),
            pltpu.VMEM((spins, vectors, width), jnp.bfloat16),
            pltpu.VMEM((spins, vectors, width), jnp.bfloat16),
            pltpu.SemaphoreType.DMA((pairs, slots)),
        ],
        compiler_params=pltpu.CompilerParams(vmem_limit_bytes=VMEM_BYTES),
        cost_estimate=pl.CostEstimate(flops=flops, bytes_accessed=moved, transcendentals=0),
    )(counts, one, other, tau, *sinks, sources)


def body(perambulator, elementals, diagrams, counts):
    devices = lax.axis_size("tm")
    me = lax.axis_index("tm")
    pair_count, slots = diagrams.shape[:2]
    columns, width = perambulator.shape[1:]
    vectors, packed = elementals.shape[2:]
    half = devices // 2
    own_set = elementals[0]
    high = (me >= half).astype(jnp.int32)
    halves = [list(range(half)), list(range(half, devices))]

    steps = [(slot + 1) * devices // (pair_count + 1) for slot in range(pair_count)]
    wanted = [passed_along(diagrams[slot, :, 0], by) for slot, by in enumerate(steps)]
    given_counts = exchanged(counts, half)
    own_sources = jnp.take(own_set, diagrams[:, :, 1].reshape(-1), axis=0, mode="clip")
    own_sources = own_sources.reshape(pair_count, slots, vectors, packed)
    given_sources = exchanged(own_sources, half)
    chosen = [jnp.take(own_set, index, axis=0, mode="clip") for index in wanted]
    given_sinks = [passed_along(sets, -by, half) for by, sets in zip(steps, chosen)]
    last = pair_count - 1
    own_sinks = [
        passed_along(sets if slot < last else tied(sets, given_sinks[0]), -by)
        for slot, (by, sets) in enumerate(zip(steps, chosen))
    ]

    tau = lax.all_to_all(
        tied(
            regrouped(perambulator, high, half, pair_count), given_counts, own_sources, *wanted
        ),
        "tm",
        split_axis=0,
        concat_axis=0,
        axis_index_groups=halves,
        tiled=True,
    ).reshape(half, 2 * pair_count, columns, width)
    if columns % 16 != 0:
        tau = jnp.moveaxis(tau, 1, 0).reshape(2 * pair_count, -1, vectors, width)
        tau = jnp.moveaxis(tau, 0, 1)

    zeros = jnp.zeros((pair_count, 2, slots), jnp.float32)
    given = pairs_sums(tau, 0, 0, given_sinks, given_sources, given_counts, zeros, zeros, 1.0)
    kept = pairs_sums(tau, 1, 0, own_sinks[:last], own_sources, counts, zeros, zeros, 1.0)
    got = exchanged(tied(given, kept), half)
    scale = 1.0 / (columns * devices)
    sums = pairs_sums(tau, 1, last, own_sinks[last:], own_sources, counts, kept, got, scale)
    return jnp.swapaxes(sums, 1, 2)


def solution(mesh):
    return jax.shard_map(
        body,
        mesh=mesh,
        in_specs=(
            P("groups", "tm", None),
            P(("groups", "tm"), None, None, None),
            P("tm", None, None),
            P("tm"),
        ),
        out_specs=P(("groups", "tm"), None, None),
        check_vma=False,
    )
```

```python
import functools

import jax
import jax.numpy as jnp
from jax import lax
from jax.experimental import pallas as pl
from jax.experimental.pallas import tpu as pltpu
from jax.sharding import PartitionSpec as P

NT_DIMS = (((1,), (1,)), ((), ()))
ANYWHERE = pl.BlockSpec(memory_space=pl.ANY)
VMEM_BYTES = 24 * 1024 * 1024
HBM = pl.BlockSpec(memory_space=pltpu.HBM)
VMEM = pl.BlockSpec(memory_space=pltpu.VMEM)
SMEM = pl.BlockSpec(memory_space=pltpu.SMEM)


def exchanged(x, mask):
    devices = lax.axis_size("tm")
    return lax.ppermute(x, "tm", [(i, i ^ mask) for i in range(devices)])


def passed_along(x, by, mask=0):
    devices = lax.axis_size("tm")
    return lax.ppermute(x, "tm", [(i, ((i + by) % devices) ^ mask) for i in range(devices)])


def regroup_kernel(high_ref, source_ref, out_ref, block_ref, in_sems, out_sems):
    high = high_ref[0]
    copies = []
    for j in range(source_ref.shape[1]):
        for side in range(2):
            which = 1 - high if side == 0 else high
            block = block_ref.at[j, side]
            n = 2 * j + side
            copies.append(
                (
                    pltpu.make_async_copy(source_ref.at[which, j], block, in_sems.at[n]),
                    pltpu.make_async_copy(block, out_ref.at[j, side], out_sems.at[n]),
                )
            )
    for copy_in, _ in copies:
        copy_in.start()
    for copy_in, copy_out in copies:
        copy_in.wait()
        copy_out.start()
    for _, copy_out in copies:
        copy_out.wait()


def regrouped(perambulator, high, half, pair_count):
    columns, width = perambulator.shape[1:]
    source = perambulator.reshape(2, half, pair_count, columns, width)
    shape = (half, 2, pair_count, columns, width)
    return pl.pallas_call(
        regroup_kernel,
        in_specs=[SMEM, HBM],
        out_specs=HBM,
        out_shape=jax.ShapeDtypeStruct(shape, perambulator.dtype),
        scratch_shapes=[
            pltpu.VMEM(shape, perambulator.dtype),
            pltpu.SemaphoreType.DMA((2 * half,)),
            pltpu.SemaphoreType.DMA((2 * half,)),
        ],
        compiler_params=pltpu.CompilerParams(vmem_limit_bytes=58 * 1024 * 1024),
    )(high.reshape(1), source)


def tied(x, *earlier):
    return pl.pallas_call(
        lambda *refs: None,
        in_specs=[ANYWHERE] * (1 + len(earlier)),
        out_specs=ANYWHERE,
        out_shape=jax.ShapeDtypeStruct(x.shape, x.dtype),
        input_output_aliases={0: 0},
    )(x, *earlier)


def halves_swapped(x):
    vectors = x.shape[1] // 2
    return jnp.concatenate([x[:, vectors:], x[:, :vectors]], axis=1)


def pairs_kernel(pairs, first, counts_ref, begin_ref, tau_ref, *refs):
    sink_refs = refs[:pairs]
    source_ref = refs[pairs]
    out_ref, sources, swap_ref, left_ref, source_sems = refs[-5:]
    slots, vectors, packed = sources.shape[1:]
    spins, _, width = swap_ref.shape
    blocks = width // packed
    pieces = tau_ref.shape[0] // spins
    pair = pl.program_id(0)
    first_half = lax.broadcasted_iota(jnp.int32, (vectors, packed), 1) < vectors

    @pl.when(pair == 0)
    def _():
        for p in range(out_ref.shape[0]):
            for d in range(slots):
                for side in range(2):
                    out_ref[p, side, d] = begin_ref[p, side, d]
        for p in range(pairs):
            for d in range(slots):

                @pl.when(d < counts_ref[first + p])
                def _():
                    pltpu.make_async_copy(
                        source_ref.at[first + p, d], sources.at[p, d], source_sems.at[p, d]
                    ).start()

    def tile(s):
        return tau_ref[s * pieces : (s + 1) * pieces, 0].reshape(vectors, width)

    def part(x, b):
        return x[:, b * packed : (b + 1) * packed]

    for s in range(spins):
        for b in range(blocks):
            swapped = halves_swapped(part(tile(s), b))
            swap_ref[s, :, b * packed : (b + 1) * packed] = jnp.where(
                first_half, -swapped, swapped
            )

    def add_diagram(sink_ref, d):
        sink = sink_ref[d]
        embedding = jnp.concatenate(
            [jnp.where(first_half, sink, -sink), halves_swapped(sink)], axis=0
        )
        block_real = jnp.zeros((vectors, vectors), jnp.float32)
        block_imag = jnp.zeros((vectors, vectors), jnp.float32)
        for s in range(spins):
            stacked = jnp.concatenate([part(tile(s), b) for b in range(blocks)], axis=0)
            left = lax.dot_general(
                stacked, embedding, NT_DIMS, preferred_element_type=jnp.float32
            ).astype(jnp.bfloat16)
            for b in range(blocks):
                left_ref[s, :, b * packed : (b + 1) * packed] = left[
                    b * vectors : (b + 1) * vectors
                ]
        for s in range(spins):
            block_real += lax.dot_general(
                left_ref[s], tile(s), NT_DIMS, preferred_element_type=jnp.float32
            )
            block_imag += lax.dot_general(
                left_ref[s], swap_ref[s], NT_DIMS, preferred_element_type=jnp.float32
            )
        pltpu.make_async_copy(
            source_ref.at[0, 0], sources.at[pair, d], source_sems.at[pair, d]
        ).wait()
        source = sources[pair, d].astype(jnp.float32)
        real = source[:, :vectors]
        imag = source[:, vectors:]
        out_ref[first + pair, 0, d] += jnp.sum(real * block_real - imag * block_imag)
        out_ref[first + pair, 1, d] += jnp.sum(real * block_imag + imag * block_real)

    for p in range(pairs):

        @pl.when(pair == p)
        def _():
            pl.loop(0, counts_ref[first + p])(functools.partial(add_diagram, sink_refs[p]))


def pairs_sums(tau, side, first, sinks, sources, counts, begin, *earlier):
    pairs = len(sinks)
    slots, vectors, packed = sinks[0].shape
    pieces, _, columns, width = tau.shape
    spins = pieces * columns // vectors
    lead = side * counts.shape[0] + first
    flops = 4 * pairs * spins * slots * width * vectors * packed
    moved = 2 * pairs * (spins * vectors * width + 2 * slots * vectors * packed)
    return pl.pallas_call(
        functools.partial(pairs_kernel, pairs, first),
        grid=(pairs,),
        in_specs=[
            SMEM,
            SMEM,
            pl.BlockSpec((pieces, 1, columns, width), lambda p: (0, lead + p, 0, 0)),
        ]
        + [VMEM] * pairs
        + [ANYWHERE] * (1 + len(earlier)),
        out_specs=SMEM,
        out_shape=jax.ShapeDtypeStruct(begin.shape, jnp.float32),
        scratch_shapes=[
            pltpu.VMEM((pairs, slots, vectors, packed), jnp.bfloat16),
            pltpu.VMEM((spins, vectors, width), jnp.bfloat16),
            pltpu.VMEM((spins, vectors, width), jnp.bfloat16),
            pltpu.SemaphoreType.DMA((pairs, slots)),
        ],
        compiler_params=pltpu.CompilerParams(vmem_limit_bytes=VMEM_BYTES),
        cost_estimate=pl.CostEstimate(flops=flops, bytes_accessed=moved, transcendentals=0),
    )(counts, begin, tau, *sinks, sources, *earlier)


def body(perambulator, elementals, diagrams, counts):
    devices = lax.axis_size("tm")
    me = lax.axis_index("tm")
    pair_count, slots = diagrams.shape[:2]
    columns, width = perambulator.shape[1:]
    vectors, packed = elementals.shape[2:]
    half = devices // 2
    own_set = elementals[0]
    high = (me >= half).astype(jnp.int32)
    halves = [list(range(half)), list(range(half, devices))]

    steps = [(slot + 1) * devices // (pair_count + 1) for slot in range(pair_count)]
    wanted = [passed_along(diagrams[slot, :, 0], by) for slot, by in enumerate(steps)]
    given_counts = exchanged(counts, half)
    own_sources = jnp.take(own_set, diagrams[:, :, 1].reshape(-1), axis=0, mode="clip")
    own_sources = own_sources.reshape(pair_count, slots, vectors, packed)
    given_sources = exchanged(own_sources, half)
    chosen = [jnp.take(own_set, index, axis=0, mode="clip") for index in wanted]
    given_sinks = [passed_along(sets, -by, half) for by, sets in zip(steps, chosen)]
    last = pair_count - 1
    own_sinks = [
        passed_along(sets if slot < last else tied(sets, given_sinks[0]), -by)
        for slot, (by, sets) in enumerate(zip(steps, chosen))
    ]

    tau = lax.all_to_all(
        tied(regrouped(perambulator, high, half, pair_count), given_counts, *wanted),
        "tm",
        split_axis=0,
        concat_axis=0,
        axis_index_groups=halves,
        tiled=True,
    ).reshape(half, 2 * pair_count, columns, width)
    if columns % 16 != 0:
        tau = jnp.moveaxis(tau, 1, 0).reshape(2 * pair_count, -1, vectors, width)
        tau = jnp.moveaxis(tau, 0, 1)

    zeros = jnp.zeros((pair_count, 2, slots), jnp.float32)
    given = pairs_sums(tau, 0, 0, given_sinks, given_sources, given_counts, zeros)
    kept = pairs_sums(tau, 1, 0, own_sinks[:last], own_sources, counts, zeros, given)
    got = exchanged(tied(given, kept), half)
    kept = pairs_sums(tau, 1, last, own_sinks[last:], own_sources, counts, kept)
    return jnp.swapaxes((kept + got) / (columns * devices), 1, 2)


def solution(mesh):
    return jax.shard_map(
        body,
        mesh=mesh,
        in_specs=(
            P("groups", "tm", None),
            P(("groups", "tm"), None, None, None),
            P("tm", None, None),
            P("tm"),
        ),
        out_specs=P(("groups", "tm"), None, None),
        check_vma=False,
    )
```

```python
import functools

import jax
import jax.numpy as jnp
from jax import lax
from jax.experimental import pallas as pl
from jax.experimental.pallas import tpu as pltpu
from jax.sharding import PartitionSpec as P

NT_DIMS = (((1,), (1,)), ((), ()))
ANYWHERE = pl.BlockSpec(memory_space=pl.ANY)
VMEM_BYTES = 56 * 1024 * 1024
HBM = pl.BlockSpec(memory_space=pltpu.HBM)
VMEM = pl.BlockSpec(memory_space=pltpu.VMEM)
SMEM = pl.BlockSpec(memory_space=pltpu.SMEM)


def exchanged(x, mask):
    devices = lax.axis_size("tm")
    return lax.ppermute(x, "tm", [(i, i ^ mask) for i in range(devices)])


def passed_along(x, by, mask=0):
    devices = lax.axis_size("tm")
    return lax.ppermute(x, "tm", [(i, ((i + by) % devices) ^ mask) for i in range(devices)])


def regroup_kernel(high_ref, source_ref, out_ref, block_ref, in_sems, out_sems):
    high = high_ref[0]
    copies = []
    for j in range(source_ref.shape[1]):
        for side in range(2):
            which = 1 - high if side == 0 else high
            block = block_ref.at[j, side]
            n = 2 * j + side
            copies.append(
                (
                    pltpu.make_async_copy(source_ref.at[which, j], block, in_sems.at[n]),
                    pltpu.make_async_copy(block, out_ref.at[j, side], out_sems.at[n]),
                )
            )
    for copy_in, _ in copies:
        copy_in.start()
    for copy_in, copy_out in copies:
        copy_in.wait()
        copy_out.start()
    for _, copy_out in copies:
        copy_out.wait()


def regrouped(perambulator, high, half, pair_count):
    columns, width = perambulator.shape[1:]
    source = perambulator.reshape(2, half, pair_count, columns, width)
    shape = (half, 2, pair_count, columns, width)
    return pl.pallas_call(
        regroup_kernel,
        in_specs=[SMEM, HBM],
        out_specs=HBM,
        out_shape=jax.ShapeDtypeStruct(shape, perambulator.dtype),
        scratch_shapes=[
            pltpu.VMEM(shape, perambulator.dtype),
            pltpu.SemaphoreType.DMA((2 * half,)),
            pltpu.SemaphoreType.DMA((2 * half,)),
        ],
        compiler_params=pltpu.CompilerParams(vmem_limit_bytes=58 * 1024 * 1024),
    )(high.reshape(1), source)


def tied(x, *earlier):
    return pl.pallas_call(
        lambda *refs: None,
        in_specs=[ANYWHERE] * (1 + len(earlier)),
        out_specs=ANYWHERE,
        out_shape=jax.ShapeDtypeStruct(x.shape, x.dtype),
        input_output_aliases={0: 0},
    )(x, *earlier)


def halves_swapped(x):
    vectors = x.shape[1] // 2
    return jnp.concatenate([x[:, vectors:], x[:, :vectors]], axis=1)


def pairs_kernel(pairs, lead, first, counts_ref, begin_ref, tau_ref, *refs):
    sink_refs = refs[:pairs]
    source_ref, out_ref, sinks, sources, both_ref, left_ref, sink_sems, source_sems = refs[pairs:]
    slots, vectors, packed = sinks.shape[1:]
    spins, _, width = left_ref.shape
    blocks = width // packed
    pieces = tau_ref.shape[0] // spins
    pair = pl.program_id(0)
    first_half = lax.broadcasted_iota(jnp.int32, (vectors, packed), 1) < vectors

    @pl.when(pair == 0)
    def _():
        for p in range(pairs):
            for d in range(slots):

                @pl.when(d < counts_ref[first + p])
                def _():
                    pltpu.make_async_copy(
                        sink_refs[p].at[d], sinks.at[p, d], sink_sems.at[p, d]
                    ).start()
                    pltpu.make_async_copy(
                        source_ref.at[first + p, d], sources.at[p, d], source_sems.at[p, d]
                    ).start()

        for p in range(out_ref.shape[0]):
            for d in range(slots):
                for side in range(2):
                    out_ref[p, side, d] = begin_ref[p, side, d]

    for s in range(spins):
        for b in range(blocks):
            lanes = slice(b * packed, (b + 1) * packed)
            tile = tau_ref[s * pieces : (s + 1) * pieces, 0, :, lanes].reshape(vectors, packed)
            swapped = halves_swapped(tile)
            both_ref[s, :vectors, lanes] = tile
            both_ref[s, vectors:, lanes] = jnp.where(first_half, -swapped, swapped)

    @pl.loop(0, counts_ref[first + pair])
    def _(d):
        pltpu.make_async_copy(
            sink_refs[0].at[0], sinks.at[pair, d], sink_sems.at[pair, d]
        ).wait()
        sink = sinks[pair, d]
        embedding = jnp.concatenate(
            [jnp.where(first_half, sink, -sink), halves_swapped(sink)], axis=0
        )
        for s in range(spins):
            stacked = jnp.concatenate(
                [both_ref[s, :vectors, b * packed : (b + 1) * packed] for b in range(blocks)],
                axis=0,
            )
            left = lax.dot_general(
                stacked, embedding, NT_DIMS, preferred_element_type=jnp.float32
            ).astype(jnp.bfloat16)
            for b in range(blocks):
                left_ref[s, :, b * packed : (b + 1) * packed] = left[
                    b * vectors : (b + 1) * vectors
                ]
        block = jnp.zeros((2 * vectors, vectors), jnp.float32)
        for s in range(spins):
            block += lax.dot_general(
                both_ref[s], left_ref[s], NT_DIMS, preferred_element_type=jnp.float32
            )
        pltpu.make_async_copy(
            source_ref.at[0, 0], sources.at[pair, d], source_sems.at[pair, d]
        ).wait()
        source = sources[pair, d].astype(jnp.float32).T
        real = source[:vectors]
        imag = source[vectors:]
        block_real = block[:vectors]
        block_imag = block[vectors:]
        row = lead + first + pair
        out_ref[row, 0, d] += jnp.sum(real * block_real - imag * block_imag)
        out_ref[row, 1, d] += jnp.sum(real * block_imag + imag * block_real)


def pairs_sums(tau, side, first, sinks, sources, counts, begin):
    pairs = len(sinks)
    slots, vectors, packed = sinks[0].shape
    pieces, _, columns, width = tau.shape
    spins = pieces * columns // vectors
    lead = side * counts.shape[0]
    flops = 4 * pairs * spins * slots * width * vectors * packed
    moved = 2 * pairs * (spins * vectors * width + 2 * slots * vectors * packed)
    elemental_copies = [pltpu.VMEM((pairs, slots, vectors, packed), jnp.bfloat16)] * 2
    return pl.pallas_call(
        functools.partial(pairs_kernel, pairs, lead, first),
        grid=(pairs,),
        in_specs=[
            SMEM,
            SMEM,
            pl.BlockSpec((pieces, 1, columns, width), lambda p: (0, lead + first + p, 0, 0)),
        ]
        + [HBM] * (pairs + 1),
        out_specs=SMEM,
        out_shape=jax.ShapeDtypeStruct(begin.shape, jnp.float32),
        scratch_shapes=elemental_copies
        + [
            pltpu.VMEM((spins, 2 * vectors, width), jnp.bfloat16),
            pltpu.VMEM((spins, vectors, width), jnp.bfloat16),
            pltpu.SemaphoreType.DMA((pairs, slots)),
            pltpu.SemaphoreType.DMA((pairs, slots)),
        ],
        compiler_params=pltpu.CompilerParams(vmem_limit_bytes=VMEM_BYTES),
        cost_estimate=pl.CostEstimate(flops=flops, bytes_accessed=moved, transcendentals=0),
    )(counts, begin, tau, *sinks, sources)


def body(perambulator, elementals, diagrams, counts):
    devices = lax.axis_size("tm")
    me = lax.axis_index("tm")
    pair_count, slots = diagrams.shape[:2]
    columns, width = perambulator.shape[1:]
    vectors, packed = elementals.shape[2:]
    half = devices // 2
    own_set = elementals[0]
    high = (me >= half).astype(jnp.int32)
    halves = [list(range(half)), list(range(half, devices))]

    steps = [(slot + 1) * devices // (pair_count + 1) for slot in range(pair_count)]
    wanted = [passed_along(diagrams[slot, :, 0], by) for slot, by in enumerate(steps)]
    given_counts = exchanged(counts, half)
    own_sources = jnp.take(own_set, diagrams[:, :, 1].reshape(-1), axis=0, mode="clip")
    own_sources = own_sources.reshape(pair_count, slots, vectors, packed)
    given_sources = exchanged(own_sources, half)
    chosen = [jnp.take(own_set, index, axis=0, mode="clip") for index in wanted]
    given_sinks = [passed_along(sets, -by, half) for by, sets in zip(steps, chosen)]
    last = pair_count - 1
    own_sinks = [
        passed_along(sets if slot < last else tied(sets, given_sinks[0]), -by)
        for slot, (by, sets) in enumerate(zip(steps, chosen))
    ]

    tau = lax.all_to_all(
        tied(regrouped(perambulator, high, half, pair_count), given_counts, *wanted),
        "tm",
        split_axis=0,
        concat_axis=0,
        axis_index_groups=halves,
        tiled=True,
    ).reshape(half, 2 * pair_count, columns, width)
    if columns % 16 != 0:
        tau = jnp.moveaxis(tau, 1, 0).reshape(2 * pair_count, -1, vectors, width)
        tau = jnp.moveaxis(tau, 0, 1)

    sums = jnp.zeros((2 * pair_count, 2, slots), jnp.float32)
    sums = pairs_sums(tau, 0, 0, given_sinks, given_sources, given_counts, sums)
    sums = pairs_sums(tau, 1, 0, own_sinks[:last], own_sources, counts, sums)
    got = exchanged(sums, half)
    sums = pairs_sums(tau, 1, last, own_sinks[last:], own_sources, counts, sums)
    total = (sums[pair_count:] + got[:pair_count]) / (columns * devices)
    return jnp.swapaxes(total, 1, 2)


def solution(mesh):
    return jax.shard_map(
        body,
        mesh=mesh,
        in_specs=(
            P("groups", "tm", None),
            P(("groups", "tm"), None, None, None),
            P("tm", None, None),
            P("tm"),
        ),
        out_specs=P(("groups", "tm"), None, None),
        check_vma=False,
    )
```

```python
import functools

import jax
import jax.numpy as jnp
from jax import lax
from jax.experimental import pallas as pl
from jax.experimental.pallas import tpu as pltpu
from jax.sharding import PartitionSpec as P

NT_DIMS = (((1,), (1,)), ((), ()))
ANYWHERE = pl.BlockSpec(memory_space=pl.ANY)
VMEM_BYTES = 56 * 1024 * 1024
HBM = pl.BlockSpec(memory_space=pltpu.HBM)
VMEM = pl.BlockSpec(memory_space=pltpu.VMEM)
SMEM = pl.BlockSpec(memory_space=pltpu.SMEM)


def exchanged(x, mask):
    devices = lax.axis_size("tm")
    return lax.ppermute(x, "tm", [(i, i ^ mask) for i in range(devices)])


def passed_along(x, by, mask=0):
    devices = lax.axis_size("tm")
    return lax.ppermute(x, "tm", [(i, ((i + by) % devices) ^ mask) for i in range(devices)])


def regroup_kernel(high_ref, source_ref, out_ref, block_ref, in_sems, out_sems):
    high = high_ref[0]
    copies = []
    for j in range(source_ref.shape[1]):
        for side in range(2):
            which = 1 - high if side == 0 else high
            block = block_ref.at[j, side]
            n = 2 * j + side
            copies.append(
                (
                    pltpu.make_async_copy(source_ref.at[which, j], block, in_sems.at[n]),
                    pltpu.make_async_copy(block, out_ref.at[j, side], out_sems.at[n]),
                )
            )
    for copy_in, _ in copies:
        copy_in.start()
    for copy_in, copy_out in copies:
        copy_in.wait()
        copy_out.start()
    for _, copy_out in copies:
        copy_out.wait()


def regrouped(perambulator, high, half, pair_count):
    columns, width = perambulator.shape[1:]
    source = perambulator.reshape(2, half, pair_count, columns, width)
    shape = (half, 2, pair_count, columns, width)
    return pl.pallas_call(
        regroup_kernel,
        in_specs=[SMEM, HBM],
        out_specs=HBM,
        out_shape=jax.ShapeDtypeStruct(shape, perambulator.dtype),
        scratch_shapes=[
            pltpu.VMEM(shape, perambulator.dtype),
            pltpu.SemaphoreType.DMA((2 * half,)),
            pltpu.SemaphoreType.DMA((2 * half,)),
        ],
        compiler_params=pltpu.CompilerParams(vmem_limit_bytes=58 * 1024 * 1024),
    )(high.reshape(1), source)


def tied(x, *earlier):
    return pl.pallas_call(
        lambda *refs: None,
        in_specs=[ANYWHERE] * (1 + len(earlier)),
        out_specs=ANYWHERE,
        out_shape=jax.ShapeDtypeStruct(x.shape, x.dtype),
        input_output_aliases={0: 0},
    )(x, *earlier)


def halves_swapped(x):
    vectors = x.shape[1] // 2
    return jnp.concatenate([x[:, vectors:], x[:, :vectors]], axis=1)


def pairs_kernel(pairs, lead, first, begins, counts_ref, tau_ref, *refs):
    begin_ref = refs[0] if begins else None
    refs = refs[begins:]
    sink_refs = refs[:pairs]
    source_ref, out_ref, sinks, sources, tall_ref, turned_ref, left_ref, sink_sems, source_sems = (
        refs[pairs:]
    )
    slots, vectors, packed = sinks.shape[1:]
    spins, _, width = left_ref.shape
    blocks = width // packed
    pieces = tau_ref.shape[0] // spins
    pair = pl.program_id(0)
    first_half = lax.broadcasted_iota(jnp.int32, (vectors, packed), 1) < vectors

    @pl.when(pair == 0)
    def _():
        for p in range(pairs):
            for d in range(slots):

                @pl.when(d < counts_ref[first + p])
                def _():
                    pltpu.make_async_copy(
                        sink_refs[p].at[d], sinks.at[p, d], sink_sems.at[p, d]
                    ).start()
                    pltpu.make_async_copy(
                        source_ref.at[first + p, d], sources.at[p, d], source_sems.at[p, d]
                    ).start()

        for p in range(out_ref.shape[0]):
            for d in range(slots):
                for side in range(2):
                    out_ref[p, side, d] = begin_ref[p, side, d] if begins else 0.0

    def part(s, b):
        lanes = slice(b * packed, (b + 1) * packed)
        return tau_ref[s * pieces : (s + 1) * pieces, 0, :, lanes].reshape(vectors, packed)

    for s in range(spins):
        for b in range(blocks):
            tall = part(s, b).T
            middle = b * packed + vectors
            tall_ref[s, b * packed : (b + 1) * packed] = tall
            turned_ref[s, b * packed : middle] = -tall[vectors:]
            turned_ref[s, middle : (b + 1) * packed] = tall[:vectors]

    @pl.loop(0, counts_ref[first + pair])
    def _(d):
        pltpu.make_async_copy(
            sink_refs[0].at[0], sinks.at[pair, d], sink_sems.at[pair, d]
        ).wait()
        sink = sinks[pair, d]
        embedding = jnp.concatenate(
            [jnp.where(first_half, sink, -sink), halves_swapped(sink)], axis=0
        )
        for s in range(spins):
            stacked = jnp.concatenate([part(s, b) for b in range(blocks)], axis=0)
            left = lax.dot_general(
                stacked, embedding, NT_DIMS, preferred_element_type=jnp.float32
            ).astype(jnp.bfloat16)
            for b in range(blocks):
                left_ref[s, :, b * packed : (b + 1) * packed] = left[
                    b * vectors : (b + 1) * vectors
                ]
        block_real = jnp.zeros((vectors, vectors), jnp.float32)
        block_imag = jnp.zeros((vectors, vectors), jnp.float32)
        for s in range(spins):
            block_real += jnp.dot(left_ref[s], tall_ref[s], preferred_element_type=jnp.float32)
            block_imag += jnp.dot(left_ref[s], turned_ref[s], preferred_element_type=jnp.float32)
        pltpu.make_async_copy(
            source_ref.at[0, 0], sources.at[pair, d], source_sems.at[pair, d]
        ).wait()
        source = sources[pair, d].astype(jnp.float32)
        real = source[:, :vectors]
        imag = source[:, vectors:]
        row = lead + first + pair
        out_ref[row, 0, d] += jnp.sum(real * block_real - imag * block_imag)
        out_ref[row, 1, d] += jnp.sum(real * block_imag + imag * block_real)


def pairs_sums(tau, side, first, sinks, sources, counts, *begin):
    pairs = len(sinks)
    slots, vectors, packed = sinks[0].shape
    pieces, _, columns, width = tau.shape
    spins = pieces * columns // vectors
    lead = side * counts.shape[0]
    flops = 4 * pairs * spins * slots * width * vectors * packed
    moved = 2 * pairs * (spins * vectors * width + 2 * slots * vectors * packed)
    elemental_copies = [pltpu.VMEM((pairs, slots, vectors, packed), jnp.bfloat16)] * 2
    return pl.pallas_call(
        functools.partial(pairs_kernel, pairs, lead, first, len(begin)),
        grid=(pairs,),
        in_specs=[
            SMEM,
            pl.BlockSpec((pieces, 1, columns, width), lambda p: (0, lead + first + p, 0, 0)),
        ]
        + [SMEM] * len(begin)
        + [HBM] * (pairs + 1),
        out_specs=SMEM,
        out_shape=jax.ShapeDtypeStruct((2 * counts.shape[0], 2, slots), jnp.float32),
        scratch_shapes=elemental_copies
        + [
            pltpu.VMEM((spins, width, vectors), jnp.bfloat16),
            pltpu.VMEM((spins, width, vectors), jnp.bfloat16),
            pltpu.VMEM((spins, vectors, width), jnp.bfloat16),
            pltpu.SemaphoreType.DMA((pairs, slots)),
            pltpu.SemaphoreType.DMA((pairs, slots)),
        ],
        compiler_params=pltpu.CompilerParams(vmem_limit_bytes=VMEM_BYTES),
        cost_estimate=pl.CostEstimate(flops=flops, bytes_accessed=moved, transcendentals=0),
    )(counts, tau, *begin, *sinks, sources)


def body(perambulator, elementals, diagrams, counts):
    devices = lax.axis_size("tm")
    me = lax.axis_index("tm")
    pair_count, slots = diagrams.shape[:2]
    columns, width = perambulator.shape[1:]
    vectors, packed = elementals.shape[2:]
    half = devices // 2
    own_set = elementals[0]
    high = (me >= half).astype(jnp.int32)
    halves = [list(range(half)), list(range(half, devices))]

    steps = [(slot + 1) * devices // (pair_count + 1) for slot in range(pair_count)]
    wanted = [passed_along(diagrams[slot, :, 0], by) for slot, by in enumerate(steps)]
    given_counts = exchanged(counts, half)
    own_sources = jnp.take(own_set, diagrams[:, :, 1].reshape(-1), axis=0, mode="clip")
    own_sources = own_sources.reshape(pair_count, slots, vectors, packed)
    given_sources = exchanged(own_sources, half)
    chosen = [jnp.take(own_set, index, axis=0, mode="clip") for index in wanted]
    given_sinks = [passed_along(sets, -by, half) for by, sets in zip(steps, chosen)]
    last = pair_count - 1
    own_sinks = [
        passed_along(sets if slot < last else tied(sets, given_sinks[0]), -by)
        for slot, (by, sets) in enumerate(zip(steps, chosen))
    ]

    tau = lax.all_to_all(
        tied(regrouped(perambulator, high, half, pair_count), given_counts, *wanted),
        "tm",
        split_axis=0,
        concat_axis=0,
        axis_index_groups=halves,
        tiled=True,
    ).reshape(half, 2 * pair_count, columns, width)
    if columns % 16 != 0:
        tau = jnp.moveaxis(tau, 1, 0).reshape(2 * pair_count, -1, vectors, width)
        tau = jnp.moveaxis(tau, 0, 1)

    sums = pairs_sums(tau, 0, 0, given_sinks, given_sources, given_counts)
    sums = pairs_sums(tau, 1, 0, own_sinks[:last], own_sources, counts, sums)
    got = exchanged(sums, half)
    sums = pairs_sums(tau, 1, last, own_sinks[last:], own_sources, counts, sums)
    total = (sums[pair_count:] + got[:pair_count]) / (columns * devices)
    return jnp.swapaxes(total, 1, 2)


def solution(mesh):
    return jax.shard_map(
        body,
        mesh=mesh,
        in_specs=(
            P("groups", "tm", None),
            P(("groups", "tm"), None, None, None),
            P("tm", None, None),
            P("tm"),
        ),
        out_specs=P(("groups", "tm"), None, None),
        check_vma=False,
    )
```

```python
import functools

import jax
import jax.numpy as jnp
from jax import lax
from jax.experimental import pallas as pl
from jax.experimental.pallas import tpu as pltpu
from jax.sharding import PartitionSpec as P

NT_DIMS = (((1,), (1,)), ((), ()))
ANYWHERE = pl.BlockSpec(memory_space=pl.ANY)
VMEM_BYTES = 60 * 1024 * 1024
HBM = pl.BlockSpec(memory_space=pltpu.HBM)
VMEM = pl.BlockSpec(memory_space=pltpu.VMEM)
SMEM = pl.BlockSpec(memory_space=pltpu.SMEM)


def exchanged(x, mask):
    devices = lax.axis_size("tm")
    return lax.ppermute(x, "tm", [(i, i ^ mask) for i in range(devices)])


def passed_along(x, by, mask=0):
    devices = lax.axis_size("tm")
    return lax.ppermute(x, "tm", [(i, ((i + by) % devices) ^ mask) for i in range(devices)])


def regroup_kernel(high_ref, source_ref, out_ref, block_ref, in_sems, out_sems):
    high = high_ref[0]
    copies = []
    for j in range(source_ref.shape[1]):
        for side in range(2):
            which = 1 - high if side == 0 else high
            block = block_ref.at[j, side]
            n = 2 * j + side
            copies.append(
                (
                    pltpu.make_async_copy(source_ref.at[which, j], block, in_sems.at[n]),
                    pltpu.make_async_copy(block, out_ref.at[j, side], out_sems.at[n]),
                )
            )
    for copy_in, _ in copies:
        copy_in.start()
    for copy_in, copy_out in copies:
        copy_in.wait()
        copy_out.start()
    for _, copy_out in copies:
        copy_out.wait()


def regrouped(perambulator, high, half, pair_count):
    columns, width = perambulator.shape[1:]
    source = perambulator.reshape(2, half, pair_count, columns, width)
    shape = (half, 2, pair_count, columns, width)
    return pl.pallas_call(
        regroup_kernel,
        in_specs=[SMEM, HBM],
        out_specs=HBM,
        out_shape=jax.ShapeDtypeStruct(shape, perambulator.dtype),
        scratch_shapes=[
            pltpu.VMEM(shape, perambulator.dtype),
            pltpu.SemaphoreType.DMA((2 * half,)),
            pltpu.SemaphoreType.DMA((2 * half,)),
        ],
        compiler_params=pltpu.CompilerParams(vmem_limit_bytes=58 * 1024 * 1024),
    )(high.reshape(1), source)


def tied(x, *earlier):
    return pl.pallas_call(
        lambda *refs: None,
        in_specs=[ANYWHERE] * (1 + len(earlier)),
        out_specs=ANYWHERE,
        out_shape=jax.ShapeDtypeStruct(x.shape, x.dtype),
        input_output_aliases={0: 0},
    )(x, *earlier)


def halves_swapped(x):
    vectors = x.shape[1] // 2
    return jnp.concatenate([x[:, vectors:], x[:, :vectors]], axis=1)


def pairs_kernel(pairs, first, begins, carries, counts_ref, tau_ref, *refs):
    begin_refs, refs = refs[:begins], refs[begins:]
    carry_refs, refs = refs[:carries], refs[carries:]
    sink_refs, source_ref, out_ref = refs[:pairs], refs[pairs], refs[pairs + 1]
    carried_refs, refs = refs[pairs + 2 : pairs + 2 + carries], refs[pairs + 2 + carries :]
    sinks, sources, swap_ref, left_ref, sink_sems, source_sems = refs
    slots, vectors, packed = sinks.shape[1:]
    spins, _, width = left_ref.shape
    blocks = width // packed
    pieces = tau_ref.shape[0] // spins
    pair = pl.program_id(0)
    first_half = lax.broadcasted_iota(jnp.int32, (vectors, packed), 1) < vectors

    @pl.when(pair == 0)
    def _():
        for p in range(pairs):
            for d in range(slots):

                @pl.when(d < counts_ref[first + p])
                def _():
                    pltpu.make_async_copy(
                        sink_refs[p].at[d], sinks.at[p, d], sink_sems.at[p, d]
                    ).start()
                    pltpu.make_async_copy(
                        source_ref.at[first + p, d], sources.at[p, d], source_sems.at[p, d]
                    ).start()

        for p in range(out_ref.shape[0]):
            for d in range(slots):
                for side in range(2):
                    out_ref[p, side, d] = begin_refs[0][p, side, d] if begins else 0.0
                    if carries:
                        carried_refs[0][p, side, d] = carry_refs[0][p, side, d]

    def tile(s):
        return tau_ref[s * pieces : (s + 1) * pieces, 0].reshape(vectors, width)

    def part(x, b):
        return x[:, b * packed : (b + 1) * packed]

    for s in range(spins):
        for b in range(blocks):
            swapped = halves_swapped(part(tile(s), b))
            swap_ref[s, :, b * packed : (b + 1) * packed] = jnp.where(
                first_half, -swapped, swapped
            )

    @pl.loop(0, counts_ref[first + pair])
    def _(d):
        pltpu.make_async_copy(
            sink_refs[0].at[0], sinks.at[pair, d], sink_sems.at[pair, d]
        ).wait()
        sink = sinks[pair, d]
        embedding = jnp.concatenate(
            [jnp.where(first_half, sink, -sink), halves_swapped(sink)], axis=0
        )
        block_real = jnp.zeros((vectors, vectors), jnp.float32)
        block_imag = jnp.zeros((vectors, vectors), jnp.float32)
        for s in range(spins):
            stacked = jnp.concatenate([part(tile(s), b) for b in range(blocks)], axis=0)
            left = lax.dot_general(
                stacked, embedding, NT_DIMS, preferred_element_type=jnp.float32
            ).astype(jnp.bfloat16)
            for b in range(blocks):
                left_ref[s, :, b * packed : (b + 1) * packed] = left[
                    b * vectors : (b + 1) * vectors
                ]
        for s in range(spins):
            block_real += lax.dot_general(
                left_ref[s], tile(s), NT_DIMS, preferred_element_type=jnp.float32
            )
            block_imag += lax.dot_general(
                left_ref[s], swap_ref[s], NT_DIMS, preferred_element_type=jnp.float32
            )
        pltpu.make_async_copy(
            source_ref.at[0, 0], sources.at[pair, d], source_sems.at[pair, d]
        ).wait()
        source = sources[pair, d].astype(jnp.float32)
        real = source[:, :vectors]
        imag = source[:, vectors:]
        out_ref[first + pair, 0, d] += jnp.sum(real * block_real - imag * block_imag)
        out_ref[first + pair, 1, d] += jnp.sum(real * block_imag + imag * block_real)


def pairs_sums(tau, side, first, sinks, sources, counts, begin=[], carry=[]):
    pairs = len(sinks)
    slots, vectors, packed = sinks[0].shape
    pieces, _, columns, width = tau.shape
    spins = pieces * columns // vectors
    lead = side * counts.shape[0] + first
    flops = 4 * pairs * spins * slots * width * vectors * packed
    moved = 2 * pairs * (spins * vectors * width + 2 * slots * vectors * packed)
    elemental_copies = [pltpu.VMEM((pairs, slots, vectors, packed), jnp.bfloat16)] * 2
    call = pl.pallas_call(
        functools.partial(pairs_kernel, pairs, first, len(begin), len(carry)),
        grid=(pairs,),
        in_specs=[
            SMEM,
            pl.BlockSpec((pieces, 1, columns, width), lambda p: (0, lead + p, 0, 0)),
        ]
        + [SMEM] * len(begin + carry)
        + [ANYWHERE] * (pairs + 1),
        out_specs=[SMEM] * (1 + len(carry)),
        out_shape=[jax.ShapeDtypeStruct((counts.shape[0], 2, slots), jnp.float32)]
        * (1 + len(carry)),
        scratch_shapes=elemental_copies
        + [
            pltpu.VMEM((spins, vectors, width), jnp.bfloat16),
            pltpu.VMEM((spins, vectors, width), jnp.bfloat16),
            pltpu.SemaphoreType.DMA((pairs, slots)),
            pltpu.SemaphoreType.DMA((pairs, slots)),
        ],
        compiler_params=pltpu.CompilerParams(vmem_limit_bytes=VMEM_BYTES),
        cost_estimate=pl.CostEstimate(flops=flops, bytes_accessed=moved, transcendentals=0),
    )
    return list(call(counts, tau, *begin, *carry, *sinks, sources))


def body(perambulator, elementals, diagrams, counts):
    devices = lax.axis_size("tm")
    me = lax.axis_index("tm")
    pair_count, slots = diagrams.shape[:2]
    columns, width = perambulator.shape[1:]
    vectors, packed = elementals.shape[2:]
    half = devices // 2
    own_set = elementals[0]
    high = (me >= half).astype(jnp.int32)
    halves = [list(range(half)), list(range(half, devices))]

    steps = [(slot + 1) * devices // (pair_count + 1) for slot in range(pair_count)]
    wanted = [passed_along(diagrams[slot, :, 0], by) for slot, by in enumerate(steps)]
    given_counts = exchanged(counts, half)
    own_sources = jnp.take(own_set, diagrams[:, :, 1].reshape(-1), axis=0, mode="clip")
    own_sources = own_sources.reshape(pair_count, slots, vectors, packed)
    given_sources = exchanged(own_sources, half)
    chosen = [jnp.take(own_set, index, axis=0, mode="clip") for index in wanted]
    given_sinks = [passed_along(sets, -by, half) for by, sets in zip(steps, chosen)]
    last = pair_count - 1
    own_sinks = [
        passed_along(sets if slot < last else tied(sets, given_sinks[0]), -by)
        for slot, (by, sets) in enumerate(zip(steps, chosen))
    ]

    tau = lax.all_to_all(
        tied(regrouped(perambulator, high, half, pair_count), given_counts, *wanted),
        "tm",
        split_axis=0,
        concat_axis=0,
        axis_index_groups=halves,
        tiled=True,
    ).reshape(half, 2 * pair_count, columns, width)
    if columns % 16 != 0:
        tau = jnp.moveaxis(tau, 1, 0).reshape(2 * pair_count, -1, vectors, width)
        tau = jnp.moveaxis(tau, 0, 1)

    given = pairs_sums(tau, 0, 0, given_sinks, given_sources, given_counts)
    kept, given = pairs_sums(tau, 1, 0, own_sinks[:last], own_sources, counts, carry=given)
    got = exchanged(given, half)
    (kept,) = pairs_sums(tau, 1, last, own_sinks[last:], own_sources, counts, [kept])
    return jnp.swapaxes((kept + got) / (columns * devices), 1, 2)


def solution(mesh):
    return jax.shard_map(
        body,
        mesh=mesh,
        in_specs=(
            P("groups", "tm", None),
            P(("groups", "tm"), None, None, None),
            P("tm", None, None),
            P("tm"),
        ),
        out_specs=P(("groups", "tm"), None, None),
        check_vma=False,
    )
```

```python
import functools

import jax
import jax.numpy as jnp
from jax import lax
from jax.experimental import pallas as pl
from jax.experimental.pallas import tpu as pltpu
from jax.sharding import PartitionSpec as P

NT_DIMS = (((1,), (1,)), ((), ()))
ANYWHERE = pl.BlockSpec(memory_space=pl.ANY)
HBM = pl.BlockSpec(memory_space=pltpu.HBM)
VMEM = pl.BlockSpec(memory_space=pltpu.VMEM)
SMEM = pl.BlockSpec(memory_space=pltpu.SMEM)


def exchanged(x, mask):
    devices = lax.axis_size("tm")
    return lax.ppermute(x, "tm", [(i, i ^ mask) for i in range(devices)])


def passed_along(x, by, mask=0):
    devices = lax.axis_size("tm")
    return lax.ppermute(x, "tm", [(i, ((i + by) % devices) ^ mask) for i in range(devices)])


def regroup_kernel(high_ref, source_ref, out_ref, block_ref, in_sems, out_sems):
    high = high_ref[0]
    copies = []
    for j in range(source_ref.shape[1]):
        for side in range(2):
            which = 1 - high if side == 0 else high
            block = block_ref.at[j, side]
            n = 2 * j + side
            copies.append(
                (
                    pltpu.make_async_copy(source_ref.at[which, j], block, in_sems.at[n]),
                    pltpu.make_async_copy(block, out_ref.at[j, side], out_sems.at[n]),
                )
            )
    for copy_in, _ in copies:
        copy_in.start()
    for copy_in, copy_out in copies:
        copy_in.wait()
        copy_out.start()
    for _, copy_out in copies:
        copy_out.wait()


def regrouped(perambulator, high, half, pair_count):
    columns, width = perambulator.shape[1:]
    source = perambulator.reshape(2, half, pair_count, columns, width)
    shape = (half, 2, pair_count, columns, width)
    return pl.pallas_call(
        regroup_kernel,
        in_specs=[SMEM, HBM],
        out_specs=HBM,
        out_shape=jax.ShapeDtypeStruct(shape, perambulator.dtype),
        scratch_shapes=[
            pltpu.VMEM(shape, perambulator.dtype),
            pltpu.SemaphoreType.DMA((2 * half,)),
            pltpu.SemaphoreType.DMA((2 * half,)),
        ],
        compiler_params=pltpu.CompilerParams(vmem_limit_bytes=58 * 1024 * 1024),
    )(high.reshape(1), source)


def tied(x, *earlier):
    return pl.pallas_call(
        lambda *refs: None,
        in_specs=[ANYWHERE] + [ANYWHERE if e.ndim > 1 else VMEM for e in earlier],
        out_specs=ANYWHERE,
        out_shape=jax.ShapeDtypeStruct(x.shape, x.dtype),
        input_output_aliases={0: 0},
    )(x, *earlier)


def halves_swapped(x):
    vectors = x.shape[1] // 2
    return jnp.concatenate([x[:, vectors:], x[:, :vectors]], axis=1)


def pairs_kernel(pairs, first, begins, carries, counts_ref, tau_ref, *refs):
    begin_refs, refs = refs[:begins], refs[begins:]
    carry_refs, refs = refs[:carries], refs[carries:]
    sink_refs, source_ref, out_ref = refs[:pairs], refs[pairs], refs[pairs + 1]
    carried_refs, refs = refs[pairs + 2 : pairs + 2 + carries], refs[pairs + 2 + carries :]
    sinks, sources, swap_ref, left_ref, sink_sems, source_sems = refs
    slots, vectors, packed = sinks.shape[1:]
    spins, _, width = left_ref.shape
    blocks = width // packed
    pieces = tau_ref.shape[0] // spins
    pair = pl.program_id(0)
    first_half = lax.broadcasted_iota(jnp.int32, (vectors, packed), 1) < vectors

    @pl.when(pair == 0)
    def _():
        for p in range(pairs):
            for d in range(slots):

                @pl.when(d < counts_ref[first + p])
                def _():
                    pltpu.make_async_copy(
                        sink_refs[p].at[d], sinks.at[p, d], sink_sems.at[p, d]
                    ).start()
                    pltpu.make_async_copy(
                        source_ref.at[first + p, d], sources.at[p, d], source_sems.at[p, d]
                    ).start()

        for p in range(out_ref.shape[0]):
            for d in range(slots):
                for side in range(2):
                    out_ref[p, side, d] = begin_refs[0][p, side, d] if begins else 0.0
                    if carries:
                        carried_refs[0][p, side, d] = carry_refs[0][p, side, d]

    def tile(s):
        return tau_ref[s * pieces : (s + 1) * pieces, 0].reshape(vectors, width)

    def part(x, b):
        return x[:, b * packed : (b + 1) * packed]

    for s in range(spins):
        for b in range(blocks):
            swapped = halves_swapped(part(tile(s), b))
            swap_ref[s, :, b * packed : (b + 1) * packed] = jnp.where(
                first_half, -swapped, swapped
            )

    @pl.loop(0, counts_ref[first + pair])
    def _(d):
        pltpu.make_async_copy(
            sink_refs[0].at[0], sinks.at[pair, d], sink_sems.at[pair, d]
        ).wait()
        sink = sinks[pair, d]
        embedding = jnp.concatenate(
            [jnp.where(first_half, sink, -sink), halves_swapped(sink)], axis=0
        )
        block_real = jnp.zeros((vectors, vectors), jnp.float32)
        block_imag = jnp.zeros((vectors, vectors), jnp.float32)
        for s in range(spins):
            stacked = jnp.concatenate([part(tile(s), b) for b in range(blocks)], axis=0)
            left = lax.dot_general(
                stacked, embedding, NT_DIMS, preferred_element_type=jnp.float32
            ).astype(jnp.bfloat16)
            for b in range(blocks):
                left_ref[s, :, b * packed : (b + 1) * packed] = left[
                    b * vectors : (b + 1) * vectors
                ]
        for s in range(spins):
            block_real += lax.dot_general(
                left_ref[s], tile(s), NT_DIMS, preferred_element_type=jnp.float32
            )
            block_imag += lax.dot_general(
                left_ref[s], swap_ref[s], NT_DIMS, preferred_element_type=jnp.float32
            )
        pltpu.make_async_copy(
            source_ref.at[0, 0], sources.at[pair, d], source_sems.at[pair, d]
        ).wait()
        source = sources[pair, d].astype(jnp.float32)
        real = source[:, :vectors]
        imag = source[:, vectors:]
        out_ref[first + pair, 0, d] += jnp.sum(real * block_real - imag * block_imag)
        out_ref[first + pair, 1, d] += jnp.sum(real * block_imag + imag * block_real)


def pairs_sums(tau, side, first, sinks, sources, counts, begin=[], carry=[], place=ANYWHERE, vmem=60):
    pairs = len(sinks)
    slots, vectors, packed = sinks[0].shape
    pieces, _, columns, width = tau.shape
    spins = pieces * columns // vectors
    lead = side * counts.shape[0] + first
    flops = 4 * pairs * spins * slots * width * vectors * packed
    moved = 2 * pairs * (spins * vectors * width + 2 * slots * vectors * packed)
    elemental_copies = [pltpu.VMEM((pairs, slots, vectors, packed), jnp.bfloat16)] * 2
    call = pl.pallas_call(
        functools.partial(pairs_kernel, pairs, first, len(begin), len(carry)),
        grid=(pairs,),
        in_specs=[
            SMEM,
            pl.BlockSpec((pieces, 1, columns, width), lambda p: (0, lead + p, 0, 0)),
        ]
        + [SMEM] * len(begin + carry)
        + [place] * pairs
        + [ANYWHERE],
        out_specs=[SMEM] * (1 + len(carry)),
        out_shape=[jax.ShapeDtypeStruct((counts.shape[0], 2, slots), jnp.float32)]
        * (1 + len(carry)),
        scratch_shapes=elemental_copies
        + [
            pltpu.VMEM((spins, vectors, width), jnp.bfloat16),
            pltpu.VMEM((spins, vectors, width), jnp.bfloat16),
            pltpu.SemaphoreType.DMA((pairs, slots)),
            pltpu.SemaphoreType.DMA((pairs, slots)),
        ],
        compiler_params=pltpu.CompilerParams(vmem_limit_bytes=vmem * 1024 * 1024),
        cost_estimate=pl.CostEstimate(flops=flops, bytes_accessed=moved, transcendentals=0),
    )
    return list(call(counts, tau, *begin, *carry, *sinks, sources))


def body(perambulator, elementals, diagrams, counts):
    devices = lax.axis_size("tm")
    me = lax.axis_index("tm")
    pair_count, slots = diagrams.shape[:2]
    columns, width = perambulator.shape[1:]
    vectors, packed = elementals.shape[2:]
    half = devices // 2
    own_set = elementals[0]
    high = (me >= half).astype(jnp.int32)
    halves = [list(range(half)), list(range(half, devices))]

    steps = [(slot + 1) * devices // (pair_count + 1) for slot in range(pair_count)]
    wanted = [passed_along(diagrams[slot, :, 0], by) for slot, by in enumerate(steps)]
    given_counts = exchanged(counts, half)
    own_sources = jnp.take(own_set, diagrams[:, :, 1].reshape(-1), axis=0, mode="clip")
    own_sources = own_sources.reshape(pair_count, slots, vectors, packed)
    given_sources = exchanged(own_sources, half)
    chosen = [jnp.take(own_set, index, axis=0, mode="clip") for index in wanted]
    given_sinks = [passed_along(sets, -by, half) for by, sets in zip(steps, chosen)]
    last = pair_count - 1
    own_sinks = [
        passed_along(sets if slot < last else tied(sets, given_sinks[0]), -by)
        for slot, (by, sets) in enumerate(zip(steps, chosen))
    ]

    tau = lax.all_to_all(
        tied(regrouped(perambulator, high, half, pair_count), given_counts, *wanted),
        "tm",
        split_axis=0,
        concat_axis=0,
        axis_index_groups=halves,
        tiled=True,
    ).reshape(half, 2 * pair_count, columns, width)
    if columns % 16 != 0:
        tau = jnp.moveaxis(tau, 1, 0).reshape(2 * pair_count, -1, vectors, width)
        tau = jnp.moveaxis(tau, 0, 1)

    given = pairs_sums(tau, 0, 0, given_sinks, given_sources, given_counts)
    kept, given = pairs_sums(tau, 1, 0, own_sinks[:last], own_sources, counts, carry=given)
    got = exchanged(given, half)
    (kept,) = pairs_sums(
        tau, 1, last, own_sinks[last:], own_sources, counts, [kept], place=VMEM, vmem=24
    )
    return jnp.swapaxes((kept + got) / (columns * devices), 1, 2)


def solution(mesh):
    return jax.shard_map(
        body,
        mesh=mesh,
        in_specs=(
            P("groups", "tm", None),
            P(("groups", "tm"), None, None, None),
            P("tm", None, None),
            P("tm"),
        ),
        out_specs=P(("groups", "tm"), None, None),
        check_vma=False,
    )
```

```python
import functools

import jax
import jax.numpy as jnp
from jax import lax
from jax.experimental import pallas as pl
from jax.experimental.pallas import tpu as pltpu
from jax.sharding import PartitionSpec as P

NT_DIMS = (((1,), (1,)), ((), ()))
ANYWHERE = pl.BlockSpec(memory_space=pl.ANY)
HBM = pl.BlockSpec(memory_space=pltpu.HBM)
VMEM = pl.BlockSpec(memory_space=pltpu.VMEM)
SMEM = pl.BlockSpec(memory_space=pltpu.SMEM)


def exchanged(x, mask):
    devices = lax.axis_size("tm")
    return lax.ppermute(x, "tm", [(i, i ^ mask) for i in range(devices)])


def passed_along(x, by, mask=0):
    devices = lax.axis_size("tm")
    return lax.ppermute(x, "tm", [(i, ((i + by) % devices) ^ mask) for i in range(devices)])


def regroup_kernel(high_ref, source_ref, out_ref, block_ref, in_sems, out_sems):
    high = high_ref[0]
    copies = []
    for j in range(source_ref.shape[1]):
        for side in range(2):
            which = 1 - high if side == 0 else high
            block = block_ref.at[j, side]
            n = 2 * j + side
            copies.append(
                (
                    pltpu.make_async_copy(source_ref.at[which, j], block, in_sems.at[n]),
                    pltpu.make_async_copy(block, out_ref.at[j, side], out_sems.at[n]),
                )
            )
    for copy_in, _ in copies:
        copy_in.start()
    for copy_in, copy_out in copies:
        copy_in.wait()
        copy_out.start()
    for _, copy_out in copies:
        copy_out.wait()


def regrouped(perambulator, high, half, pair_count):
    columns, width = perambulator.shape[1:]
    source = perambulator.reshape(2, half, pair_count, columns, width)
    shape = (half, 2, pair_count, columns, width)
    return pl.pallas_call(
        regroup_kernel,
        in_specs=[SMEM, HBM],
        out_specs=HBM,
        out_shape=jax.ShapeDtypeStruct(shape, perambulator.dtype),
        scratch_shapes=[
            pltpu.VMEM(shape, perambulator.dtype),
            pltpu.SemaphoreType.DMA((2 * half,)),
            pltpu.SemaphoreType.DMA((2 * half,)),
        ],
        compiler_params=pltpu.CompilerParams(vmem_limit_bytes=58 * 1024 * 1024),
    )(high.reshape(1), source)


def tied(x, *earlier):
    return pl.pallas_call(
        lambda *refs: None,
        in_specs=[ANYWHERE] * (1 + len(earlier)),
        out_specs=ANYWHERE,
        out_shape=jax.ShapeDtypeStruct(x.shape, x.dtype),
        input_output_aliases={0: 0},
    )(x, *earlier)


def halves_swapped(x):
    vectors = x.shape[1] // 2
    return jnp.concatenate([x[:, vectors:], x[:, :vectors]], axis=1)


def pairs_kernel(pairs, first, begins, carries, direct, counts_ref, tau_ref, *refs):
    begin_refs, refs = refs[:begins], refs[begins:]
    carry_refs, refs = refs[:carries], refs[carries:]
    sink_refs, source_ref, out_ref = refs[:pairs], refs[pairs], refs[pairs + 1]
    carried_refs, refs = refs[pairs + 2 : pairs + 2 + carries], refs[pairs + 2 + carries :]
    sinks, sources, swap_ref, left_ref, sink_sems, source_sems = refs
    slots, vectors, packed = sinks.shape[1:]
    spins, _, width = swap_ref.shape
    blocks = width // packed
    pieces = tau_ref.shape[0] // spins
    pair = pl.program_id(0)
    first_half = lax.broadcasted_iota(jnp.int32, (vectors, packed), 1) < vectors

    @pl.when(pair == 0)
    def _():
        for p in range(pairs):
            for d in range(slots):

                @pl.when((d == 0) | (counts_ref[first + p] > 1))
                def _():
                    if not direct:
                        pltpu.make_async_copy(
                            sink_refs[p].at[d], sinks.at[p, d], sink_sems.at[p, d]
                        ).start()
                    pltpu.make_async_copy(
                        source_ref.at[first + p, d], sources.at[p, d], source_sems.at[p, d]
                    ).start()

        for p in range(out_ref.shape[0]):
            for d in range(slots):
                for side in range(2):
                    out_ref[p, side, d] = begin_refs[0][p, side, d] if begins else 0.0
                    if carries:
                        carried_refs[0][p, side, d] = carry_refs[0][p, side, d]

    def tile(s):
        return tau_ref[s * pieces : (s + 1) * pieces, 0].reshape(vectors, width)

    def part(x, b):
        return x[:, b * packed : (b + 1) * packed]

    for s in range(spins):
        for b in range(blocks):
            swapped = halves_swapped(part(tile(s), b))
            swap_ref[s, :, b * packed : (b + 1) * packed] = jnp.where(
                first_half, -swapped, swapped
            )

    def embedded(d):
        if direct:
            sink = sink_refs[0][d]
        else:
            pltpu.make_async_copy(
                sink_refs[0].at[0], sinks.at[pair, d], sink_sems.at[pair, d]
            ).wait()
            sink = sinks[pair, d]
        return [jnp.where(first_half, sink, -sink), halves_swapped(sink)]

    def add_slots(taken):
        embedding = jnp.concatenate([half for d in range(taken) for half in embedded(d)], axis=0)
        for s in range(spins):
            stacked = jnp.concatenate([part(tile(s), b) for b in range(blocks)], axis=0)
            left = lax.dot_general(
                stacked, embedding, NT_DIMS, preferred_element_type=jnp.float32
            ).astype(jnp.bfloat16)
            for d in range(taken):
                for b in range(blocks):
                    left_ref[
                        s, d * vectors : (d + 1) * vectors, b * packed : (b + 1) * packed
                    ] = left[b * vectors : (b + 1) * vectors, d * packed : (d + 1) * packed]
        block_real = jnp.zeros((taken * vectors, vectors), jnp.float32)
        block_imag = jnp.zeros((taken * vectors, vectors), jnp.float32)
        for s in range(spins):
            left = left_ref[s, : taken * vectors]
            block_real += lax.dot_general(
                left, tile(s), NT_DIMS, preferred_element_type=jnp.float32
            )
            block_imag += lax.dot_general(
                left, swap_ref[s], NT_DIMS, preferred_element_type=jnp.float32
            )
        for d in range(taken):
            pltpu.make_async_copy(
                source_ref.at[0, 0], sources.at[pair, d], source_sems.at[pair, d]
            ).wait()
            source = sources[pair, d].astype(jnp.float32)
            real = source[:, :vectors]
            imag = source[:, vectors:]
            own_real = block_real[d * vectors : (d + 1) * vectors]
            own_imag = block_imag[d * vectors : (d + 1) * vectors]
            live = d < counts_ref[first + pair]
            out_ref[first + pair, 0, d] += jnp.where(
                live, jnp.sum(real * own_real - imag * own_imag), 0.0
            )
            out_ref[first + pair, 1, d] += jnp.where(
                live, jnp.sum(real * own_imag + imag * own_real), 0.0
            )

    several = counts_ref[first + pair] > 1
    pl.when(several)(lambda: add_slots(slots))
    pl.when(jnp.logical_not(several))(lambda: add_slots(1))


def pairs_sums(tau, side, first, sinks, sources, counts, begin=[], carry=[], place=ANYWHERE, vmem=60):
    pairs = len(sinks)
    slots, vectors, packed = sinks[0].shape
    pieces, _, columns, width = tau.shape
    spins = pieces * columns // vectors
    lead = side * counts.shape[0] + first
    flops = 4 * pairs * spins * slots * width * vectors * packed
    moved = 2 * pairs * (spins * vectors * width + 2 * slots * vectors * packed)
    elemental_copies = [pltpu.VMEM((pairs, slots, vectors, packed), jnp.bfloat16)] * 2
    call = pl.pallas_call(
        functools.partial(
            pairs_kernel, pairs, first, len(begin), len(carry), place is VMEM
        ),
        grid=(pairs,),
        in_specs=[
            SMEM,
            pl.BlockSpec((pieces, 1, columns, width), lambda p: (0, lead + p, 0, 0)),
        ]
        + [SMEM] * len(begin + carry)
        + [place] * pairs
        + [ANYWHERE],
        out_specs=[SMEM] * (1 + len(carry)),
        out_shape=[jax.ShapeDtypeStruct((counts.shape[0], 2, slots), jnp.float32)]
        * (1 + len(carry)),
        scratch_shapes=elemental_copies
        + [
            pltpu.VMEM((spins, vectors, width), jnp.bfloat16),
            pltpu.VMEM((spins, slots * vectors, width), jnp.bfloat16),
            pltpu.SemaphoreType.DMA((pairs, slots)),
            pltpu.SemaphoreType.DMA((pairs, slots)),
        ],
        compiler_params=pltpu.CompilerParams(vmem_limit_bytes=vmem * 1024 * 1024),
        cost_estimate=pl.CostEstimate(flops=flops, bytes_accessed=moved, transcendentals=0),
    )
    return list(call(counts, tau, *begin, *carry, *sinks, sources))


def body(perambulator, elementals, diagrams, counts):
    devices = lax.axis_size("tm")
    me = lax.axis_index("tm")
    pair_count, slots = diagrams.shape[:2]
    columns, width = perambulator.shape[1:]
    vectors, packed = elementals.shape[2:]
    half = devices // 2
    own_set = elementals[0]
    high = (me >= half).astype(jnp.int32)
    halves = [list(range(half)), list(range(half, devices))]

    steps = [(slot + 1) * devices // (pair_count + 1) for slot in range(pair_count)]
    wanted = [passed_along(diagrams[slot, :, 0], by) for slot, by in enumerate(steps)]
    given_counts = exchanged(counts, half)
    own_sources = jnp.take(own_set, diagrams[:, :, 1].reshape(-1), axis=0, mode="clip")
    own_sources = own_sources.reshape(pair_count, slots, vectors, packed)
    given_sources = exchanged(own_sources, half)
    chosen = [jnp.take(own_set, index, axis=0, mode="clip") for index in wanted]
    given_sinks = [passed_along(sets, -by, half) for by, sets in zip(steps, chosen)]
    last = pair_count - 1
    own_sinks = [
        passed_along(sets if slot < last else tied(sets, given_sinks[0]), -by)
        for slot, (by, sets) in enumerate(zip(steps, chosen))
    ]

    tau = lax.all_to_all(
        tied(regrouped(perambulator, high, half, pair_count), given_counts, *wanted),
        "tm",
        split_axis=0,
        concat_axis=0,
        axis_index_groups=halves,
        tiled=True,
    ).reshape(half, 2 * pair_count, columns, width)
    if columns % 16 != 0:
        tau = jnp.moveaxis(tau, 1, 0).reshape(2 * pair_count, -1, vectors, width)
        tau = jnp.moveaxis(tau, 0, 1)

    given = pairs_sums(tau, 0, 0, given_sinks, given_sources, given_counts)
    kept, given = pairs_sums(tau, 1, 0, own_sinks[:last], own_sources, counts, carry=given)
    got = exchanged(given, half)
    (kept,) = pairs_sums(
        tau, 1, last, own_sinks[last:], own_sources, counts, [kept], place=VMEM, vmem=24
    )
    return jnp.swapaxes((kept + got) / (columns * devices), 1, 2)


def solution(mesh):
    return jax.shard_map(
        body,
        mesh=mesh,
        in_specs=(
            P("groups", "tm", None),
            P(("groups", "tm"), None, None, None),
            P("tm", None, None),
            P("tm"),
        ),
        out_specs=P(("groups", "tm"), None, None),
        check_vma=False,
    )
```

```python
import functools

import jax
import jax.numpy as jnp
from jax import lax
from jax.experimental import pallas as pl
from jax.experimental.pallas import tpu as pltpu
from jax.sharding import PartitionSpec as P

NT_DIMS = (((1,), (1,)), ((), ()))
ANYWHERE = pl.BlockSpec(memory_space=pl.ANY)
HBM = pl.BlockSpec(memory_space=pltpu.HBM)
VMEM = pl.BlockSpec(memory_space=pltpu.VMEM)
SMEM = pl.BlockSpec(memory_space=pltpu.SMEM)


def exchanged(x, mask):
    devices = lax.axis_size("tm")
    return lax.ppermute(x, "tm", [(i, i ^ mask) for i in range(devices)])


def passed_along(x, by, mask=0):
    devices = lax.axis_size("tm")
    return lax.ppermute(x, "tm", [(i, ((i + by) % devices) ^ mask) for i in range(devices)])


def regroup_kernel(high_ref, source_ref, out_ref, block_ref, in_sems, out_sems):
    high = high_ref[0]
    copies = []
    for j in range(source_ref.shape[1]):
        for side in range(2):
            which = 1 - high if side == 0 else high
            block = block_ref.at[j, side]
            n = 2 * j + side
            copies.append(
                (
                    pltpu.make_async_copy(source_ref.at[which, j], block, in_sems.at[n]),
                    pltpu.make_async_copy(block, out_ref.at[j, side], out_sems.at[n]),
                )
            )
    for copy_in, _ in copies:
        copy_in.start()
    for copy_in, copy_out in copies:
        copy_in.wait()
        copy_out.start()
    for _, copy_out in copies:
        copy_out.wait()


def regrouped(perambulator, high, half, pair_count):
    columns, width = perambulator.shape[1:]
    source = perambulator.reshape(2, half, pair_count, columns, width)
    shape = (half, 2, pair_count, columns, width)
    return pl.pallas_call(
        regroup_kernel,
        in_specs=[SMEM, HBM],
        out_specs=HBM,
        out_shape=jax.ShapeDtypeStruct(shape, perambulator.dtype),
        scratch_shapes=[
            pltpu.VMEM(shape, perambulator.dtype),
            pltpu.SemaphoreType.DMA((2 * half,)),
            pltpu.SemaphoreType.DMA((2 * half,)),
        ],
        compiler_params=pltpu.CompilerParams(vmem_limit_bytes=58 * 1024 * 1024),
    )(high.reshape(1), source)


def tied(x, *earlier):
    return pl.pallas_call(
        lambda *refs: None,
        in_specs=[ANYWHERE] * (1 + len(earlier)),
        out_specs=ANYWHERE,
        out_shape=jax.ShapeDtypeStruct(x.shape, x.dtype),
        input_output_aliases={0: 0},
    )(x, *earlier)


def halves_swapped(x):
    vectors = x.shape[1] // 2
    return jnp.concatenate([x[:, vectors:], x[:, :vectors]], axis=1)


def pairs_kernel(pairs, first, begins, carries, direct, counts_ref, tau_ref, *refs):
    begin_refs, refs = refs[:begins], refs[begins:]
    carry_refs, refs = refs[:carries], refs[carries:]
    sink_refs, source_ref, out_ref = refs[:pairs], refs[pairs], refs[pairs + 1]
    carried_refs, refs = refs[pairs + 2 : pairs + 2 + carries], refs[pairs + 2 + carries :]
    sinks, sources, swap_ref, left_ref, sink_sems, source_sems = refs
    slots, vectors, packed = sinks.shape[1:]
    spins, _, width = swap_ref.shape
    blocks = width // packed
    pieces = tau_ref.shape[0] // spins
    pair = pl.program_id(0)
    first_half = lax.broadcasted_iota(jnp.int32, (vectors, packed), 1) < vectors

    @pl.when(pair == 0)
    def _():
        for p in range(pairs):
            for d in range(slots):

                @pl.when((d == 0) | (counts_ref[first + p] > 1))
                def _():
                    if not direct:
                        pltpu.make_async_copy(
                            sink_refs[p].at[d], sinks.at[p, d], sink_sems.at[p, d]
                        ).start()
                    pltpu.make_async_copy(
                        source_ref.at[first + p, d], sources.at[p, d], source_sems.at[p, d]
                    ).start()

        for p in range(out_ref.shape[0]):
            for d in range(slots):
                for side in range(2):
                    out_ref[p, side, d] = begin_refs[0][p, side, d] if begins else 0.0
                    if carries:
                        carried_refs[0][p, side, d] = carry_refs[0][p, side, d]

    def tile(s):
        return tau_ref[s * pieces : (s + 1) * pieces, 0].reshape(vectors, width)

    def part(x, b):
        return x[:, b * packed : (b + 1) * packed]

    for s in range(spins):
        for b in range(blocks):
            swapped = halves_swapped(part(tile(s), b))
            swap_ref[s, :, b * packed : (b + 1) * packed] = jnp.where(
                first_half, -swapped, swapped
            )

    def embedded(d):
        if direct:
            sink = sink_refs[0][d]
        else:
            pltpu.make_async_copy(
                sink_refs[0].at[0], sinks.at[pair, d], sink_sems.at[pair, d]
            ).wait()
            sink = sinks[pair, d]
        return [jnp.where(first_half, sink, -sink), halves_swapped(sink)]

    def add_slots(taken):
        embedding = jnp.concatenate([half for d in range(taken) for half in embedded(d)], axis=0)
        for s in range(spins):
            for pick in (range(blocks // 2), range(blocks // 2, blocks)):
                stacked = jnp.concatenate([part(tile(s), b) for b in pick], axis=0)
                left = lax.dot_general(
                    stacked, embedding, NT_DIMS, preferred_element_type=jnp.float32
                ).astype(jnp.bfloat16)
                for d in range(taken):
                    for n, b in enumerate(pick):
                        left_ref[
                            s, d * vectors : (d + 1) * vectors, b * packed : (b + 1) * packed
                        ] = left[n * vectors : (n + 1) * vectors, d * packed : (d + 1) * packed]
        block_real = jnp.zeros((taken * vectors, vectors), jnp.float32)
        block_imag = jnp.zeros((taken * vectors, vectors), jnp.float32)
        for s in range(spins):
            left = left_ref[s, : taken * vectors]
            block_real += lax.dot_general(
                left, tile(s), NT_DIMS, preferred_element_type=jnp.float32
            )
            block_imag += lax.dot_general(
                left, swap_ref[s], NT_DIMS, preferred_element_type=jnp.float32
            )
        for d in range(taken):
            pltpu.make_async_copy(
                source_ref.at[0, 0], sources.at[pair, d], source_sems.at[pair, d]
            ).wait()
            source = sources[pair, d].astype(jnp.float32)
            real = source[:, :vectors]
            imag = source[:, vectors:]
            own_real = block_real[d * vectors : (d + 1) * vectors]
            own_imag = block_imag[d * vectors : (d + 1) * vectors]
            live = d < counts_ref[first + pair]
            out_ref[first + pair, 0, d] += jnp.where(
                live, jnp.sum(real * own_real - imag * own_imag), 0.0
            )
            out_ref[first + pair, 1, d] += jnp.where(
                live, jnp.sum(real * own_imag + imag * own_real), 0.0
            )

    several = counts_ref[first + pair] > 1
    pl.when(several)(lambda: add_slots(slots))
    pl.when(jnp.logical_not(several))(lambda: add_slots(1))


def pairs_sums(tau, side, first, sinks, sources, counts, begin=[], carry=[], place=ANYWHERE, vmem=60):
    pairs = len(sinks)
    slots, vectors, packed = sinks[0].shape
    pieces, _, columns, width = tau.shape
    spins = pieces * columns // vectors
    lead = side * counts.shape[0] + first
    flops = 4 * pairs * spins * slots * width * vectors * packed
    moved = 2 * pairs * (spins * vectors * width + 2 * slots * vectors * packed)
    elemental_copies = [pltpu.VMEM((pairs, slots, vectors, packed), jnp.bfloat16)] * 2
    call = pl.pallas_call(
        functools.partial(
            pairs_kernel, pairs, first, len(begin), len(carry), place is VMEM
        ),
        grid=(pairs,),
        in_specs=[
            SMEM,
            pl.BlockSpec((pieces, 1, columns, width), lambda p: (0, lead + p, 0, 0)),
        ]
        + [SMEM] * len(begin + carry)
        + [place] * pairs
        + [ANYWHERE],
        out_specs=[SMEM] * (1 + len(carry)),
        out_shape=[jax.ShapeDtypeStruct((counts.shape[0], 2, slots), jnp.float32)]
        * (1 + len(carry)),
        scratch_shapes=elemental_copies
        + [
            pltpu.VMEM((spins, vectors, width), jnp.bfloat16),
            pltpu.VMEM((spins, slots * vectors, width), jnp.bfloat16),
            pltpu.SemaphoreType.DMA((pairs, slots)),
            pltpu.SemaphoreType.DMA((pairs, slots)),
        ],
        compiler_params=pltpu.CompilerParams(vmem_limit_bytes=vmem * 1024 * 1024),
        cost_estimate=pl.CostEstimate(flops=flops, bytes_accessed=moved, transcendentals=0),
    )
    return list(call(counts, tau, *begin, *carry, *sinks, sources))


def body(perambulator, elementals, diagrams, counts):
    devices = lax.axis_size("tm")
    me = lax.axis_index("tm")
    pair_count, slots = diagrams.shape[:2]
    columns, width = perambulator.shape[1:]
    vectors, packed = elementals.shape[2:]
    half = devices // 2
    own_set = elementals[0]
    high = (me >= half).astype(jnp.int32)
    halves = [list(range(half)), list(range(half, devices))]

    steps = [(slot + 1) * devices // (pair_count + 1) for slot in range(pair_count)]
    wanted = [passed_along(diagrams[slot, :, 0], by) for slot, by in enumerate(steps)]
    given_counts = exchanged(counts, half)
    own_sources = jnp.take(own_set, diagrams[:, :, 1].reshape(-1), axis=0, mode="clip")
    own_sources = own_sources.reshape(pair_count, slots, vectors, packed)
    given_sources = exchanged(own_sources, half)
    chosen = [jnp.take(own_set, index, axis=0, mode="clip") for index in wanted]
    given_sinks = [passed_along(sets, -by, half) for by, sets in zip(steps, chosen)]
    last = pair_count - 1
    own_sinks = [
        passed_along(sets if slot < last else tied(sets, given_sinks[0]), -by)
        for slot, (by, sets) in enumerate(zip(steps, chosen))
    ]

    tau = lax.all_to_all(
        tied(regrouped(perambulator, high, half, pair_count), given_counts, *wanted),
        "tm",
        split_axis=0,
        concat_axis=0,
        axis_index_groups=halves,
        tiled=True,
    ).reshape(half, 2 * pair_count, columns, width)
    if columns % 16 != 0:
        tau = jnp.moveaxis(tau, 1, 0).reshape(2 * pair_count, -1, vectors, width)
        tau = jnp.moveaxis(tau, 0, 1)

    given = pairs_sums(tau, 0, 0, given_sinks, given_sources, given_counts)
    kept, given = pairs_sums(tau, 1, 0, own_sinks[:last], own_sources, counts, carry=given, vmem=24)
    got = exchanged(given, half)
    (kept,) = pairs_sums(
        tau, 1, last, own_sinks[last:], own_sources, counts, [kept], place=VMEM, vmem=24
    )
    return jnp.swapaxes((kept + got) / (columns * devices), 1, 2)


def solution(mesh):
    return jax.shard_map(
        body,
        mesh=mesh,
        in_specs=(
            P("groups", "tm", None),
            P(("groups", "tm"), None, None, None),
            P("tm", None, None),
            P("tm"),
        ),
        out_specs=P(("groups", "tm"), None, None),
        check_vma=False,
    )
```

```python
import functools

import jax
import jax.numpy as jnp
from jax import lax
from jax.experimental import pallas as pl
from jax.experimental.pallas import tpu as pltpu
from jax.sharding import PartitionSpec as P

NT_DIMS = (((1,), (1,)), ((), ()))
ANYWHERE = pl.BlockSpec(memory_space=pl.ANY)
HBM = pl.BlockSpec(memory_space=pltpu.HBM)
VMEM = pl.BlockSpec(memory_space=pltpu.VMEM)
SMEM = pl.BlockSpec(memory_space=pltpu.SMEM)


def exchanged(x, mask):
    devices = lax.axis_size("tm")
    return lax.ppermute(x, "tm", [(i, i ^ mask) for i in range(devices)])


def passed_along(x, by, mask=0):
    devices = lax.axis_size("tm")
    return lax.ppermute(x, "tm", [(i, ((i + by) % devices) ^ mask) for i in range(devices)])


def regroup_kernel(high_ref, source_ref, out_ref, block_ref, in_sems, out_sems):
    high = high_ref[0]
    copies = []
    for j in range(source_ref.shape[1]):
        for side in range(2):
            which = 1 - high if side == 0 else high
            block = block_ref.at[j, side]
            n = 2 * j + side
            copies.append(
                (
                    pltpu.make_async_copy(source_ref.at[which, j], block, in_sems.at[n]),
                    pltpu.make_async_copy(block, out_ref.at[j, side], out_sems.at[n]),
                )
            )
    for copy_in, _ in copies:
        copy_in.start()
    for copy_in, copy_out in copies:
        copy_in.wait()
        copy_out.start()
    for _, copy_out in copies:
        copy_out.wait()


def regrouped(perambulator, high, half, pair_count):
    columns, width = perambulator.shape[1:]
    source = perambulator.reshape(2, half, pair_count, columns, width)
    shape = (half, 2, pair_count, columns, width)
    return pl.pallas_call(
        regroup_kernel,
        in_specs=[SMEM, HBM],
        out_specs=HBM,
        out_shape=jax.ShapeDtypeStruct(shape, perambulator.dtype),
        scratch_shapes=[
            pltpu.VMEM(shape, perambulator.dtype),
            pltpu.SemaphoreType.DMA((2 * half,)),
            pltpu.SemaphoreType.DMA((2 * half,)),
        ],
        compiler_params=pltpu.CompilerParams(vmem_limit_bytes=58 * 1024 * 1024),
    )(high.reshape(1), source)


def tied(x, *earlier):
    return pl.pallas_call(
        lambda *refs: None,
        in_specs=[ANYWHERE] * (1 + len(earlier)),
        out_specs=ANYWHERE,
        out_shape=jax.ShapeDtypeStruct(x.shape, x.dtype),
        input_output_aliases={0: 0},
    )(x, *earlier)


def halves_swapped(x):
    vectors = x.shape[1] // 2
    return jnp.concatenate([x[:, vectors:], x[:, :vectors]], axis=1)


def pairs_kernel(pairs, first, begins, carries, direct, counts_ref, tau_ref, *refs):
    begin_refs, refs = refs[:begins], refs[begins:]
    carry_refs, refs = refs[:carries], refs[carries:]
    sink_refs, source_ref, out_ref = refs[:pairs], refs[pairs], refs[pairs + 1]
    carried_refs, refs = refs[pairs + 2 : pairs + 2 + carries], refs[pairs + 2 + carries :]
    sinks, sources, swap_ref, left_ref, sink_sems, source_sems = refs
    slots, vectors, packed = sinks.shape[1:]
    spins, _, width = swap_ref.shape
    blocks = width // packed
    pieces = tau_ref.shape[0] // spins
    pair = pl.program_id(0)
    first_half = lax.broadcasted_iota(jnp.int32, (vectors, packed), 1) < vectors

    @pl.when(pair == 0)
    def _():
        for p in range(pairs):
            for d in range(slots):

                @pl.when((d == 0) | (counts_ref[first + p] > 1))
                def _():
                    if not direct:
                        pltpu.make_async_copy(
                            sink_refs[p].at[d], sinks.at[p, d], sink_sems.at[p, d]
                        ).start()
                    pltpu.make_async_copy(
                        source_ref.at[first + p, d], sources.at[p, d], source_sems.at[p, d]
                    ).start()

        for p in range(out_ref.shape[0]):
            for d in range(slots):
                for side in range(2):
                    out_ref[p, side, d] = begin_refs[0][p, side, d] if begins else 0.0
                    if carries:
                        carried_refs[0][p, side, d] = carry_refs[0][p, side, d]

    def tile(s):
        return tau_ref[s * pieces : (s + 1) * pieces, 0].reshape(vectors, width)

    def part(x, b):
        return x[:, b * packed : (b + 1) * packed]

    for s in range(spins):
        for b in range(blocks):
            swapped = halves_swapped(part(tile(s), b))
            swap_ref[s, :, b * packed : (b + 1) * packed] = jnp.where(
                first_half, -swapped, swapped
            )

    def embedded(d):
        if direct:
            sink = sink_refs[0][d]
        else:
            pltpu.make_async_copy(
                sink_refs[0].at[0], sinks.at[pair, d], sink_sems.at[pair, d]
            ).wait()
            sink = sinks[pair, d]
        return [jnp.where(first_half, sink, -sink), halves_swapped(sink)]

    def add_slots(taken):
        embedding = jnp.concatenate([half for d in range(taken) for half in embedded(d)], axis=0)
        for s in range(spins):
            stacked = jnp.concatenate([part(tile(s), b) for b in range(blocks)], axis=0)
            left = lax.dot_general(
                stacked, embedding, NT_DIMS, preferred_element_type=jnp.float32
            ).astype(jnp.bfloat16)
            for d in range(taken):
                for b in range(blocks):
                    left_ref[
                        s, d * vectors : (d + 1) * vectors, b * packed : (b + 1) * packed
                    ] = left[b * vectors : (b + 1) * vectors, d * packed : (d + 1) * packed]
        block_real = jnp.zeros((taken * vectors, vectors), jnp.float32)
        block_imag = jnp.zeros((taken * vectors, vectors), jnp.float32)
        for s in range(spins):
            left = left_ref[s, : taken * vectors]
            block_real += lax.dot_general(
                left, tile(s), NT_DIMS, preferred_element_type=jnp.float32
            )
            block_imag += lax.dot_general(
                left, swap_ref[s], NT_DIMS, preferred_element_type=jnp.float32
            )
        for d in range(taken):
            pltpu.make_async_copy(
                source_ref.at[0, 0], sources.at[pair, d], source_sems.at[pair, d]
            ).wait()
            source = sources[pair, d].astype(jnp.float32)
            real = source[:, :vectors]
            imag = source[:, vectors:]
            own_real = block_real[d * vectors : (d + 1) * vectors]
            own_imag = block_imag[d * vectors : (d + 1) * vectors]
            live = d < counts_ref[first + pair]
            out_ref[first + pair, 0, d] += jnp.where(
                live, jnp.sum(real * own_real - imag * own_imag), 0.0
            )
            out_ref[first + pair, 1, d] += jnp.where(
                live, jnp.sum(real * own_imag + imag * own_real), 0.0
            )

    several = counts_ref[first + pair] > 1
    pl.when(several)(lambda: add_slots(slots))
    pl.when(jnp.logical_not(several))(lambda: add_slots(1))


def pairs_sums(tau, side, first, sinks, sources, counts, begin=[], carry=[], place=ANYWHERE, vmem=60):
    pairs = len(sinks)
    slots, vectors, packed = sinks[0].shape
    pieces, _, columns, width = tau.shape
    spins = pieces * columns // vectors
    lead = side * counts.shape[0] + first
    flops = 4 * pairs * spins * slots * width * vectors * packed
    moved = 2 * pairs * (spins * vectors * width + 2 * slots * vectors * packed)
    elemental_copies = [pltpu.VMEM((pairs, slots, vectors, packed), jnp.bfloat16)] * 2
    call = pl.pallas_call(
        functools.partial(
            pairs_kernel, pairs, first, len(begin), len(carry), place is VMEM
        ),
        grid=(pairs,),
        in_specs=[
            SMEM,
            pl.BlockSpec((pieces, 1, columns, width), lambda p: (0, lead + p, 0, 0)),
        ]
        + [SMEM] * len(begin + carry)
        + [place] * pairs
        + [ANYWHERE],
        out_specs=[SMEM] * (1 + len(carry)),
        out_shape=[jax.ShapeDtypeStruct((counts.shape[0], 2, slots), jnp.float32)]
        * (1 + len(carry)),
        scratch_shapes=elemental_copies
        + [
            pltpu.VMEM((spins, vectors, width), jnp.bfloat16),
            pltpu.VMEM((spins, slots * vectors, width), jnp.bfloat16),
            pltpu.SemaphoreType.DMA((pairs, slots)),
            pltpu.SemaphoreType.DMA((pairs, slots)),
        ],
        compiler_params=pltpu.CompilerParams(vmem_limit_bytes=vmem * 1024 * 1024),
        cost_estimate=pl.CostEstimate(flops=flops, bytes_accessed=moved, transcendentals=0),
    )
    return list(call(counts, tau, *begin, *carry, *sinks, sources))


def body(perambulator, elementals, diagrams, counts):
    devices = lax.axis_size("tm")
    me = lax.axis_index("tm")
    pair_count, slots = diagrams.shape[:2]
    columns, width = perambulator.shape[1:]
    vectors, packed = elementals.shape[2:]
    half = devices // 2
    own_set = elementals[0]
    high = (me >= half).astype(jnp.int32)
    halves = [list(range(half)), list(range(half, devices))]

    steps = [(slot + 1) * devices // (pair_count + 1) for slot in range(pair_count)]
    wanted = [passed_along(diagrams[slot, :, 0], by) for slot, by in enumerate(steps)]
    given_counts = exchanged(counts, half)
    own_sources = jnp.take(own_set, diagrams[:, :, 1].reshape(-1), axis=0, mode="clip")
    own_sources = own_sources.reshape(pair_count, slots, vectors, packed)
    given_sources = exchanged(own_sources, half)
    chosen = [jnp.take(own_set, index, axis=0, mode="clip") for index in wanted]
    given_sinks = [passed_along(sets, -by, half) for by, sets in zip(steps, chosen)]
    last = pair_count - 1
    own_sinks = [
        passed_along(tied(sets, sent), -by) for by, sets, sent in zip(steps, chosen, given_sinks)
    ]

    tau = lax.all_to_all(
        tied(regrouped(perambulator, high, half, pair_count), given_counts, *wanted),
        "tm",
        split_axis=0,
        concat_axis=0,
        axis_index_groups=halves,
        tiled=True,
    ).reshape(half, 2 * pair_count, columns, width)
    if columns % 16 != 0:
        tau = jnp.moveaxis(tau, 1, 0).reshape(2 * pair_count, -1, vectors, width)
        tau = jnp.moveaxis(tau, 0, 1)

    given = pairs_sums(tau, 0, 0, given_sinks, given_sources, given_counts)
    kept, given = pairs_sums(tau, 1, 0, own_sinks[:last], own_sources, counts, carry=given)
    got = exchanged(given, half)
    (kept,) = pairs_sums(
        tau, 1, last, own_sinks[last:], own_sources, counts, [kept], place=VMEM, vmem=24
    )
    return jnp.swapaxes((kept + got) / (columns * devices), 1, 2)


def solution(mesh):
    return jax.shard_map(
        body,
        mesh=mesh,
        in_specs=(
            P("groups", "tm", None),
            P(("groups", "tm"), None, None, None),
            P("tm", None, None),
            P("tm"),
        ),
        out_specs=P(("groups", "tm"), None, None),
        check_vma=False,
    )
```

```python
import functools

import jax
import jax.numpy as jnp
from jax import lax
from jax.experimental import pallas as pl
from jax.experimental.pallas import tpu as pltpu
from jax.sharding import PartitionSpec as P

NT_DIMS = (((1,), (1,)), ((), ()))
ANYWHERE = pl.BlockSpec(memory_space=pl.ANY)
HBM = pl.BlockSpec(memory_space=pltpu.HBM)
VMEM = pl.BlockSpec(memory_space=pltpu.VMEM)
SMEM = pl.BlockSpec(memory_space=pltpu.SMEM)


def exchanged(x, mask):
    devices = lax.axis_size("tm")
    return lax.ppermute(x, "tm", [(i, i ^ mask) for i in range(devices)])


def passed_along(x, by, mask=0):
    devices = lax.axis_size("tm")
    return lax.ppermute(x, "tm", [(i, ((i + by) % devices) ^ mask) for i in range(devices)])


def regroup_kernel(high_ref, source_ref, out_ref, block_ref, in_sems, out_sems):
    high = high_ref[0]
    copies = []
    for j in range(source_ref.shape[1]):
        for side in range(2):
            which = 1 - high if side == 0 else high
            block = block_ref.at[j, side]
            n = 2 * j + side
            copies.append(
                (
                    pltpu.make_async_copy(source_ref.at[which, j], block, in_sems.at[n]),
                    pltpu.make_async_copy(block, out_ref.at[j, side], out_sems.at[n]),
                )
            )
    for copy_in, _ in copies:
        copy_in.start()
    for copy_in, copy_out in copies:
        copy_in.wait()
        copy_out.start()
    for _, copy_out in copies:
        copy_out.wait()


def regrouped(perambulator, high, half, pair_count):
    columns, width = perambulator.shape[1:]
    source = perambulator.reshape(2, half, pair_count, columns, width)
    shape = (half, 2, pair_count, columns, width)
    return pl.pallas_call(
        regroup_kernel,
        in_specs=[SMEM, HBM],
        out_specs=HBM,
        out_shape=jax.ShapeDtypeStruct(shape, perambulator.dtype),
        scratch_shapes=[
            pltpu.VMEM(shape, perambulator.dtype),
            pltpu.SemaphoreType.DMA((2 * half,)),
            pltpu.SemaphoreType.DMA((2 * half,)),
        ],
        compiler_params=pltpu.CompilerParams(vmem_limit_bytes=58 * 1024 * 1024),
    )(high.reshape(1), source)


def tied(x, *earlier):
    return pl.pallas_call(
        lambda *refs: None,
        in_specs=[ANYWHERE] * (1 + len(earlier)),
        out_specs=ANYWHERE,
        out_shape=jax.ShapeDtypeStruct(x.shape, x.dtype),
        input_output_aliases={0: 0},
    )(x, *earlier)


def halves_swapped(x):
    vectors = x.shape[1] // 2
    return jnp.concatenate([x[:, vectors:], x[:, :vectors]], axis=1)


def pairs_kernel(pairs, first, begins, carries, direct, counts_ref, tau_ref, *refs):
    begin_refs, refs = refs[:begins], refs[begins:]
    carry_refs, refs = refs[:carries], refs[carries:]
    sink_refs, source_ref, out_ref = refs[:pairs], refs[pairs], refs[pairs + 1]
    carried_refs, refs = refs[pairs + 2 : pairs + 2 + carries], refs[pairs + 2 + carries :]
    sinks, sources, swap_ref, left_ref, sink_sems, source_sems = refs
    slots, vectors, packed = sinks.shape[1:]
    spins, _, width = swap_ref.shape
    blocks = width // packed
    pieces = tau_ref.shape[0] // spins
    pair = pl.program_id(0)
    first_half = lax.broadcasted_iota(jnp.int32, (vectors, packed), 1) < vectors

    @pl.when(pair == 0)
    def _():
        for p in range(pairs):
            for d in range(slots):

                @pl.when((d == 0) | (counts_ref[first + p] > 1))
                def _():
                    if not direct:
                        pltpu.make_async_copy(
                            sink_refs[p].at[d], sinks.at[p, d], sink_sems.at[p, d]
                        ).start()
                    pltpu.make_async_copy(
                        source_ref.at[first + p, d], sources.at[p, d], source_sems.at[p, d]
                    ).start()

        for p in range(out_ref.shape[0]):
            for d in range(slots):
                for side in range(2):
                    out_ref[p, side, d] = begin_refs[0][p, side, d] if begins else 0.0
                    if carries:
                        carried_refs[0][p, side, d] = carry_refs[0][p, side, d]

    def tile(s):
        return tau_ref[s * pieces : (s + 1) * pieces, 0].reshape(vectors, width)

    def part(x, b):
        return x[:, b * packed : (b + 1) * packed]

    for s in range(spins):
        for b in range(blocks):
            swapped = halves_swapped(part(tile(s), b))
            swap_ref[s, :, b * packed : (b + 1) * packed] = jnp.where(
                first_half, -swapped, swapped
            )

    def embedded(d):
        if direct:
            sink = sink_refs[0][d]
        else:
            pltpu.make_async_copy(
                sink_refs[0].at[0], sinks.at[pair, d], sink_sems.at[pair, d]
            ).wait()
            sink = sinks[pair, d]
        return [jnp.where(first_half, sink, -sink), halves_swapped(sink)]

    def add_slots(taken):
        embedding = jnp.concatenate([half for d in range(taken) for half in embedded(d)], axis=0)
        for s in range(spins):
            stacked = jnp.concatenate([part(tile(s), b) for b in range(blocks)], axis=0)
            left = lax.dot_general(
                stacked, embedding, NT_DIMS, preferred_element_type=jnp.float32
            ).astype(jnp.bfloat16)
            for d in range(taken):
                for b in range(blocks):
                    left_ref[
                        s, d * vectors : (d + 1) * vectors, b * packed : (b + 1) * packed
                    ] = left[b * vectors : (b + 1) * vectors, d * packed : (d + 1) * packed]
        block_real = jnp.zeros((taken * vectors, vectors), jnp.float32)
        block_imag = jnp.zeros((taken * vectors, vectors), jnp.float32)
        for s in range(spins):
            left = left_ref[s, : taken * vectors]
            block_real += lax.dot_general(
                left, tile(s), NT_DIMS, preferred_element_type=jnp.float32
            )
            block_imag += lax.dot_general(
                left, swap_ref[s], NT_DIMS, preferred_element_type=jnp.float32
            )
        for d in range(taken):
            pltpu.make_async_copy(
                source_ref.at[0, 0], sources.at[pair, d], source_sems.at[pair, d]
            ).wait()
            source = sources[pair, d].astype(jnp.float32)
            real = source[:, :vectors]
            imag = source[:, vectors:]
            own_real = block_real[d * vectors : (d + 1) * vectors]
            own_imag = block_imag[d * vectors : (d + 1) * vectors]
            live = d < counts_ref[first + pair]
            out_ref[first + pair, 0, d] += jnp.where(
                live, jnp.sum(real * own_real - imag * own_imag), 0.0
            )
            out_ref[first + pair, 1, d] += jnp.where(
                live, jnp.sum(real * own_imag + imag * own_real), 0.0
            )

    several = counts_ref[first + pair] > 1
    pl.when(several)(lambda: add_slots(slots))
    pl.when(jnp.logical_not(several))(lambda: add_slots(1))


def pairs_sums(tau, side, first, sinks, sources, counts, begin=[], carry=[], place=ANYWHERE, vmem=60):
    pairs = len(sinks)
    slots, vectors, packed = sinks[0].shape
    pieces, _, columns, width = tau.shape
    spins = pieces * columns // vectors
    lead = side * counts.shape[0] + first
    flops = 4 * pairs * spins * slots * width * vectors * packed
    moved = 2 * pairs * (spins * vectors * width + 2 * slots * vectors * packed)
    elemental_copies = [pltpu.VMEM((pairs, slots, vectors, packed), jnp.bfloat16)] * 2
    call = pl.pallas_call(
        functools.partial(
            pairs_kernel, pairs, first, len(begin), len(carry), place is VMEM
        ),
        grid=(pairs,),
        in_specs=[
            SMEM,
            pl.BlockSpec((pieces, 1, columns, width), lambda p: (0, lead + p, 0, 0)),
        ]
        + [SMEM] * len(begin + carry)
        + [place] * pairs
        + [ANYWHERE],
        out_specs=[SMEM] * (1 + len(carry)),
        out_shape=[jax.ShapeDtypeStruct((counts.shape[0], 2, slots), jnp.float32)]
        * (1 + len(carry)),
        scratch_shapes=elemental_copies
        + [
            pltpu.VMEM((spins, vectors, width), jnp.bfloat16),
            pltpu.VMEM((spins, slots * vectors, width), jnp.bfloat16),
            pltpu.SemaphoreType.DMA((pairs, slots)),
            pltpu.SemaphoreType.DMA((pairs, slots)),
        ],
        compiler_params=pltpu.CompilerParams(vmem_limit_bytes=vmem * 1024 * 1024),
        cost_estimate=pl.CostEstimate(flops=flops, bytes_accessed=moved, transcendentals=0),
    )
    return list(call(counts, tau, *begin, *carry, *sinks, sources))


def body(perambulator, elementals, diagrams, counts):
    devices = lax.axis_size("tm")
    me = lax.axis_index("tm")
    pair_count, slots = diagrams.shape[:2]
    columns, width = perambulator.shape[1:]
    vectors, packed = elementals.shape[2:]
    half = devices // 2
    own_set = elementals[0]
    high = (me >= half).astype(jnp.int32)
    halves = [list(range(half)), list(range(half, devices))]

    steps = [(slot + 1) * devices // (pair_count + 1) for slot in range(pair_count)]
    wanted = [passed_along(diagrams[slot, :, 0], by) for slot, by in enumerate(steps)]
    given_counts = exchanged(counts, half)
    own_sources = jnp.take(own_set, diagrams[:, :, 1].reshape(-1), axis=0, mode="clip")
    own_sources = own_sources.reshape(pair_count, slots, vectors, packed)
    given_sources = exchanged(own_sources, half)
    chosen = [jnp.take(own_set, index, axis=0, mode="clip") for index in wanted]
    given_sinks = [passed_along(sets, -by, half) for by, sets in zip(steps, chosen)]
    last = pair_count - 1
    own_sinks = [
        passed_along(sets if slot < last else tied(sets, given_sinks[0]), -by)
        for slot, (by, sets) in enumerate(zip(steps, chosen))
    ]

    tau = lax.all_to_all(
        tied(regrouped(perambulator, high, half, pair_count), given_counts, *wanted),
        "tm",
        split_axis=0,
        concat_axis=0,
        axis_index_groups=halves,
        tiled=True,
    ).reshape(half, 2 * pair_count, columns, width)
    if columns % 16 != 0:
        tau = jnp.moveaxis(tau, 1, 0).reshape(2 * pair_count, -1, vectors, width)
        tau = jnp.moveaxis(tau, 0, 1)

    given = []
    for slot, sink in enumerate(given_sinks):
        given = pairs_sums(tau, 0, slot, [sink], given_sources, given_counts, given)
    kept, given = pairs_sums(tau, 1, 0, own_sinks[:last], own_sources, counts, carry=given)
    got = exchanged(given, half)
    (kept,) = pairs_sums(
        tau, 1, last, own_sinks[last:], own_sources, counts, [kept], place=VMEM, vmem=24
    )
    return jnp.swapaxes((kept + got) / (columns * devices), 1, 2)


def solution(mesh):
    return jax.shard_map(
        body,
        mesh=mesh,
        in_specs=(
            P("groups", "tm", None),
            P(("groups", "tm"), None, None, None),
            P("tm", None, None),
            P("tm"),
        ),
        out_specs=P(("groups", "tm"), None, None),
        check_vma=False,
    )
```

```python
import functools

import jax
import jax.numpy as jnp
from jax import lax
from jax.experimental import pallas as pl
from jax.experimental.pallas import tpu as pltpu
from jax.sharding import PartitionSpec as P

NT_DIMS = (((1,), (1,)), ((), ()))
ANYWHERE = pl.BlockSpec(memory_space=pl.ANY)
HBM = pl.BlockSpec(memory_space=pltpu.HBM)
VMEM = pl.BlockSpec(memory_space=pltpu.VMEM)
SMEM = pl.BlockSpec(memory_space=pltpu.SMEM)


def exchanged(x, mask):
    devices = lax.axis_size("tm")
    return lax.ppermute(x, "tm", [(i, i ^ mask) for i in range(devices)])


def passed_along(x, by, mask=0):
    devices = lax.axis_size("tm")
    return lax.ppermute(x, "tm", [(i, ((i + by) % devices) ^ mask) for i in range(devices)])


def regroup_kernel(high_ref, source_ref, out_ref, block_ref, in_sems, out_sems):
    high = high_ref[0]
    copies = []
    for j in range(source_ref.shape[1]):
        for side in range(2):
            which = 1 - high if side == 0 else high
            block = block_ref.at[j, side]
            n = 2 * j + side
            copies.append(
                (
                    pltpu.make_async_copy(source_ref.at[which, j], block, in_sems.at[n]),
                    pltpu.make_async_copy(block, out_ref.at[j, side], out_sems.at[n]),
                )
            )
    for copy_in, _ in copies:
        copy_in.start()
    for copy_in, copy_out in copies:
        copy_in.wait()
        copy_out.start()
    for _, copy_out in copies:
        copy_out.wait()


def regrouped(perambulator, high, half, pair_count):
    columns, width = perambulator.shape[1:]
    source = perambulator.reshape(2, half, pair_count, columns, width)
    shape = (half, 2, pair_count, columns, width)
    return pl.pallas_call(
        regroup_kernel,
        in_specs=[SMEM, HBM],
        out_specs=HBM,
        out_shape=jax.ShapeDtypeStruct(shape, perambulator.dtype),
        scratch_shapes=[
            pltpu.VMEM(shape, perambulator.dtype),
            pltpu.SemaphoreType.DMA((2 * half,)),
            pltpu.SemaphoreType.DMA((2 * half,)),
        ],
        compiler_params=pltpu.CompilerParams(vmem_limit_bytes=58 * 1024 * 1024),
    )(high.reshape(1), source)


def tied(x, *earlier):
    return pl.pallas_call(
        lambda *refs: None,
        in_specs=[ANYWHERE] * (1 + len(earlier)),
        out_specs=ANYWHERE,
        out_shape=jax.ShapeDtypeStruct(x.shape, x.dtype),
        input_output_aliases={0: 0},
    )(x, *earlier)


def halves_swapped(x):
    vectors = x.shape[1] // 2
    return jnp.concatenate([x[:, vectors:], x[:, :vectors]], axis=1)


def pairs_kernel(pairs, first, begins, carries, direct, counts_ref, tau_ref, *refs):
    begin_refs, refs = refs[:begins], refs[begins:]
    carry_refs, refs = refs[:carries], refs[carries:]
    sink_refs, source_ref, out_ref = refs[:pairs], refs[pairs], refs[pairs + 1]
    carried_refs, refs = refs[pairs + 2 : pairs + 2 + carries], refs[pairs + 2 + carries :]
    sinks, sources, swap_ref, left_ref, sink_sems, source_sems = refs
    slots, vectors, packed = sinks.shape[1:]
    spins, _, width = swap_ref.shape
    blocks = width // packed
    pieces = tau_ref.shape[0] // spins
    pair = pl.program_id(0)
    first_half = lax.broadcasted_iota(jnp.int32, (vectors, packed), 1) < vectors

    @pl.when(pair == 0)
    def _():
        for p in range(pairs):
            for d in range(slots):

                @pl.when((d == 0) | (counts_ref[first + p] > 1))
                def _():
                    if not direct:
                        pltpu.make_async_copy(
                            sink_refs[p].at[d], sinks.at[p, d], sink_sems.at[p, d]
                        ).start()
                    pltpu.make_async_copy(
                        source_ref.at[first + p, d], sources.at[p, d], source_sems.at[p, d]
                    ).start()

        for p in range(out_ref.shape[0]):
            for d in range(slots):
                for side in range(2):
                    out_ref[p, side, d] = begin_refs[0][p, side, d] if begins else 0.0
                    if carries:
                        carried_refs[0][p, side, d] = carry_refs[0][p, side, d]

    def tile(s):
        return tau_ref[s * pieces : (s + 1) * pieces, 0].reshape(vectors, width)

    def part(x, b):
        return x[:, b * packed : (b + 1) * packed]

    for s in range(spins):
        for b in range(blocks):
            swapped = halves_swapped(part(tile(s), b))
            swap_ref[s, :, b * packed : (b + 1) * packed] = jnp.where(
                first_half, -swapped, swapped
            )

    def embedded(d):
        if direct:
            sink = sink_refs[0][d]
        else:
            pltpu.make_async_copy(
                sink_refs[0].at[0], sinks.at[pair, d], sink_sems.at[pair, d]
            ).wait()
            sink = sinks[pair, d]
        return [jnp.where(first_half, sink, -sink), halves_swapped(sink)]

    def add_slots(taken):
        embedding = jnp.concatenate([half for d in range(taken) for half in embedded(d)], axis=0)
        for s in range(spins):
            stacked = jnp.concatenate([part(tile(s), b) for b in range(blocks)], axis=0)
            left = lax.dot_general(
                stacked, embedding, NT_DIMS, preferred_element_type=jnp.float32
            ).astype(jnp.bfloat16)
            for d in range(taken):
                for b in range(blocks):
                    left_ref[
                        s, d * vectors : (d + 1) * vectors, b * packed : (b + 1) * packed
                    ] = left[b * vectors : (b + 1) * vectors, d * packed : (d + 1) * packed]
        block_real = jnp.zeros((taken * vectors, vectors), jnp.float32)
        block_imag = jnp.zeros((taken * vectors, vectors), jnp.float32)
        for s in range(spins):
            left = left_ref[s, : taken * vectors]
            block_real += lax.dot_general(
                left, tile(s), NT_DIMS, preferred_element_type=jnp.float32
            )
            block_imag += lax.dot_general(
                left, swap_ref[s], NT_DIMS, preferred_element_type=jnp.float32
            )
        for d in range(taken):
            pltpu.make_async_copy(
                source_ref.at[0, 0], sources.at[pair, d], source_sems.at[pair, d]
            ).wait()
            source = sources[pair, d].astype(jnp.float32)
            real = source[:, :vectors]
            imag = source[:, vectors:]
            own_real = block_real[d * vectors : (d + 1) * vectors]
            own_imag = block_imag[d * vectors : (d + 1) * vectors]
            live = d < counts_ref[first + pair]
            out_ref[first + pair, 0, d] += jnp.where(
                live, jnp.sum(real * own_real - imag * own_imag), 0.0
            )
            out_ref[first + pair, 1, d] += jnp.where(
                live, jnp.sum(real * own_imag + imag * own_real), 0.0
            )

    several = counts_ref[first + pair] > 1
    pl.when(several)(lambda: add_slots(slots))
    pl.when(jnp.logical_not(several))(lambda: add_slots(1))


def pairs_sums(tau, side, first, sinks, sources, counts, begin=[], carry=[], place=ANYWHERE, vmem=60):
    pairs = len(sinks)
    slots, vectors, packed = sinks[0].shape
    pieces, _, columns, width = tau.shape
    spins = pieces * columns // vectors
    lead = side * counts.shape[0] + first
    flops = 4 * pairs * spins * slots * width * vectors * packed
    moved = 2 * pairs * (spins * vectors * width + 2 * slots * vectors * packed)
    elemental_copies = [pltpu.VMEM((pairs, slots, vectors, packed), jnp.bfloat16)] * 2
    call = pl.pallas_call(
        functools.partial(
            pairs_kernel, pairs, first, len(begin), len(carry), place is VMEM
        ),
        grid=(pairs,),
        in_specs=[
            SMEM,
            pl.BlockSpec((pieces, 1, columns, width), lambda p: (0, lead + p, 0, 0)),
        ]
        + [SMEM] * len(begin + carry)
        + [place] * pairs
        + [ANYWHERE],
        out_specs=[SMEM] * (1 + len(carry)),
        out_shape=[jax.ShapeDtypeStruct((counts.shape[0], 2, slots), jnp.float32)]
        * (1 + len(carry)),
        scratch_shapes=elemental_copies
        + [
            pltpu.VMEM((spins, vectors, width), jnp.bfloat16),
            pltpu.VMEM((spins, slots * vectors, width), jnp.bfloat16),
            pltpu.SemaphoreType.DMA((pairs, slots)),
            pltpu.SemaphoreType.DMA((pairs, slots)),
        ],
        compiler_params=pltpu.CompilerParams(vmem_limit_bytes=vmem * 1024 * 1024),
        cost_estimate=pl.CostEstimate(flops=flops, bytes_accessed=moved, transcendentals=0),
    )
    return list(call(counts, tau, *begin, *carry, *sinks, sources))


def body(perambulator, elementals, diagrams, counts):
    devices = lax.axis_size("tm")
    me = lax.axis_index("tm")
    pair_count, slots = diagrams.shape[:2]
    columns, width = perambulator.shape[1:]
    vectors, packed = elementals.shape[2:]
    half = devices // 2
    own_set = elementals[0]
    high = (me >= half).astype(jnp.int32)
    halves = [list(range(half)), list(range(half, devices))]

    steps = [(slot + 1) * devices // (pair_count + 1) for slot in range(pair_count)]
    wanted = [passed_along(diagrams[slot, :, 0], by) for slot, by in enumerate(steps)]
    given_counts = exchanged(counts, half)
    own_sources = jnp.take(own_set, diagrams[:, :, 1].reshape(-1), axis=0, mode="clip")
    own_sources = own_sources.reshape(pair_count, slots, vectors, packed)
    given_sources = exchanged(own_sources, half)
    chosen = [jnp.take(own_set, index, axis=0, mode="clip") for index in wanted]
    given_sinks = [passed_along(sets, -by, half) for by, sets in zip(steps, chosen)]
    last = pair_count - 1
    own_sinks = [
        passed_along(sets if slot < last else tied(sets, given_sinks[0]), -by)
        for slot, (by, sets) in enumerate(zip(steps, chosen))
    ]

    tau = lax.all_to_all(
        tied(regrouped(perambulator, high, half, pair_count), *wanted),
        "tm",
        split_axis=0,
        concat_axis=0,
        axis_index_groups=halves,
        tiled=True,
    ).reshape(half, 2 * pair_count, columns, width)
    if columns % 16 != 0:
        tau = jnp.moveaxis(tau, 1, 0).reshape(2 * pair_count, -1, vectors, width)
        tau = jnp.moveaxis(tau, 0, 1)

    given = pairs_sums(tau, 0, 0, given_sinks, given_sources, given_counts)
    kept, given = pairs_sums(tau, 1, 0, own_sinks[:last], own_sources, counts, carry=given)
    got = exchanged(given, half)
    (kept,) = pairs_sums(
        tau, 1, last, own_sinks[last:], own_sources, counts, [kept], place=VMEM, vmem=24
    )
    return jnp.swapaxes((kept + got) / (columns * devices), 1, 2)


def solution(mesh):
    return jax.shard_map(
        body,
        mesh=mesh,
        in_specs=(
            P("groups", "tm", None),
            P(("groups", "tm"), None, None, None),
            P("tm", None, None),
            P("tm"),
        ),
        out_specs=P(("groups", "tm"), None, None),
        check_vma=False,
    )
```
